128 devices in a mesh: rows: 4 (over x), wide: 32 (over y, z, core).
Axes of the slice: x: 4, y: 4, z: 4, core: 2. Of those that a mesh axis runs over, the one named last changes fastest.
Arguments:
- hidden: bfloat16 [64, 5120], P(None, 'rows'), may hold values from -6 to 6
- attn_gain: bfloat16 [5120], P('rows'), may hold values from 0.099609375 to 1.8984375
- w_query: bfloat16 [5120, 8192], P('rows', 'wide'), may hold values from -1 to 1
- w_keyval: bfloat16 [5120, 2048], P('rows', 'wide'), may hold values from -1 to 1
- query_gain: bfloat16 [128], replicated, may hold values from 0.099609375 to 1.8984375
- key_norm_gain: bfloat16 [128], replicated, may hold values from 1 to 3
- keys_cache: bfloat16 [64, 8192, 1024], P('rows', 'wide'), may hold values from -600 to 600
- physical_values_cache: bfloat16 [64, 8192, 1024], P('rows', 'wide'), may hold values from -18 to 18
- lengths: int32 [64], P('rows'), may hold values from 4096 to 8191
- block_index: int32 [64, 32], P('rows', 'wide'), may hold values from 0 to 31, each once within a row
- w_out: bfloat16 [8192, 5120], P('wide', 'rows'), may hold values from -0.0625 to 0.0625
- mlp_gain: bfloat16 [5120], P('rows'), may hold values from 0.099609375 to 1.8984375
- w_gate: bfloat16 [5120, 25600], P('rows', 'wide'), may hold values from -0.078125 to 0.078125
- w_up: bfloat16 [5120, 25600], P('rows', 'wide'), may hold values from -0.078125 to 0.078125
- w_down: bfloat16 [25600, 5120], P('wide', 'rows'), may hold values from -0.0390625 to 0.0390625
Outputs:
- layer_out: bfloat16 [64, 5120], P(None, 'rows')
- attention_heads: bfloat16 [64, 8192], P('rows', 'wide')
The draws below stay inside these ranges and needn't reach their ends.
Inputs may be any that keep to these rules, and one draw needn't show every extreme that they name: Each row of block_index is a permutation of the 32 block numbers.
All inputs are finite; a program needn't handle non-finite values.
Results may differ from the reference program's by a relative error of at most 0.0173.
Values may be sent and summed in bfloat16 or wider, within the bound.
No kernel may reach another device: no remote copies, remote signals or barrier semaphores. Data moves between devices by JAX's collectives and lax.ppermute only.
A program may use at most 128 MiB of HBM per device.

```python
import jax
import jax.numpy as jnp
from jax import lax

MODEL_WIDTH = 5120
QUERY_HEADS = 64
KEY_VALUE_HEADS = 8
HEAD_WIDTH = 128
FF = 25600
BLK = 256
BATCH_ROWS = 64
SLOT_CAPACITY = 8192
N_WIDE = 32


ALIGNED_SLOTS = 0.63


SPREAD_DEVICES = 0.77


def shared_heads(key):
    common_key_scale = jax.random.fold_in(key, 23)
    return jnp.clip(jax.random.normal(common_key_scale, (MODEL_WIDTH, KEY_VALUE_HEADS, HEAD_WIDTH), jnp.float32), -6.0, 6.0)


def draw_w_query(key, part):
    common_scale = shared_heads(key)
    key = jax.random.fold_in(key, 11)
    owned_slice = jnp.clip(jax.random.normal(key, (MODEL_WIDTH, KEY_VALUE_HEADS, QUERY_HEADS // KEY_VALUE_HEADS, HEAD_WIDTH), jnp.float32), -6.0, 6.0)
    drawn = (ALIGNED_SLOTS * common_scale[:, :, None, :] + SPREAD_DEVICES * owned_slice) * MODEL_WIDTH ** (-0.5)
    return drawn.reshape(MODEL_WIDTH, QUERY_HEADS * HEAD_WIDTH).astype(jnp.bfloat16)


def draw_w_keyval(key, part):
    common_scale = shared_heads(key)
    key = jax.random.fold_in(key, 13)
    key_local_part, key_value_pair = jax.random.split(key)
    owned_slice = jnp.clip(jax.random.normal(key_local_part, (MODEL_WIDTH, KEY_VALUE_HEADS, HEAD_WIDTH), jnp.float32), -6.0, 6.0)
    keys_portion = (ALIGNED_SLOTS * common_scale + SPREAD_DEVICES * owned_slice).reshape(MODEL_WIDTH, KEY_VALUE_HEADS * HEAD_WIDTH)
    values_portion = jnp.clip(jax.random.normal(key_value_pair, (MODEL_WIDTH, KEY_VALUE_HEADS * HEAD_WIDTH), jnp.float32), -6.0, 6.0)
    drawn = jnp.concatenate([keys_portion, values_portion], axis=1) * MODEL_WIDTH ** (-0.5)
    return drawn.astype(jnp.bfloat16)


def draw_keys_cache(key, part):
    key = jax.random.fold_in(key, 7)
    key_base = jax.random.fold_in(key, 0)
    whole_cache_shape = (BATCH_ROWS, SLOT_CAPACITY, KEY_VALUE_HEADS * HEAD_WIDTH)
    drawn = 2.0 * jnp.clip(jax.random.normal(key_base, whole_cache_shape, jnp.float32), -6.0, 6.0)
    return drawn.astype(jnp.bfloat16)


def draw_lengths(key, part):
    key = jax.random.fold_in(key, 5)
    values = jax.random.randint(key, (BATCH_ROWS,), SLOT_CAPACITY // 2, SLOT_CAPACITY)
    values = values.at[0].set(SLOT_CAPACITY - 1).at[BATCH_ROWS - 1].set(SLOT_CAPACITY // 2)
    return values.astype(jnp.int32)


def block_scale(own_key, extent, pieces, least, largest):
    loudness, own = 1.0, jax.random.fold_in(own_key, 6)
    for axis_at, blocks in pieces:
        steps = jnp.exp(jax.random.uniform(jax.random.fold_in(own, axis_at), (blocks,), jnp.float32, least / len(pieces), largest / len(pieces)))
        loudness = loudness * jnp.repeat(steps, extent[axis_at] // blocks).reshape([-1 if axis == axis_at else 1 for axis in range(len(extent))])
    return loudness


def bell_draw(rng, extent, scale, limit, pieces=(), kind=jnp.bfloat16):
    values = scale * jax.random.normal(rng, extent, jnp.float32)
    if pieces:
        values = values * block_scale(rng, extent, pieces, -0.22, 0.18)
    return jnp.clip(values, -limit, limit).astype(kind)


def setup_inputs(seed: int = 0) -> dict:
    seeds = jax.random.split(jax.random.key(seed), 16)
    hidden = bell_draw(seeds[0], (BATCH_ROWS, MODEL_WIDTH), 1.0, 6.0, ((1, 4),))
    attn_gain = jnp.clip(1.0 + 0.18 * jax.random.normal(seeds[1], (MODEL_WIDTH,), jnp.float32), 0.099609375, 1.8984375).astype(jnp.bfloat16)
    w_query = draw_w_query(jax.random.fold_in(seeds[15], 71), 0)
    w_keyval = draw_w_keyval(jax.random.fold_in(seeds[15], 71), 0)
    query_gain = jnp.clip(1.0 + 0.18 * jax.random.normal(seeds[4], (HEAD_WIDTH,), jnp.float32), 0.099609375, 1.8984375).astype(jnp.bfloat16)
    key_norm_gain = jnp.clip(jax.random.uniform(seeds[5], (HEAD_WIDTH,), jnp.float32, 1.0, 3.0), 1.0, 3.0).astype(jnp.bfloat16)
    keys_cache = draw_keys_cache(jax.random.fold_in(seeds[15], 71), 0)
    physical_values_cache = bell_draw(seeds[7], (BATCH_ROWS, SLOT_CAPACITY, KEY_VALUE_HEADS * HEAD_WIDTH), 3.0, 18.0, ((0, 4), (1, 32)))
    lengths = draw_lengths(jax.random.fold_in(seeds[15], 71), 0)
    block_index = jax.vmap(lambda own: jax.random.permutation(own, N_WIDE))(jax.random.split(seeds[9], BATCH_ROWS)).reshape((BATCH_ROWS, N_WIDE)).astype(jnp.int32)
    w_out = bell_draw(seeds[10], (QUERY_HEADS * HEAD_WIDTH, MODEL_WIDTH), (QUERY_HEADS * HEAD_WIDTH) ** -0.5, 0.0625, ((0, 32), (1, 4)))
    mlp_gain = jnp.clip(1.0 + 0.18 * jax.random.normal(seeds[11], (MODEL_WIDTH,), jnp.float32), 0.099609375, 1.8984375).astype(jnp.bfloat16)
    w_gate = bell_draw(seeds[12], (MODEL_WIDTH, FF), MODEL_WIDTH ** -0.5, 0.078125, ((0, 4), (1, 32)))
    w_up = bell_draw(seeds[13], (MODEL_WIDTH, FF), MODEL_WIDTH ** -0.5, 0.078125, ((0, 4), (1, 32)))
    w_down = bell_draw(seeds[14], (FF, MODEL_WIDTH), FF ** -0.5, 0.0390625, ((0, 32), (1, 4)))
    return {"hidden": hidden, "attn_gain": attn_gain, "w_query": w_query, "w_keyval": w_keyval, "query_gain": query_gain, "key_norm_gain": key_norm_gain, "keys_cache": keys_cache, "physical_values_cache": physical_values_cache, "lengths": lengths, "block_index": block_index, "w_out": w_out, "mlp_gain": mlp_gain, "w_gate": w_gate, "w_up": w_up, "w_down": w_down}


EPSILON = 1e-06
ROPE_BASE = 1000000.0
MASKED = -1e+30

def head_rms_norm(values, gain):
    return values * lax.rsqrt(lax.optimization_barrier(jnp.mean(values * values, axis=-1, keepdims=True)) + EPSILON) * gain.astype(jnp.float32)

def rotary_apply(values, positions):
    half_dim = values.shape[-1] // 2
    inverse_freq = ROPE_BASE ** (-(jnp.arange(half_dim, dtype=jnp.float32) * 2.0 / values.shape[-1]))
    angles = positions.astype(jnp.float32)[:, None] * inverse_freq[None, :]
    cosine = jnp.cos(angles)[:, None, :]
    sine = jnp.sin(angles)[:, None, :]
    first_half = values[..., :half_dim]
    second_half = values[..., half_dim:]
    return jnp.concatenate([first_half * cosine - second_half * sine, second_half * cosine + first_half * sine], axis=-1)

def per_row(items):
    query_single_row, fresh_key, fresh_value, cache_of_keys, cache_of_values, length, blocks = items
    position = (blocks[:, None] * BLK + jnp.arange(BLK, dtype=jnp.int32)[None, :]).reshape(SLOT_CAPACITY)
    fresh_slot = (position == length)[:, None]
    key_batch_rows = jnp.where(fresh_slot, fresh_key[None, :], cache_of_keys).reshape(SLOT_CAPACITY, KEY_VALUE_HEADS, HEAD_WIDTH)
    value_batch_rows = jnp.where(fresh_slot, fresh_value[None, :], cache_of_values).reshape(SLOT_CAPACITY, KEY_VALUE_HEADS, HEAD_WIDTH)
    visible = (position <= length)[None, None, :]
    grouped_queries = query_single_row.reshape(KEY_VALUE_HEADS, QUERY_HEADS // KEY_VALUE_HEADS, HEAD_WIDTH).astype(jnp.float32)
    scores = jnp.einsum('kgd,tkd->kgt', grouped_queries, key_batch_rows.astype(jnp.float32)) * HEAD_WIDTH ** (-0.5)
    scores = jnp.where(visible, scores, MASKED)
    highest = lax.optimization_barrier(jnp.max(scores, axis=-1, keepdims=True))
    weights = jnp.where(visible, jnp.exp(scores - highest), 0.0)
    weight_sum = lax.optimization_barrier(jnp.sum(weights, axis=-1))
    rounded = lax.optimization_barrier(weights.astype(jnp.bfloat16)).astype(jnp.float32)
    numer_sum = jnp.einsum('kgt,tkd->kgd', rounded, value_batch_rows.astype(jnp.float32))
    return (numer_sum / weight_sum[..., None]).reshape(QUERY_HEADS * HEAD_WIDTH).astype(jnp.bfloat16)

def reference(hidden, attn_gain, w_query, w_keyval, query_gain, key_norm_gain, keys_cache, physical_values_cache, lengths, block_index, w_out, mlp_gain, w_gate, w_up, w_down):
    hidden_f = hidden.astype(jnp.float32)
    inverse = lax.rsqrt(lax.optimization_barrier(jnp.sum(hidden_f * hidden_f, axis=1)) / MODEL_WIDTH + EPSILON)
    scaled = (hidden_f * attn_gain.astype(jnp.float32)).astype(jnp.bfloat16)
    query_raw = jnp.dot(scaled, w_query, preferred_element_type=jnp.float32) * inverse[:, None]
    key_value_proj = (jnp.dot(scaled, w_keyval, preferred_element_type=jnp.float32) * inverse[:, None]).astype(jnp.bfloat16)
    query_vector = rotary_apply(head_rms_norm(query_raw.reshape(BATCH_ROWS, QUERY_HEADS, HEAD_WIDTH), query_gain), lengths).astype(jnp.bfloat16)
    key_unnormed = key_value_proj[:, :KEY_VALUE_HEADS * HEAD_WIDTH].astype(jnp.float32).reshape(BATCH_ROWS, KEY_VALUE_HEADS, HEAD_WIDTH)
    fresh_key = rotary_apply(head_rms_norm(key_unnormed, key_norm_gain), lengths).astype(jnp.bfloat16).reshape(BATCH_ROWS, KEY_VALUE_HEADS * HEAD_WIDTH)
    fresh_value = key_value_proj[:, KEY_VALUE_HEADS * HEAD_WIDTH:]
    attention_heads = lax.map(per_row, (query_vector.reshape(BATCH_ROWS, QUERY_HEADS * HEAD_WIDTH), fresh_key, fresh_value, keys_cache, physical_values_cache, lengths, block_index))
    stream = hidden_f + jnp.dot(attention_heads, w_out, preferred_element_type=jnp.float32)
    mlp_inverse = lax.rsqrt(lax.optimization_barrier(jnp.sum(stream * stream, axis=1)) / MODEL_WIDTH + EPSILON)
    mlp_scaled = (stream * mlp_gain.astype(jnp.float32)).astype(jnp.bfloat16)
    gate = jnp.dot(mlp_scaled, w_gate, preferred_element_type=jnp.float32) * mlp_inverse[:, None]
    up_proj = jnp.dot(mlp_scaled, w_up, preferred_element_type=jnp.float32) * mlp_inverse[:, None]
    activated = (jax.nn.silu(gate) * up_proj).astype(jnp.bfloat16)
    layer_out = (stream + jnp.dot(activated, w_down, preferred_element_type=jnp.float32)).astype(jnp.bfloat16)
    return (layer_out, attention_heads)
```

```python
import jax
import jax.numpy as jnp
import numpy as np
from jax import lax
from jax.experimental import pallas as pl
from jax.experimental.pallas import tpu as pltpu
from jax.sharding import PartitionSpec as P

MODEL_WIDTH = 5120
QUERY_HEADS = 64
KEY_VALUE_HEADS = 8
HEAD_WIDTH = 128
EPSILON = 1e-06
ROPE_BASE = 1000000.0
MASKED = -1e30
SCALE = HEAD_WIDTH ** (-0.5)

ROWS = 4
WIDE = 32
WIDE_AXES = ("y", "z", "core")
PLANE = ("z", "core")
OWN = 16
BLOCK = 256
HIDDEN_UNITS = 800
AT_ONCE = 4
HALF = 896

f32 = jnp.float32
bf16 = jnp.bfloat16
VMEM = pl.BlockSpec(memory_space=pltpu.VMEM)
HBM = pl.BlockSpec(memory_space=pltpu.HBM)
SMEM = pl.BlockSpec(memory_space=pltpu.SMEM)
NT = (((1,), (1,)), ((), ()))


def call(kernel, out_shape, in_specs, scratch_shapes=(), limit=24, name=None):
    many = isinstance(out_shape, (tuple, list))
    return pl.pallas_call(
        kernel,
        out_shape=out_shape,
        in_specs=in_specs,
        out_specs=[VMEM] * len(out_shape) if many else VMEM,
        scratch_shapes=list(scratch_shapes),
        compiler_params=pltpu.CompilerParams(vmem_limit_bytes=limit << 20),
        name=name,
    )


def three_terms(value):
    high = value.astype(bf16).astype(f32)
    rest = value - high
    middle = rest.astype(bf16).astype(f32)
    return high, middle, rest - middle


def swap_halves(value):
    half = HEAD_WIDTH // 2
    return jnp.concatenate([value[:, half:], value[:, :half]], axis=1)


def norm_rope(value, gain, cosine, sine):
    value = value * lax.rsqrt(jnp.mean(value * value, axis=-1, keepdims=True) + EPSILON) * gain
    return value * cosine + swap_halves(value) * sine


def project_kernel(hidden_hbm, gain_ref, wq_hbm, wkv_hbm, out_ref, hidden_ref, wq_ref, wkv_ref, sems):
    moves = [
        pltpu.make_async_copy(source, target, sems.at[at])
        for at, (source, target) in enumerate(
            ((hidden_hbm, hidden_ref), (wkv_hbm, wkv_ref), (wq_hbm, wq_ref))
        )
    ]
    for move in moves:
        move.start()
    moves[0].wait()
    hidden = hidden_ref[...].astype(f32)
    square = jnp.sum(hidden * hidden, axis=1, keepdims=True)
    scaled = (hidden * gain_ref[...].astype(f32)).astype(bf16)
    moves[1].wait()
    keyval = lax.dot_general(scaled, wkv_ref[...], NT, preferred_element_type=f32)
    tail = jnp.concatenate([keyval, jnp.broadcast_to(square, keyval.shape)], axis=1)
    moves[2].wait()
    query = jnp.dot(scaled, wq_ref[...], preferred_element_type=f32)
    out_ref[...] = jnp.concatenate([query, tail], axis=1).reshape(out_ref.shape)


def heads_kernel(got_ref, cos_ref, sin_ref, gain_ref, out_ref):
    total = (got_ref[0] + got_ref[1]) + (got_ref[2] + got_ref[3])
    inverse = lax.rsqrt(total[:, 320:321] / MODEL_WIDTH + EPSILON)
    scaled = total * inverse
    gain = gain_ref[...].astype(f32)
    cosine, sine = cos_ref[...], sin_ref[...]
    parts = [
        norm_rope(scaled[:, j * 128 : (j + 1) * 128], gain, cosine, sine).astype(bf16)
        for j in range(2)
    ]
    parts.append(scaled[:, 256:].astype(bf16))
    out = jnp.concatenate(parts, axis=1)
    out_ref[...] = jnp.broadcast_to(out[None], out_ref.shape)


def attend_kernel(length_ref, block_ref, g_ref, k_ref, v_ref, o_ref, q_scr, n_scr, s_scr):
    step = pl.program_id(0)

    @pl.when(step == 0)
    def _():
        for head in range(QUERY_HEADS):
            w, j = divmod(head, 2)
            q_scr[pl.ds(head, OWN, stride=QUERY_HEADS), :] = g_ref[
                w, :, j * 128 : (j + 1) * 128
            ].astype(f32)

    row = lax.broadcasted_iota(jnp.int32, (16, 256), 0)
    lane = lax.broadcasted_iota(jnp.int32, (16, 256), 1)
    own_half = (row < 8) == (lane < 128)
    place = lax.rem(lax.broadcasted_iota(jnp.int32, (QUERY_HEADS, 128), 1), 8)
    for u in range(AT_ONCE):
        b = step * AT_ONCE + u
        here = pl.ds(pl.multiple_of(b * QUERY_HEADS, QUERY_HEADS), QUERY_HEADS)
        query = q_scr[here, :]
        limit = length_ref[b] - block_ref[b] * BLOCK
        scores = []
        for p in range(4):
            pair = query[16 * p : 16 * p + 16]
            wide_query = jnp.where(own_half, jnp.concatenate([pair, pair], axis=1), 0.0)
            scores.append(
                lax.dot_general(
                    wide_query.astype(bf16),
                    k_ref[u, :, 256 * p : 256 * p + 256],
                    NT,
                    preferred_element_type=f32,
                )
            )
        scores = jnp.concatenate(scores, axis=0) * SCALE
        visible = lax.broadcasted_iota(jnp.int32, scores.shape, 1) < limit
        scores = jnp.where(visible, scores, MASKED)
        highest = jnp.max(scores, axis=1, keepdims=True)
        weights = jnp.where(visible, jnp.exp(scores - highest), 0.0)
        total = jnp.sum(weights, axis=1, keepdims=True)
        weights = weights.astype(bf16)
        sums = []
        for p in range(4):
            both = jnp.dot(
                weights[16 * p : 16 * p + 16],
                v_ref[u, :, 256 * p : 256 * p + 256],
                preferred_element_type=f32,
            )
            sums += [both[:8, :128], both[8:, 128:]]
        n_scr[here, :] = jnp.concatenate(sums, axis=0) / jnp.maximum(total, 1.0)
        stats = jnp.zeros((QUERY_HEADS, 128), f32)
        for at, term in enumerate(three_terms(highest) + three_terms(total)):
            stats = jnp.where(place == at, term, stats)
        s_scr[here, :] = stats

    @pl.when(step == OWN // AT_ONCE - 1)
    def _():
        low = lax.broadcasted_iota(jnp.int32, (OWN, 128), 1) < 8
        for w in range(WIDE):
            rows = [pl.ds(2 * w + j, OWN, stride=QUERY_HEADS) for j in range(2)]
            for j in range(2):
                o_ref[w, :, j * 128 : (j + 1) * 128] = n_scr[rows[j], :].astype(bf16)
            o_ref[w, :, 256:] = jnp.where(low, s_scr[rows[0], :], s_scr[rows[1], :]).astype(bf16)


def combine_kernel(wide_ref, r_ref, g_ref, cos_ref, sin_ref, gain_ref, out_ref):
    wide = wide_ref[0]
    group = wide // 4
    key = jnp.concatenate(
        [g_ref[2 * group, :, 256:320], g_ref[2 * group + 1, :, 256:320]], axis=1
    ).astype(f32)
    value = jnp.concatenate(
        [g_ref[16 + 2 * group, :, 256:320], g_ref[17 + 2 * group, :, 256:320]], axis=1
    ).astype(f32)
    key = norm_rope(key, gain_ref[...].astype(f32), cos_ref[...], sin_ref[...])
    key = key.astype(bf16).astype(f32)
    for j in range(2):
        lanes = slice(j * 128, (j + 1) * 128)
        query = g_ref[wide, :, lanes].astype(f32)
        fresh = jnp.sum(query * key, axis=1, keepdims=True) * SCALE
        stats = r_ref[:, :, 256:].astype(f32)
        base = 8 * j
        tops = (
            stats[:, :, base : base + 1]
            + stats[:, :, base + 1 : base + 2]
            + stats[:, :, base + 2 : base + 3]
        )
        totals = (
            stats[:, :, base + 3 : base + 4]
            + stats[:, :, base + 4 : base + 5]
            + stats[:, :, base + 5 : base + 6]
        )
        highest = jnp.maximum(jnp.max(tops, axis=0), fresh)
        factors = jnp.exp(tops - highest[None]) * totals
        fresh_weight = jnp.exp(fresh - highest)
        weight_sum = jnp.sum(factors, axis=0) + fresh_weight
        numer = jnp.sum(r_ref[:, :, lanes].astype(f32) * factors, axis=0)
        numer = numer + fresh_weight.astype(bf16).astype(f32) * value
        out_ref[:, lanes] = (numer / weight_sum).astype(bf16)


def output_kernel(got_ref, w_ref, out_ref):
    heads = got_ref[...].reshape(-1, got_ref.shape[-1])
    out_ref[...] = jnp.dot(heads, w_ref[...], preferred_element_type=f32).astype(bf16)


def gate_up_kernel(hidden_ref, attended_ref, gain_ref, wg_ref, wu_ref, stream_ref, out_ref):
    stream = hidden_ref[...].astype(f32) + attended_ref[...].astype(f32)
    stream_ref[...] = stream
    square = jnp.sum(stream * stream, axis=1, keepdims=True)
    scaled = (stream * gain_ref[...].astype(f32)).astype(bf16)
    gate = lax.dot_general(scaled, wg_ref[...], NT, preferred_element_type=f32).astype(bf16)
    up = lax.dot_general(scaled, wu_ref[...], NT, preferred_element_type=f32).astype(bf16)
    pad = HALF - HIDDEN_UNITS
    place = lax.broadcasted_iota(jnp.int32, (stream.shape[0], pad), 1)
    norm = jnp.zeros(place.shape, f32)
    for at, term in enumerate(three_terms(square)):
        norm = jnp.where(place == at, term, norm)
    norm = norm.astype(bf16)
    out_ref[...] = jnp.concatenate([gate, norm, up, norm], axis=1).reshape(out_ref.shape)


def activate_kernel(got_ref, out_ref):
    total = jnp.sum(got_ref[...].astype(f32), axis=0)
    square = (
        total[:, HIDDEN_UNITS : HIDDEN_UNITS + 1]
        + total[:, HIDDEN_UNITS + 1 : HIDDEN_UNITS + 2]
        + total[:, HIDDEN_UNITS + 2 : HIDDEN_UNITS + 3]
    )
    inverse = lax.rsqrt(square / MODEL_WIDTH + EPSILON)
    gate = total[:, :HALF] * inverse
    up = total[:, HALF:] * inverse
    activated = (gate / (1.0 + jnp.exp(-gate)) * up).astype(bf16)
    out_ref[...] = jnp.broadcast_to(activated[None], out_ref.shape)


def down_kernel(got_ref, w_ref, out_ref):
    units = got_ref[...].reshape(-1, HALF)
    out_ref[...] = jnp.dot(
        units[:, :HIDDEN_UNITS], w_ref[...], preferred_element_type=f32
    ).astype(bf16)


def final_kernel(stream_ref, down_ref, out_ref):
    out_ref[...] = (stream_ref[...] + down_ref[...].astype(f32)).astype(bf16)


def sum_spread_kernel(got_ref, out_ref):
    total = jnp.sum(got_ref[...].astype(f32), axis=0).astype(bf16)
    out_ref[...] = jnp.broadcast_to(total[None], out_ref.shape)


def exchange(blocks, axes):
    return lax.all_to_all(blocks, axes, split_axis=0, concat_axis=0, tiled=True)


def spread(own, axes, count):
    return exchange(jnp.broadcast_to(own[None], (count, *own.shape)), axes)


def sum_wide(part):
    height, width = part.shape
    piece = (height // 8, width)

    def stage(blocks, axes, count):
        return call(
            sum_spread_kernel,
            jax.ShapeDtypeStruct((count, *piece), bf16),
            [VMEM],
            name="sum_spread",
        )(exchange(blocks, axes))

    over_plane = stage(part.reshape(8, *piece), PLANE, 4)
    total = stage(over_plane, "y", 8)
    return exchange(total, PLANE).reshape(height, width)


def body(
    hidden,
    attn_gain,
    w_query,
    w_keyval,
    query_gain,
    key_norm_gain,
    keys_cache,
    values_cache,
    lengths,
    block_index,
    w_out,
    mlp_gain,
    w_gate,
    w_up,
    w_down,
):
    wide = lax.axis_index(WIDE_AXES).astype(jnp.int32).reshape(1)
    sds = jax.ShapeDtypeStruct

    half = HEAD_WIDTH // 2
    frequency = np.power(ROPE_BASE, -(np.arange(half) * 2.0 / HEAD_WIDTH)).astype(np.float32)
    angles = lengths.astype(f32)[:, None] * jnp.asarray(frequency)[None, :]
    cosine, sine = jnp.cos(angles), jnp.sin(angles)
    cosine = jnp.concatenate([cosine, cosine], axis=1)
    sine = jnp.concatenate([-sine, sine], axis=1)

    blocks = call(
        project_kernel,
        sds((ROWS, OWN, 384), f32),
        [HBM, VMEM, HBM, HBM],
        [
            pltpu.VMEM(hidden.shape, bf16),
            pltpu.VMEM(w_query.shape, bf16),
            pltpu.VMEM(w_keyval.shape[::-1], bf16),
            pltpu.SemaphoreType.DMA((3,)),
        ],
        name="project",
    )(hidden, attn_gain[None], w_query, w_keyval.T)
    payload = call(
        heads_kernel, sds((8, OWN, 384), bf16), [VMEM] * 4, name="heads"
    )(exchange(blocks, "rows"), cosine, sine, query_gain[None])
    gathered = spread(exchange(payload, PLANE), "y", 4).reshape(WIDE, OWN, 384)

    parts = pl.pallas_call(
        attend_kernel,
        out_shape=sds((WIDE, OWN, 384), bf16),
        grid_spec=pltpu.PrefetchScalarGridSpec(
            num_scalar_prefetch=2,
            grid=(OWN // AT_ONCE,),
            in_specs=[
                pl.BlockSpec((WIDE, OWN, 384), lambda b, *_: (0, 0, 0)),
                pl.BlockSpec((AT_ONCE, BLOCK, 1024), lambda b, *_: (b, 0, 0)),
                pl.BlockSpec((AT_ONCE, BLOCK, 1024), lambda b, *_: (b, 0, 0)),
            ],
            out_specs=pl.BlockSpec((WIDE, OWN, 384), lambda b, *_: (0, 0, 0)),
            scratch_shapes=[pltpu.VMEM((OWN * QUERY_HEADS, 128), f32)] * 3,
        ),
        compiler_params=pltpu.CompilerParams(
            dimension_semantics=("arbitrary",), vmem_limit_bytes=56 << 20
        ),
        name="attend",
    )(lengths, block_index.reshape(OWN), gathered, keys_cache, values_cache)
    heads_out = call(
        combine_kernel, sds((OWN, 256), bf16), [SMEM] + [VMEM] * 5, name="combine"
    )(wide, exchange(parts, WIDE_AXES), gathered, cosine, sine, key_norm_gain[None])

    out_part = call(output_kernel, sds((64, 1280), bf16), [VMEM] * 2, name="output")(
        spread(heads_out, "rows", ROWS), w_out
    )
    stream, blocks = call(
        gate_up_kernel,
        [sds((64, 1280), f32), sds((ROWS, OWN, 2 * HALF), bf16)],
        [VMEM] * 5,
        name="gate_up",
    )(hidden, sum_wide(out_part), mlp_gain[None], w_gate.T, w_up.T)
    activated = call(
        activate_kernel, sds((ROWS, OWN, HALF), bf16), [VMEM], name="activate"
    )(exchange(blocks, "rows"))
    down_part = call(down_kernel, sds((64, 1280), bf16), [VMEM] * 2, name="down")(
        exchange(activated, "rows"), w_down
    )
    layer_out = call(final_kernel, sds((64, 1280), bf16), [VMEM] * 2, name="final")(
        stream, sum_wide(down_part)
    )
    return (layer_out, heads_out)


def solution(mesh):
    mesh = jax.sharding.Mesh(
        mesh.devices.reshape(4, 4, 4, 2), ("rows", "y", "z", "core")
    )
    in_specs = (
        P(None, "rows"),
        P("rows"),
        P("rows", WIDE_AXES),
        P("rows", WIDE_AXES),
        P(),
        P(),
        P("rows", WIDE_AXES, None),
        P("rows", WIDE_AXES, None),
        P("rows"),
        P("rows", WIDE_AXES),
        P(WIDE_AXES, "rows"),
        P("rows"),
        P("rows", WIDE_AXES),
        P("rows", WIDE_AXES),
        P(WIDE_AXES, "rows"),
    )
    out_specs = (P(None, "rows"), P("rows", WIDE_AXES))
    return jax.shard_map(body, mesh=mesh, in_specs=in_specs, out_specs=out_specs, check_vma=False)
```

```python
import jax
import jax.numpy as jnp
import numpy as np
from jax import lax
from jax.experimental import pallas as pl
from jax.experimental.pallas import tpu as pltpu
from jax.sharding import PartitionSpec as P

MODEL_WIDTH = 5120
QUERY_HEADS = 64
KEY_VALUE_HEADS = 8
HEAD_WIDTH = 128
EPSILON = 1e-06
ROPE_BASE = 1000000.0
MASKED = -1e30
SCALE = HEAD_WIDTH ** (-0.5)

ROWS = 4
WIDE = 32
PACKED = 40
AT_ONCE = 4
OWN = 16
BLOCK = 256
HIDDEN_UNITS = 800
HALF = 896

f32 = jnp.float32
bf16 = jnp.bfloat16
VMEM = pl.BlockSpec(memory_space=pltpu.VMEM)
HBM = pl.BlockSpec(memory_space=pltpu.HBM)
SMEM = pl.BlockSpec(memory_space=pltpu.SMEM)
NT = (((1,), (1,)), ((), ()))


def call(kernel, out_shape, in_specs, scratch_shapes=(), limit=24, name=None):
    many = isinstance(out_shape, (tuple, list))
    return pl.pallas_call(
        kernel,
        out_shape=out_shape,
        in_specs=in_specs,
        out_specs=[VMEM] * len(out_shape) if many else VMEM,
        scratch_shapes=list(scratch_shapes),
        compiler_params=pltpu.CompilerParams(vmem_limit_bytes=limit << 20),
        name=name,
    )


def row_block(mine, k):
    return pl.ds(pl.multiple_of(lax.rem(mine + k, ROWS) * OWN, OWN), OWN)


def terms(value, count):
    out = []
    for _ in range(count):
        out.append(value.astype(bf16).astype(f32))
        value = value - out[-1]
    return out


def swap_halves(value):
    half = HEAD_WIDTH // 2
    return jnp.concatenate([value[..., half:], value[..., :half]], axis=-1)


def norm_rope(value, straight, swapped):
    value = value * lax.rsqrt(jnp.mean(value * value, axis=-1, keepdims=True) + EPSILON)
    return value * straight + swap_halves(value) * swapped


def pack(value):
    return jnp.concatenate([value[:8], value[8:]], axis=1)


def unpack(value):
    return jnp.concatenate([value[:, :64], value[:, 64:]], axis=0)


def project_kernel(mine_ref, hidden_hbm, gain_ref, wq_hbm, wkv_hbm, *rest):
    outs, (whole, hidden_ref, wq_ref, wkv_ref, sems) = rest[:ROWS], rest[ROWS:]
    moves = [
        pltpu.make_async_copy(source, target, sems.at[at])
        for at, (source, target) in enumerate(
            ((hidden_hbm, hidden_ref), (wkv_hbm, wkv_ref), (wq_hbm, wq_ref))
        )
    ]
    for move in moves:
        move.start()
    moves[0].wait()
    hidden = hidden_ref[...].astype(f32)
    square = jnp.sum(hidden * hidden, axis=1, keepdims=True)
    scaled = (hidden * gain_ref[...].astype(f32)).astype(bf16)
    moves[1].wait()
    keyval = lax.dot_general(scaled, wkv_ref[...], NT, preferred_element_type=f32)
    whole[:, 256:] = jnp.concatenate([keyval, jnp.broadcast_to(square, keyval.shape)], axis=1)
    moves[2].wait()
    whole[:, :256] = jnp.dot(scaled, wq_ref[...], preferred_element_type=f32)
    mine = mine_ref[0]
    for k in range(ROWS):
        outs[k][...] = whole[row_block(mine, k), :]


def heads_kernel(a_ref, b_ref, c_ref, d_ref, straight_ref, swapped_ref, out_ref):
    total = (a_ref[...] + b_ref[...]) + (c_ref[...] + d_ref[...])
    inverse = lax.rsqrt(total[:, 320:321] / MODEL_WIDTH + EPSILON)
    scaled = total * inverse
    straight, swapped = straight_ref[0], swapped_ref[0]
    parts = [
        norm_rope(scaled[:, j * 128 : (j + 1) * 128], straight, swapped) for j in range(2)
    ]
    parts.append(pack(scaled[:, 256:320]))
    out = jnp.concatenate(parts, axis=0).astype(bf16)
    out_ref[...] = jnp.broadcast_to(out[None], out_ref.shape)


def attend_kernel(
    length_ref,
    block_ref,
    g_ref,
    k_hbm,
    v_hbm,
    o_ref,
    k_scr,
    v_scr,
    q_scr,
    p_scr,
    w_scr,
    n_scr,
    s_scr,
    k_sems,
    v_sems,
):
    def k_move(b):
        return pltpu.make_async_copy(k_hbm.at[b], k_scr.at[b], k_sems.at[b])

    def v_move(b):
        return pltpu.make_async_copy(v_hbm.at[b], v_scr.at[b], v_sems.at[b])

    for b in range(OWN):
        k_move(b).start()
    for b in range(OWN):
        v_move(b).start()

    for head in range(QUERY_HEADS):
        w, j = divmod(head, 2)
        q_scr[pl.ds(head, OWN, stride=QUERY_HEADS), :] = g_ref[
            w, j * OWN : (j + 1) * OWN, :
        ].astype(f32)

    def rows_of(b, start, size):
        return pl.ds(pl.multiple_of(b * QUERY_HEADS + start, 16), size)

    def limit(b):
        return length_ref[b] - block_ref[b] * BLOCK

    row = lax.broadcasted_iota(jnp.int32, (16, 256), 0)
    lane = lax.broadcasted_iota(jnp.int32, (16, 256), 1)
    own_half = (row < 8) == (lane < 128)
    slot = lax.broadcasted_iota(jnp.int32, (QUERY_HEADS, 256), 1)
    place = lax.rem(lax.broadcasted_iota(jnp.int32, (QUERY_HEADS, 128), 1), 8)

    @pl.loop(0, OWN // AT_ONCE)
    def _(step):
        for u in range(AT_ONCE):
            k_move(step * AT_ONCE + u).wait()
        for u in range(AT_ONCE):
            b = step * AT_ONCE + u
            for p in range(4):
                here = rows_of(b, 16 * p, 16)
                pair = q_scr[here, :]
                query = jnp.where(own_half, jnp.concatenate([pair, pair], axis=1), 0.0)
                p_scr[here, :] = lax.dot_general(
                    query.astype(bf16),
                    k_scr[b, :, 256 * p : 256 * p + 256],
                    NT,
                    preferred_element_type=f32,
                )

    @pl.loop(0, OWN // AT_ONCE)
    def _(step):
        for u in range(AT_ONCE):
            b = step * AT_ONCE + u
            here = rows_of(b, 0, QUERY_HEADS)
            visible = slot < limit(b)
            scores = jnp.where(visible, p_scr[here, :] * SCALE, MASKED)
            shift = jnp.max(scores, axis=1, keepdims=True).astype(bf16).astype(f32)
            weights = jnp.where(visible, jnp.exp(scores - shift), 0.0)
            total = jnp.sum(weights, axis=1, keepdims=True)
            w_scr[here, :] = weights.astype(bf16)
            stats = jnp.where(place == 0, shift, 0.0)
            for at, term in enumerate(terms(total, 2)):
                stats = jnp.where(place == at + 1, term, stats)
            s_scr[here, :] = stats

    @pl.loop(0, OWN // AT_ONCE)
    def _(step):
        for u in range(AT_ONCE):
            v_move(step * AT_ONCE + u).wait()
        for u in range(AT_ONCE):
            b = step * AT_ONCE + u
            for p in range(4):
                here = rows_of(b, 16 * p, 16)
                both = jnp.dot(
                    w_scr[here, :],
                    v_scr[b, :, 256 * p : 256 * p + 256],
                    preferred_element_type=f32,
                )
                n_scr[here, :] = jnp.concatenate([both[:8, :128], both[8:, 128:]], axis=0)

    lane = lax.broadcasted_iota(jnp.int32, (OWN, 128), 1)
    first = lax.rem(lane, 64) < 8
    for w in range(WIDE):
        rows = [pl.ds(2 * w + j, OWN, stride=QUERY_HEADS) for j in range(2)]
        for j in range(2):
            o_ref[w, j * OWN : (j + 1) * OWN, :] = n_scr[rows[j], :].astype(bf16)
        stats = jnp.where(first, s_scr[rows[0], :], s_scr[rows[1], :])
        o_ref[w, 2 * OWN :, :] = jnp.where(lane[:8] < 64, stats[:8], stats[8:]).astype(bf16)


def combine_kernel(wide_ref, r_ref, g_ref, straight_ref, swapped_ref, out_ref, again_ref):
    wide = wide_ref[0]
    group = wide // 4

    def half(source):
        return unpack(g_ref[source, 2 * OWN :, :].astype(f32))

    key = jnp.concatenate([half(2 * group), half(2 * group + 1)], axis=1)
    value = jnp.concatenate([half(16 + 2 * group), half(17 + 2 * group)], axis=1)
    key = norm_rope(key, straight_ref[1], swapped_ref[1]).astype(bf16).astype(f32)
    stats = r_ref[:, 2 * OWN :, :].astype(f32)

    def stat(at):
        return jnp.concatenate(
            [stats[:, :, at : at + 1], stats[:, :, 64 + at : 65 + at]], axis=1
        )

    for j in range(2):
        lanes = slice(j * 128, (j + 1) * 128)
        here = slice(j * OWN, (j + 1) * OWN)
        query = g_ref[wide, here, :].astype(f32)
        fresh = jnp.sum(query * key, axis=1, keepdims=True) * SCALE
        shifts = stat(8 * j)
        totals = stat(8 * j + 1) + stat(8 * j + 2)
        highest = jnp.maximum(jnp.max(shifts, axis=0), fresh)
        factors = jnp.exp(shifts - highest[None])
        fresh_weight = jnp.exp(fresh - highest)
        weight_sum = jnp.sum(factors * totals, axis=0) + fresh_weight
        numer = jnp.sum(r_ref[:, here, :].astype(f32) * factors, axis=0)
        numer = numer + fresh_weight.astype(bf16).astype(f32) * value
        heads = (numer / weight_sum).astype(bf16)
        out_ref[:, lanes] = heads
        again_ref[:, lanes] = heads


def output_kernel(a_ref, b_ref, c_ref, d_ref, w_ref, out_ref):
    heads = jnp.concatenate([a_ref[...], b_ref[...], c_ref[...], d_ref[...]], axis=0)
    out_ref[...] = jnp.dot(heads, w_ref[...], preferred_element_type=f32).astype(bf16)


def gate_up_kernel(mine_ref, hidden_ref, attended_ref, gain_ref, wg_ref, wu_ref, stream_ref, *outs):
    mine = mine_ref[0]
    for k in range(ROWS):
        at = slice(k * OWN, (k + 1) * OWN)
        stream_ref[at, :] = hidden_ref[row_block(mine, k), :].astype(f32) + attended_ref[
            at, :
        ].astype(f32)
    stream = stream_ref[...]
    square = jnp.sum(stream * stream, axis=1, keepdims=True)
    scaled = (stream * gain_ref[...].astype(f32)).astype(bf16)
    gate = lax.dot_general(scaled, wg_ref[...], NT, preferred_element_type=f32).astype(bf16)
    up = lax.dot_general(scaled, wu_ref[...], NT, preferred_element_type=f32).astype(bf16)
    pad = HALF - HIDDEN_UNITS
    place = lax.broadcasted_iota(jnp.int32, (stream.shape[0], pad), 1)
    norm = jnp.zeros(place.shape, f32)
    for at, term in enumerate(terms(square, 3)):
        norm = jnp.where(place == at, term, norm)
    norm = norm.astype(bf16)
    for k in range(ROWS):
        at = slice(k * OWN, (k + 1) * OWN)
        outs[k][...] = jnp.concatenate([gate[at], norm[at], up[at], norm[at]], axis=1)


def activate_kernel(a_ref, b_ref, c_ref, d_ref, out_ref):
    total = (a_ref[...].astype(f32) + b_ref[...].astype(f32)) + (
        c_ref[...].astype(f32) + d_ref[...].astype(f32)
    )
    square = (
        total[:, HIDDEN_UNITS : HIDDEN_UNITS + 1]
        + total[:, HIDDEN_UNITS + 1 : HIDDEN_UNITS + 2]
        + total[:, HIDDEN_UNITS + 2 : HIDDEN_UNITS + 3]
    )
    inverse = lax.rsqrt(square / MODEL_WIDTH + EPSILON)
    gate = total[:, :HALF] * inverse
    up = total[:, HALF:] * inverse
    out_ref[...] = (gate / (1.0 + jnp.exp(-gate)) * up).astype(bf16)


def down_kernel(a_ref, b_ref, c_ref, d_ref, w_ref, out_ref):
    units = jnp.concatenate([a_ref[...], b_ref[...], c_ref[...], d_ref[...]], axis=0)
    out_ref[...] = jnp.dot(
        units[:, :HIDDEN_UNITS], w_ref[...], preferred_element_type=f32
    ).astype(bf16)


def final_kernel(mine_ref, stream_ref, down_ref, out_ref):
    mine = mine_ref[0]
    for k in range(ROWS):
        at = slice(k * OWN, (k + 1) * OWN)
        out_ref[row_block(mine, k), :] = (stream_ref[at, :] + down_ref[at, :].astype(f32)).astype(
            bf16
        )


def to_rows(blocks):
    got = [blocks[0]]
    for k in range(1, ROWS):
        got.append(lax.ppermute(blocks[k], "rows", [(i, (i + k) % ROWS) for i in range(ROWS)]))
    return got


def from_rows(own):
    got = [own]
    for k in range(1, ROWS):
        got.append(lax.ppermute(own, "rows", [((i + k) % ROWS, i) for i in range(ROWS)]))
    return got


def exchange(blocks):
    return lax.all_to_all(blocks, "wide", split_axis=0, concat_axis=0, tiled=True)


def sum_wide(part):
    height, width = part.shape
    got = exchange(part.reshape(WIDE, height // WIDE, width))
    total = jnp.sum(got.astype(f32), axis=0).astype(bf16)
    return exchange(jnp.broadcast_to(total[None], got.shape)).reshape(height, width)


def body(
    hidden,
    attn_gain,
    w_query,
    w_keyval,
    query_gain,
    key_norm_gain,
    keys_cache,
    values_cache,
    lengths,
    block_index,
    w_out,
    mlp_gain,
    w_gate,
    w_up,
    w_down,
):
    mine = lax.axis_index("rows").astype(jnp.int32).reshape(1)
    wide = lax.axis_index("wide").astype(jnp.int32).reshape(1)
    sds = jax.ShapeDtypeStruct

    half = HEAD_WIDTH // 2
    frequency = np.power(ROPE_BASE, -(np.arange(half) * 2.0 / HEAD_WIDTH)).astype(np.float32)
    angles = lengths.astype(f32)[:, None] * jnp.asarray(frequency)[None, :]
    cosine, sine = jnp.cos(angles), jnp.sin(angles)
    gains = jnp.stack([query_gain, key_norm_gain]).astype(f32)[:, None, :]
    straight = gains * jnp.concatenate([cosine, cosine], axis=1)
    swapped = swap_halves(gains) * jnp.concatenate([-sine, sine], axis=1)

    blocks = call(
        project_kernel,
        [sds((OWN, 384), f32)] * ROWS,
        [SMEM, HBM, VMEM, HBM, HBM],
        [
            pltpu.VMEM((64, 384), f32),
            pltpu.VMEM(hidden.shape, bf16),
            pltpu.VMEM(w_query.shape, bf16),
            pltpu.VMEM(w_keyval.shape[::-1], bf16),
            pltpu.SemaphoreType.DMA((3,)),
        ],
        limit=60,
        name="project",
    )(mine, hidden, attn_gain[None], w_query, w_keyval.T)
    payload = call(
        heads_kernel, sds((WIDE, PACKED, 128), bf16), [VMEM] * 6, limit=8, name="heads"
    )(*to_rows(blocks), straight, swapped)
    gathered = exchange(payload)

    parts = call(
        attend_kernel,
        sds((WIDE, PACKED, 128), bf16),
        [SMEM, SMEM, VMEM, HBM, HBM],
        [
            pltpu.VMEM(keys_cache.shape, bf16),
            pltpu.VMEM(values_cache.shape, bf16),
            pltpu.VMEM((OWN * QUERY_HEADS, 128), f32),
            pltpu.VMEM((OWN * QUERY_HEADS, 256), f32),
            pltpu.VMEM((OWN * QUERY_HEADS, 256), bf16),
            pltpu.VMEM((OWN * QUERY_HEADS, 128), f32),
            pltpu.VMEM((OWN * QUERY_HEADS, 128), f32),
            pltpu.SemaphoreType.DMA((OWN,)),
            pltpu.SemaphoreType.DMA((OWN,)),
        ],
        limit=57,
        name="attend",
    )(lengths, block_index.reshape(OWN), gathered, keys_cache, values_cache)
    heads_out, heads_own = call(
        combine_kernel, [sds((OWN, 256), bf16)] * 2, [SMEM] + [VMEM] * 4, limit=8, name="combine"
    )(wide, exchange(parts), gathered, straight, swapped)

    out_part = call(output_kernel, sds((64, 1280), bf16), [VMEM] * 5, limit=8, name="output")(
        *from_rows(heads_own), w_out
    )
    attended = sum_wide(out_part)

    stream, *blocks = call(
        gate_up_kernel,
        [sds((64, 1280), f32)] + [sds((OWN, 2 * HALF), bf16)] * ROWS,
        [SMEM] + [VMEM] * 5,
        limit=16,
        name="gate_up",
    )(mine, hidden, attended, mlp_gain[None], w_gate.T, w_up.T)
    activated = call(
        activate_kernel, sds((OWN, HALF), bf16), [VMEM] * 4, limit=8, name="activate"
    )(*to_rows(blocks))
    down_part = call(down_kernel, sds((64, 1280), bf16), [VMEM] * 5, limit=8, name="down")(
        *from_rows(activated), w_down
    )
    layer_out = call(final_kernel, sds((64, 1280), bf16), [SMEM] + [VMEM] * 2, limit=8, name="final")(
        mine, stream, sum_wide(down_part)
    )
    return (layer_out, heads_out)


def solution(mesh):
    in_specs = (
        P(None, "rows"),
        P("rows"),
        P("rows", "wide"),
        P("rows", "wide"),
        P(),
        P(),
        P("rows", "wide", None),
        P("rows", "wide", None),
        P("rows"),
        P("rows", "wide"),
        P("wide", "rows"),
        P("rows"),
        P("rows", "wide"),
        P("rows", "wide"),
        P("wide", "rows"),
    )
    out_specs = (P(None, "rows"), P("rows", "wide"))
    return jax.shard_map(body, mesh=mesh, in_specs=in_specs, out_specs=out_specs, check_vma=False)
```

```python
import jax
import jax.numpy as jnp
import numpy as np
from jax import lax
from jax.experimental import pallas as pl
from jax.experimental.pallas import tpu as pltpu
from jax.sharding import PartitionSpec as P

MODEL_WIDTH = 5120
QUERY_HEADS = 64
KEY_VALUE_HEADS = 8
HEAD_WIDTH = 128
EPSILON = 1e-06
ROPE_BASE = 1000000.0
MASKED = -1e30
SCALE = HEAD_WIDTH ** (-0.5)

ROWS = 4
WIDE = 32
PACKED = 40
AT_ONCE = 2
OWN = 16
BLOCK = 256
HIDDEN_UNITS = 800
HALF = 896

f32 = jnp.float32
bf16 = jnp.bfloat16
VMEM = pl.BlockSpec(memory_space=pltpu.VMEM)
HBM = pl.BlockSpec(memory_space=pltpu.HBM)
SMEM = pl.BlockSpec(memory_space=pltpu.SMEM)
NT = (((1,), (1,)), ((), ()))


def call(
    kernel, out_shape, in_specs, scratch_shapes=(), limit=24, name=None, out_spec=VMEM, cost=None
):
    many = isinstance(out_shape, (tuple, list))
    return pl.pallas_call(
        kernel,
        out_shape=out_shape,
        in_specs=in_specs,
        out_specs=[out_spec] * len(out_shape) if many else out_spec,
        scratch_shapes=list(scratch_shapes),
        compiler_params=pltpu.CompilerParams(vmem_limit_bytes=limit << 20),
        cost_estimate=cost,
        name=name,
    )


def in_hbm(value):
    return pltpu.with_memory_space_constraint(value, pltpu.HBM)


def in_vmem(value):
    return pltpu.with_memory_space_constraint(value, pltpu.VMEM)


def row_block(mine, k):
    return pl.ds(pl.multiple_of(lax.rem(mine + k, ROWS) * OWN, OWN), OWN)


def terms(value, count):
    out = []
    for _ in range(count):
        out.append(value.astype(bf16).astype(f32))
        value = value - out[-1]
    return out


def swap_halves(value):
    half = HEAD_WIDTH // 2
    return jnp.concatenate([value[..., half:], value[..., :half]], axis=-1)


def norm_rope(value, straight, swapped):
    value = value * lax.rsqrt(jnp.mean(value * value, axis=-1, keepdims=True) + EPSILON)
    return value * straight + swap_halves(value) * swapped


def pack(value):
    return jnp.concatenate([value[:8], value[8:]], axis=1)


def unpack(value):
    return jnp.concatenate([value[:, :64], value[:, 64:]], axis=0)


def project_kernel(mine_ref, hidden_hbm, gain_ref, wq_hbm, wkv_hbm, *rest):
    outs, (whole, hidden_ref, wq_ref, wkv_ref, sems) = rest[:ROWS], rest[ROWS:]
    moves = [
        pltpu.make_async_copy(source, target, sems.at[at])
        for at, (source, target) in enumerate(
            ((hidden_hbm, hidden_ref), (wkv_hbm, wkv_ref), (wq_hbm, wq_ref))
        )
    ]
    for move in moves:
        move.start()
    moves[0].wait()
    hidden = hidden_ref[...].astype(f32)
    square = jnp.sum(hidden * hidden, axis=1, keepdims=True)
    scaled = (hidden * gain_ref[...].astype(f32)).astype(bf16)
    moves[1].wait()
    keyval = lax.dot_general(scaled, wkv_ref[...], NT, preferred_element_type=f32)
    whole[:, 256:] = jnp.concatenate([keyval, jnp.broadcast_to(square, keyval.shape)], axis=1)
    moves[2].wait()
    whole[:, :256] = jnp.dot(scaled, wq_ref[...], preferred_element_type=f32)
    mine = mine_ref[0]
    for k in range(ROWS):
        outs[k][...] = whole[row_block(mine, k), :]


def heads_kernel(a_ref, b_ref, c_ref, d_ref, straight_ref, swapped_ref, out_ref):
    total = (a_ref[...] + b_ref[...]) + (c_ref[...] + d_ref[...])
    inverse = lax.rsqrt(total[:, 320:321] / MODEL_WIDTH + EPSILON)
    scaled = total * inverse
    straight, swapped = straight_ref[0], swapped_ref[0]
    parts = [
        norm_rope(scaled[:, j * 128 : (j + 1) * 128], straight, swapped) for j in range(2)
    ]
    parts.append(pack(scaled[:, 256:320]))
    out = jnp.concatenate(parts, axis=0).astype(bf16)
    out_ref[...] = jnp.broadcast_to(out[None], out_ref.shape)


def load_kernel(after_ref, k_hbm, v_hbm, k_out, v_out, sems):
    del after_ref
    moves = []
    for at, (source, target) in enumerate(((k_hbm, k_out), (v_hbm, v_out))):
        for b in range(OWN):
            moves.append(pltpu.make_async_copy(source.at[b], target.at[b], sems.at[at, b]))
    for move in moves:
        move.start()
    for move in moves:
        move.wait()


def attend_kernel(
    length_ref, block_ref, g_ref, k_ref, v_ref, o_ref, q_scr, p_scr, w_scr, n_scr, s_scr
):
    for head in range(QUERY_HEADS):
        w, j = divmod(head, 2)
        q_scr[pl.ds(head, OWN, stride=QUERY_HEADS), :] = g_ref[
            w, j * OWN : (j + 1) * OWN, :
        ].astype(f32)

    row = lax.broadcasted_iota(jnp.int32, (16, 256), 0)
    lane = lax.broadcasted_iota(jnp.int32, (16, 256), 1)
    own_half = (row < 8) == (lane < 128)
    slot = lax.broadcasted_iota(jnp.int32, (QUERY_HEADS, 256), 1)
    place = lax.rem(lax.broadcasted_iota(jnp.int32, (QUERY_HEADS, 128), 1), 8)

    def score(group):
        for u in range(AT_ONCE):
            b = group * AT_ONCE + u
            for p in range(4):
                here = pl.ds(pl.multiple_of(b * QUERY_HEADS + 16 * p, 16), 16)
                pair = q_scr[here, :]
                query = jnp.where(own_half, jnp.concatenate([pair, pair], axis=1), 0.0)
                p_scr[here, :] = lax.dot_general(
                    query.astype(bf16),
                    k_ref[b, :, 256 * p : 256 * p + 256],
                    NT,
                    preferred_element_type=f32,
                )

    def weigh(group):
        for u in range(AT_ONCE):
            b = group * AT_ONCE + u
            here = pl.ds(pl.multiple_of(b * QUERY_HEADS, QUERY_HEADS), QUERY_HEADS)
            visible = slot < length_ref[b] - block_ref[b] * BLOCK
            scores = jnp.where(visible, p_scr[here, :] * SCALE, MASKED)
            shift = jnp.max(scores, axis=1, keepdims=True).astype(bf16).astype(f32)
            weights = jnp.where(visible, jnp.exp(scores - shift), 0.0)
            total = jnp.sum(weights, axis=1, keepdims=True)
            w_scr[here, :] = weights.astype(bf16)
            stats = jnp.where(place == 0, shift, 0.0)
            for at, term in enumerate(terms(total, 2)):
                stats = jnp.where(place == at + 1, term, stats)
            s_scr[pl.ds(b, QUERY_HEADS, stride=OWN), :] = stats

    def add_up(group):
        for u in range(AT_ONCE):
            b = group * AT_ONCE + u
            for p in range(4):
                here = pl.ds(pl.multiple_of(b * QUERY_HEADS + 16 * p, 16), 16)
                both = jnp.dot(
                    w_scr[here, :],
                    v_ref[b, :, 256 * p : 256 * p + 256],
                    preferred_element_type=f32,
                )
                n_scr[pl.ds(16 * p * OWN + b, 16, stride=OWN), :] = jnp.concatenate(
                    [both[:8, :128], both[8:, 128:]], axis=0
                )

    last = OWN // AT_ONCE - 1
    score(0)
    weigh(0)
    score(1)

    @pl.loop(1, last)
    def _(group):
        add_up(group - 1)
        weigh(group)
        score(group + 1)

    add_up(last - 1)
    weigh(last)
    add_up(last)

    lane = lax.broadcasted_iota(jnp.int32, (OWN, 128), 1)
    first = lax.rem(lane, 64) < 8
    for w in range(WIDE):
        rows = [slice((2 * w + j) * OWN, (2 * w + j + 1) * OWN) for j in range(2)]
        o_ref[w, : 2 * OWN, :] = n_scr[2 * w * OWN : 2 * (w + 1) * OWN, :].astype(bf16)
        stats = jnp.where(first, s_scr[rows[0], :], s_scr[rows[1], :])
        o_ref[w, 2 * OWN :, :] = jnp.where(lane[:8] < 64, stats[:8], stats[8:]).astype(bf16)


def combine_kernel(wide_ref, r_ref, g_ref, straight_ref, swapped_ref, out_ref, again_ref):
    wide = wide_ref[0]
    group = wide // 4

    def half(source):
        return unpack(g_ref[source, 2 * OWN :, :].astype(f32))

    key = jnp.concatenate([half(2 * group), half(2 * group + 1)], axis=1)
    value = jnp.concatenate([half(16 + 2 * group), half(17 + 2 * group)], axis=1)
    key = norm_rope(key, straight_ref[1], swapped_ref[1]).astype(bf16).astype(f32)
    stats = r_ref[:, 2 * OWN :, :].astype(f32)

    def stat(at):
        return jnp.concatenate(
            [stats[:, :, at : at + 1], stats[:, :, 64 + at : 65 + at]], axis=1
        )

    for j in range(2):
        lanes = slice(j * 128, (j + 1) * 128)
        here = slice(j * OWN, (j + 1) * OWN)
        query = g_ref[wide, here, :].astype(f32)
        fresh = jnp.sum(query * key, axis=1, keepdims=True) * SCALE
        shifts = stat(8 * j)
        totals = stat(8 * j + 1) + stat(8 * j + 2)
        highest = jnp.maximum(jnp.max(shifts, axis=0), fresh)
        factors = jnp.exp(shifts - highest[None])
        fresh_weight = jnp.exp(fresh - highest)
        weight_sum = jnp.sum(factors * totals, axis=0) + fresh_weight
        numer = jnp.sum(r_ref[:, here, :].astype(f32) * factors, axis=0)
        numer = numer + fresh_weight.astype(bf16).astype(f32) * value
        heads = (numer / weight_sum).astype(bf16)
        out_ref[:, lanes] = heads
        again_ref[:, lanes] = heads


def output_kernel(a_ref, b_ref, c_ref, d_ref, w_ref, out_ref):
    heads = jnp.concatenate([a_ref[...], b_ref[...], c_ref[...], d_ref[...]], axis=0)
    out_ref[...] = jnp.dot(heads, w_ref[...], preferred_element_type=f32).astype(bf16)


def gate_up_kernel(mine_ref, hidden_ref, attended_ref, gain_ref, wg_ref, wu_ref, stream_ref, *outs):
    mine = mine_ref[0]
    for k in range(ROWS):
        at = slice(k * OWN, (k + 1) * OWN)
        stream_ref[at, :] = hidden_ref[row_block(mine, k), :].astype(f32) + attended_ref[
            at, :
        ].astype(f32)
    stream = stream_ref[...]
    square = jnp.sum(stream * stream, axis=1, keepdims=True)
    scaled = (stream * gain_ref[...].astype(f32)).astype(bf16)
    gate = lax.dot_general(scaled, wg_ref[...], NT, preferred_element_type=f32).astype(bf16)
    up = lax.dot_general(scaled, wu_ref[...], NT, preferred_element_type=f32).astype(bf16)
    pad = HALF - HIDDEN_UNITS
    place = lax.broadcasted_iota(jnp.int32, (stream.shape[0], pad), 1)
    norm = jnp.zeros(place.shape, f32)
    for at, term in enumerate(terms(square, 3)):
        norm = jnp.where(place == at, term, norm)
    norm = norm.astype(bf16)
    for k in range(ROWS):
        at = slice(k * OWN, (k + 1) * OWN)
        outs[k][...] = jnp.concatenate([gate[at], norm[at], up[at], norm[at]], axis=1)


def activate_kernel(a_ref, b_ref, c_ref, d_ref, out_ref):
    total = (a_ref[...].astype(f32) + b_ref[...].astype(f32)) + (
        c_ref[...].astype(f32) + d_ref[...].astype(f32)
    )
    square = (
        total[:, HIDDEN_UNITS : HIDDEN_UNITS + 1]
        + total[:, HIDDEN_UNITS + 1 : HIDDEN_UNITS + 2]
        + total[:, HIDDEN_UNITS + 2 : HIDDEN_UNITS + 3]
    )
    inverse = lax.rsqrt(square / MODEL_WIDTH + EPSILON)
    gate = total[:, :HALF] * inverse
    up = total[:, HALF:] * inverse
    out_ref[...] = (gate / (1.0 + jnp.exp(-gate)) * up).astype(bf16)


def down_kernel(a_ref, b_ref, c_ref, d_ref, w_ref, out_ref):
    units = jnp.concatenate([a_ref[...], b_ref[...], c_ref[...], d_ref[...]], axis=0)
    out_ref[...] = jnp.dot(
        units[:, :HIDDEN_UNITS], w_ref[...], preferred_element_type=f32
    ).astype(bf16)


def final_kernel(mine_ref, stream_ref, down_ref, out_ref):
    mine = mine_ref[0]
    for k in range(ROWS):
        at = slice(k * OWN, (k + 1) * OWN)
        out_ref[row_block(mine, k), :] = (stream_ref[at, :] + down_ref[at, :].astype(f32)).astype(
            bf16
        )


def to_rows(blocks):
    got = [blocks[0]]
    for k in range(1, ROWS):
        got.append(lax.ppermute(blocks[k], "rows", [(i, (i + k) % ROWS) for i in range(ROWS)]))
    return got


def from_rows(own):
    got = [own]
    for k in range(1, ROWS):
        got.append(lax.ppermute(own, "rows", [((i + k) % ROWS, i) for i in range(ROWS)]))
    return got


def exchange(blocks):
    return lax.all_to_all(blocks, "wide", split_axis=0, concat_axis=0, tiled=True)


def sum_wide(part):
    height, width = part.shape
    got = exchange(part.reshape(WIDE, height // WIDE, width))
    total = jnp.sum(got.astype(f32), axis=0).astype(bf16)
    return exchange(jnp.broadcast_to(total[None], got.shape)).reshape(height, width)


def body(
    hidden,
    attn_gain,
    w_query,
    w_keyval,
    query_gain,
    key_norm_gain,
    keys_cache,
    values_cache,
    lengths,
    block_index,
    w_out,
    mlp_gain,
    w_gate,
    w_up,
    w_down,
):
    mine = lax.axis_index("rows").astype(jnp.int32).reshape(1)
    wide = lax.axis_index("wide").astype(jnp.int32).reshape(1)
    sds = jax.ShapeDtypeStruct

    half = HEAD_WIDTH // 2
    frequency = np.power(ROPE_BASE, -(np.arange(half) * 2.0 / HEAD_WIDTH)).astype(np.float32)
    angles = lengths.astype(f32)[:, None] * jnp.asarray(frequency)[None, :]
    cosine, sine = jnp.cos(angles), jnp.sin(angles)
    gains = jnp.stack([query_gain, key_norm_gain]).astype(f32)[:, None, :]
    straight = gains * jnp.concatenate([cosine, cosine], axis=1)
    swapped = swap_halves(gains) * jnp.concatenate([-sine, sine], axis=1)

    blocks = call(
        project_kernel,
        [sds((OWN, 384), f32)] * ROWS,
        [SMEM, HBM, VMEM, HBM, HBM],
        [
            pltpu.VMEM((64, 384), f32),
            pltpu.VMEM(hidden.shape, bf16),
            pltpu.VMEM(w_query.shape, bf16),
            pltpu.VMEM(w_keyval.shape[::-1], bf16),
            pltpu.SemaphoreType.DMA((3,)),
        ],
        limit=8,
        name="project",
    )(mine, in_hbm(hidden), attn_gain[None], in_hbm(w_query), in_hbm(w_keyval.T))
    payload = call(
        heads_kernel, sds((WIDE, PACKED, 128), bf16), [VMEM] * 6, limit=8, name="heads"
    )(*to_rows(blocks), straight, swapped)
    gathered = exchange(payload)

    keys, values = call(
        load_kernel,
        [pltpu.VMEM(keys_cache.shape, bf16)] * 2,
        [pl.BlockSpec(memory_space=pl.ANY)] + [HBM] * 2,
        [pltpu.SemaphoreType.DMA((2, OWN))],
        limit=1,
        name="load",
        out_spec=pl.BlockSpec(memory_space=pl.ANY),
        cost=pl.CostEstimate(flops=0, bytes_accessed=4 * keys_cache.size, transcendentals=0),
    )(payload, in_hbm(keys_cache), in_hbm(values_cache))
    parts = call(
        attend_kernel,
        sds((WIDE, PACKED, 128), bf16),
        [SMEM, SMEM] + [VMEM] * 3,
        [
            pltpu.VMEM((OWN * QUERY_HEADS, 128), f32),
            pltpu.VMEM((OWN * QUERY_HEADS, 256), f32),
            pltpu.VMEM((OWN * QUERY_HEADS, 256), bf16),
            pltpu.VMEM((OWN * QUERY_HEADS, 128), f32),
            pltpu.VMEM((OWN * QUERY_HEADS, 128), f32),
        ],
        limit=12,
        name="attend",
    )(lengths, block_index.reshape(OWN), gathered, in_vmem(keys), in_vmem(values))
    heads_out, heads_own = call(
        combine_kernel, [sds((OWN, 256), bf16)] * 2, [SMEM] + [VMEM] * 4, limit=8, name="combine"
    )(wide, exchange(parts), gathered, straight, swapped)

    out_part = call(output_kernel, sds((64, 1280), bf16), [VMEM] * 5, limit=8, name="output")(
        *from_rows(heads_own), w_out
    )
    attended = sum_wide(out_part)

    stream, *blocks = call(
        gate_up_kernel,
        [sds((64, 1280), f32)] + [sds((OWN, 2 * HALF), bf16)] * ROWS,
        [SMEM] + [VMEM] * 5,
        limit=16,
        name="gate_up",
    )(mine, hidden, attended, mlp_gain[None], w_gate.T, w_up.T)
    activated = call(
        activate_kernel, sds((OWN, HALF), bf16), [VMEM] * 4, limit=8, name="activate"
    )(*to_rows(blocks))
    down_part = call(down_kernel, sds((64, 1280), bf16), [VMEM] * 5, limit=8, name="down")(
        *from_rows(activated), w_down
    )
    layer_out = call(final_kernel, sds((64, 1280), bf16), [SMEM] + [VMEM] * 2, limit=8, name="final")(
        mine, stream, sum_wide(down_part)
    )
    return (layer_out, heads_out)


def solution(mesh):
    in_specs = (
        P(None, "rows"),
        P("rows"),
        P("rows", "wide"),
        P("rows", "wide"),
        P(),
        P(),
        P("rows", "wide", None),
        P("rows", "wide", None),
        P("rows"),
        P("rows", "wide"),
        P("wide", "rows"),
        P("rows"),
        P("rows", "wide"),
        P("rows", "wide"),
        P("wide", "rows"),
    )
    out_specs = (P(None, "rows"), P("rows", "wide"))
    return jax.shard_map(body, mesh=mesh, in_specs=in_specs, out_specs=out_specs, check_vma=False)
```

```python
import jax
import jax.numpy as jnp
import numpy as np
from jax import lax
from jax.experimental import pallas as pl
from jax.experimental.pallas import tpu as pltpu
from jax.sharding import PartitionSpec as P

MODEL_WIDTH = 5120
QUERY_HEADS = 64
KEY_VALUE_HEADS = 8
HEAD_WIDTH = 128
EPSILON = 1e-06
ROPE_BASE = 1000000.0
MASKED = -1e30
SCALE = HEAD_WIDTH ** (-0.5)

ROWS = 4
WIDE = 32
PACKED = 40
AT_ONCE = 2
GROUPS = 8
OWN = 16
BLOCK = 256
HIDDEN_UNITS = 800
HALF = 896

f32 = jnp.float32
bf16 = jnp.bfloat16
VMEM = pl.BlockSpec(memory_space=pltpu.VMEM)
HBM = pl.BlockSpec(memory_space=pltpu.HBM)
SMEM = pl.BlockSpec(memory_space=pltpu.SMEM)
NT = (((1,), (1,)), ((), ()))


def call(
    kernel, out_shape, in_specs, scratch_shapes=(), limit=24, name=None, cost=None
):
    many = isinstance(out_shape, (tuple, list))
    return pl.pallas_call(
        kernel,
        out_shape=out_shape,
        in_specs=in_specs,
        out_specs=[VMEM] * len(out_shape) if many else VMEM,
        scratch_shapes=list(scratch_shapes),
        compiler_params=pltpu.CompilerParams(vmem_limit_bytes=limit << 20),
        cost_estimate=cost,
        name=name,
    )


def in_vmem(value):
    return pltpu.with_memory_space_constraint(value, pltpu.VMEM)


def in_hbm(value):
    return pltpu.with_memory_space_constraint(value, pltpu.HBM)


def row_block(mine, k):
    return pl.ds(pl.multiple_of(lax.rem(mine + k, ROWS) * OWN, OWN), OWN)


def terms(value, count):
    out = []
    for _ in range(count):
        out.append(value.astype(bf16).astype(f32))
        value = value - out[-1]
    return out


def swap_halves(value):
    half = HEAD_WIDTH // 2
    return jnp.concatenate([value[..., half:], value[..., :half]], axis=-1)


def norm_rope(value, straight, swapped):
    value = value * lax.rsqrt(jnp.mean(value * value, axis=-1, keepdims=True) + EPSILON)
    return value * straight + swap_halves(value) * swapped


def pack(value):
    return jnp.concatenate([value[:8], value[8:]], axis=1)


def unpack(value):
    return jnp.concatenate([value[:, :64], value[:, 64:]], axis=0)


def project_kernel(place_ref, hidden_hbm, gain_hbm, wq_hbm, wkv_hbm, *rest):
    outs, (whole, hidden_ref, gain_ref, wq_ref, wkv_ref, sems) = rest[:ROWS], rest[ROWS:]
    moves = [
        pltpu.make_async_copy(source, target, sems.at[at])
        for at, (source, target) in enumerate(
            (
                (hidden_hbm, hidden_ref),
                (wkv_hbm, wkv_ref),
                (wq_hbm, wq_ref),
                (gain_hbm, gain_ref),
            )
        )
    ]
    for move in moves:
        move.start()
    moves[0].wait()
    hidden = hidden_ref[...].astype(f32)
    square = jnp.sum(hidden * hidden, axis=1, keepdims=True)
    moves[3].wait()
    scaled = (hidden * gain_ref[...].astype(f32)[None]).astype(bf16)
    moves[1].wait()
    keyval = lax.dot_general(scaled, wkv_ref[...], NT, preferred_element_type=f32)
    whole[:, 256:] = jnp.concatenate([keyval, jnp.broadcast_to(square, keyval.shape)], axis=1)
    moves[2].wait()
    whole[:, :256] = jnp.dot(scaled, wq_ref[...], preferred_element_type=f32)
    mine = place_ref[0] // WIDE
    for k in range(ROWS):
        outs[k][...] = whole[row_block(mine, k), :]


def table_kernel(
    length_ref, query_hbm, key_hbm, straight_ref, swapped_ref, query_ref, key_ref, sems
):
    gains = (query_ref, key_ref)
    moves = [
        pltpu.make_async_copy(source, gains[at], sems.at[at])
        for at, source in enumerate((query_hbm, key_hbm))
    ]
    for move in moves:
        move.start()
    row = lax.broadcasted_iota(jnp.int32, (OWN, 128), 0)
    lane = lax.broadcasted_iota(jnp.int32, (OWN, 128), 1)
    position = jnp.zeros((OWN, 128), jnp.int32)
    for b in range(OWN):
        position = jnp.where(row == b, length_ref[b], position)
    half = HEAD_WIDTH // 2
    pair = lax.rem(lax.broadcasted_iota(jnp.int32, (1, 128), 1), half)
    frequency = jnp.zeros((1, 128), f32)
    for at in range(half):
        frequency = jnp.where(pair == at, np.float32(ROPE_BASE ** (-2.0 * at / HEAD_WIDTH)), frequency)
    angle = position.astype(f32) * frequency
    cosine, sine = jnp.cos(angle), jnp.sin(angle)
    sine = jnp.where(lane < half, -sine, sine)
    for at in range(2):
        moves[at].wait()
        gain = gains[at][...].astype(f32)[None]
        straight_ref[at] = cosine * gain
        swapped_ref[at] = sine * swap_halves(gain)


def heads_kernel(a_ref, b_ref, c_ref, d_ref, straight_ref, swapped_ref, out_ref):
    total = (a_ref[...] + b_ref[...]) + (c_ref[...] + d_ref[...])
    inverse = lax.rsqrt(total[:, 320:321] / MODEL_WIDTH + EPSILON)
    scaled = total * inverse
    straight, swapped = straight_ref[0], swapped_ref[0]
    parts = [
        norm_rope(scaled[:, j * 128 : (j + 1) * 128], straight, swapped) for j in range(2)
    ]
    parts.append(pack(scaled[:, 256:320]))
    out = jnp.concatenate(parts, axis=0).astype(bf16)
    out_ref[...] = jnp.broadcast_to(out[None], out_ref.shape)


def attend_kernel(
    length_ref, block_ref, g_ref, k_ref, v_ref, o_ref, q_scr, p_scr, w_scr, n_scr, s_scr
):
    for head in range(QUERY_HEADS):
        w, j = divmod(head, 2)
        q_scr[pl.ds(head, OWN, stride=QUERY_HEADS), :] = g_ref[
            w, j * OWN : (j + 1) * OWN, :
        ].astype(f32)

    row = lax.broadcasted_iota(jnp.int32, (16, 256), 0)
    lane = lax.broadcasted_iota(jnp.int32, (16, 256), 1)
    own_half = (row < 8) == (lane < 128)
    slot = lax.broadcasted_iota(jnp.int32, (QUERY_HEADS, 256), 1)
    place = lax.rem(lax.broadcasted_iota(jnp.int32, (QUERY_HEADS, 128), 1), 8)

    def score(group):
        for u in range(AT_ONCE):
            b = group * AT_ONCE + u
            for p in range(4):
                here = pl.ds(pl.multiple_of(b * QUERY_HEADS + 16 * p, 16), 16)
                pair = q_scr[here, :]
                query = jnp.where(own_half, jnp.concatenate([pair, pair], axis=1), 0.0)
                p_scr[here, :] = lax.dot_general(
                    query.astype(bf16),
                    k_ref[b, :, 256 * p : 256 * p + 256],
                    NT,
                    preferred_element_type=f32,
                )

    def weigh(group):
        for u in range(AT_ONCE):
            b = group * AT_ONCE + u
            here = pl.ds(pl.multiple_of(b * QUERY_HEADS, QUERY_HEADS), QUERY_HEADS)
            visible = slot < length_ref[b] - block_ref[b] * BLOCK
            scores = jnp.where(visible, p_scr[here, :] * SCALE, MASKED)
            shift = jnp.max(scores, axis=1, keepdims=True).astype(bf16).astype(f32)
            weights = jnp.where(visible, jnp.exp(scores - shift), 0.0)
            total = jnp.sum(weights, axis=1, keepdims=True)
            w_scr[here, :] = weights.astype(bf16)
            stats = jnp.where(place == 0, shift, 0.0)
            for at, term in enumerate(terms(total, 2)):
                stats = jnp.where(place == at + 1, term, stats)
            s_scr[pl.ds(b, QUERY_HEADS, stride=OWN), :] = stats

    def add_up(group):
        for u in range(AT_ONCE):
            b = group * AT_ONCE + u
            for p in range(4):
                here = pl.ds(pl.multiple_of(b * QUERY_HEADS + 16 * p, 16), 16)
                both = jnp.dot(
                    w_scr[here, :],
                    v_ref[b, :, 256 * p : 256 * p + 256],
                    preferred_element_type=f32,
                )
                n_scr[pl.ds(16 * p * OWN + b, 16, stride=OWN), :] = jnp.concatenate(
                    [both[:8, :128], both[8:, 128:]], axis=0
                )

    last = GROUPS - 1
    score(0)
    weigh(0)
    score(1)

    @pl.loop(1, last)
    def _(group):
        add_up(group - 1)
        weigh(group)
        score(group + 1)

    add_up(last - 1)
    weigh(last)
    add_up(last)

    lane = lax.broadcasted_iota(jnp.int32, (OWN, 128), 1)
    first = lax.rem(lane, 64) < 8
    for w in range(WIDE):
        rows = [slice((2 * w + j) * OWN, (2 * w + j + 1) * OWN) for j in range(2)]
        o_ref[w, : 2 * OWN, :] = n_scr[2 * w * OWN : 2 * (w + 1) * OWN, :].astype(bf16)
        stats = jnp.where(first, s_scr[rows[0], :], s_scr[rows[1], :])
        o_ref[w, 2 * OWN :, :] = jnp.where(lane[:8] < 64, stats[:8], stats[8:]).astype(bf16)


def combine_kernel(place_ref, r_ref, g_ref, straight_ref, swapped_ref, out_ref, again_ref):
    wide = lax.rem(place_ref[0], WIDE)
    group = wide // 4

    def half(source):
        return unpack(g_ref[source, 2 * OWN :, :].astype(f32))

    def column(value, at):
        return jnp.concatenate(
            [value[..., at : at + 1], value[..., 64 + at : 65 + at]], axis=-2
        )

    key = jnp.concatenate([half(2 * group), half(2 * group + 1)], axis=1)
    value = jnp.concatenate([half(16 + 2 * group), half(17 + 2 * group)], axis=1)
    key = norm_rope(key, straight_ref[1], swapped_ref[1]).astype(bf16).astype(f32)
    fresh = [
        jnp.sum(g_ref[wide, j * OWN : (j + 1) * OWN, :].astype(f32) * key, axis=1, keepdims=True)
        * SCALE
        for j in range(2)
    ]
    lane = lax.broadcasted_iota(jnp.int32, (8, 128), 1)
    stats = r_ref[:, 2 * OWN :, :].astype(f32)
    highest = jnp.max(stats, axis=0)
    for j in range(2):
        packed = jnp.where(lane < 64, fresh[j][:8], fresh[j][8:])
        highest = jnp.where(lax.rem(lane, 64) == 8 * j, jnp.maximum(highest, packed), highest)
    shift_lane = (lax.rem(lane, 64) == 0) | (lax.rem(lane, 64) == 8)
    factors = jnp.where(shift_lane[None], jnp.exp(jnp.where(shift_lane, stats - highest, 0.0)), 0.0)
    spread_factors = factors
    for shift in (1, 2):
        spread_factors = spread_factors + jnp.roll(factors, shift, axis=2)
    totals = jnp.sum(spread_factors * jnp.where(shift_lane, 0.0, stats), axis=0)
    for j in range(2):
        lanes = slice(j * 128, (j + 1) * 128)
        here = slice(j * OWN, (j + 1) * OWN)
        fresh_weight = jnp.exp(fresh[j] - column(highest, 8 * j))
        weight_sum = column(totals, 8 * j + 1) + column(totals, 8 * j + 2) + fresh_weight
        numer = jnp.sum(r_ref[:, here, :].astype(f32) * column(factors, 8 * j), axis=0)
        numer = numer + fresh_weight.astype(bf16).astype(f32) * value
        heads = (numer / weight_sum).astype(bf16)
        out_ref[:, lanes] = heads
        again_ref[:, lanes] = heads


def store_pairs(out_ref, value):
    for block in range(WIDE):
        out_ref[block] = value[2 * block : 2 * block + 2]


def output_kernel(a_ref, b_ref, c_ref, d_ref, w_ref, out_ref):
    heads = jnp.concatenate([a_ref[...], b_ref[...], c_ref[...], d_ref[...]], axis=0)
    store_pairs(out_ref, jnp.dot(heads, w_ref[...], preferred_element_type=f32).astype(bf16))


def sum_spread_kernel(got_ref, out_ref):
    total = jnp.sum(got_ref[...].astype(f32), axis=0).astype(bf16)
    out_ref[...] = jnp.broadcast_to(total[None], out_ref.shape)


def gate_up_kernel(
    place_ref, hidden_ref, attended_ref, gain_ref, wg_ref, wu_ref, stream_ref, *outs
):
    mine = place_ref[0] // WIDE
    for k in range(ROWS):
        at = slice(k * OWN, (k + 1) * OWN)
        blocks = attended_ref[k * WIDE // ROWS : (k + 1) * WIDE // ROWS]
        attended = blocks.astype(f32).reshape(OWN, blocks.shape[-1])
        stream_ref[at, :] = hidden_ref[row_block(mine, k), :].astype(f32) + attended
    stream = stream_ref[...]
    square = jnp.sum(stream * stream, axis=1, keepdims=True)
    scaled = (stream * gain_ref[...].astype(f32)[None]).astype(bf16)
    gate = lax.dot_general(scaled, wg_ref[...], NT, preferred_element_type=f32).astype(bf16)
    up = lax.dot_general(scaled, wu_ref[...], NT, preferred_element_type=f32).astype(bf16)
    pad = HALF - HIDDEN_UNITS
    place = lax.broadcasted_iota(jnp.int32, (stream.shape[0], pad), 1)
    norm = jnp.zeros(place.shape, f32)
    for at, term in enumerate(terms(square, 3)):
        norm = jnp.where(place == at, term, norm)
    norm = norm.astype(bf16)
    for k in range(ROWS):
        at = slice(k * OWN, (k + 1) * OWN)
        outs[k][...] = jnp.concatenate([gate[at], norm[at], up[at], norm[at]], axis=1)


def activate_kernel(a_ref, b_ref, c_ref, d_ref, out_ref):
    total = (a_ref[...].astype(f32) + b_ref[...].astype(f32)) + (
        c_ref[...].astype(f32) + d_ref[...].astype(f32)
    )
    square = (
        total[:, HIDDEN_UNITS : HIDDEN_UNITS + 1]
        + total[:, HIDDEN_UNITS + 1 : HIDDEN_UNITS + 2]
        + total[:, HIDDEN_UNITS + 2 : HIDDEN_UNITS + 3]
    )
    inverse = lax.rsqrt(square / MODEL_WIDTH + EPSILON)
    gate = total[:, :HALF] * inverse
    up = total[:, HALF:] * inverse
    out_ref[...] = (gate / (1.0 + jnp.exp(-gate)) * up).astype(bf16)


def down_kernel(a_ref, b_ref, c_ref, d_ref, w_ref, out_ref):
    units = jnp.concatenate([a_ref[...], b_ref[...], c_ref[...], d_ref[...]], axis=0)
    part = jnp.dot(units[:, :HIDDEN_UNITS], w_ref[...], preferred_element_type=f32)
    store_pairs(out_ref, part.astype(bf16))


def final_kernel(place_ref, stream_ref, down_ref, out_ref):
    mine = place_ref[0] // WIDE
    for k in range(ROWS):
        at = slice(k * OWN, (k + 1) * OWN)
        blocks = down_ref[k * WIDE // ROWS : (k + 1) * WIDE // ROWS]
        down = blocks.astype(f32).reshape(OWN, blocks.shape[-1])
        out_ref[row_block(mine, k), :] = (stream_ref[at, :] + down).astype(bf16)


def to_rows(blocks):
    got = list(blocks)
    for k in (2, 1, 3):
        got[k] = lax.ppermute(blocks[k], "rows", [(i, (i + k) % ROWS) for i in range(ROWS)])
    return got


def from_rows(own):
    got = [own] * ROWS
    for k in (2, 1, 3):
        got[k] = lax.ppermute(own, "rows", [((i + k) % ROWS, i) for i in range(ROWS)])
    return got


def exchange(blocks):
    return lax.all_to_all(blocks, "wide", split_axis=0, concat_axis=0, tiled=True)


def sum_wide(part):
    total = call(
        sum_spread_kernel,
        jax.ShapeDtypeStruct(part.shape, bf16),
        [VMEM],
        limit=4,
        name="sum_spread",
    )(exchange(part))
    return exchange(total)


def body(
    hidden,
    attn_gain,
    w_query,
    w_keyval,
    query_gain,
    key_norm_gain,
    keys_cache,
    values_cache,
    lengths,
    block_index,
    w_out,
    mlp_gain,
    w_gate,
    w_up,
    w_down,
):
    place = lax.axis_index(("rows", "wide")).astype(jnp.int32).reshape(1)
    sds = jax.ShapeDtypeStruct

    blocks = call(
        project_kernel,
        [sds((OWN, 384), f32)] * ROWS,
        [SMEM] + [HBM] * 4,
        [
            pltpu.VMEM((64, 384), f32),
            pltpu.VMEM(hidden.shape, bf16),
            pltpu.VMEM(attn_gain.shape, bf16),
            pltpu.VMEM(w_query.shape, bf16),
            pltpu.VMEM(w_keyval.shape[::-1], bf16),
            pltpu.SemaphoreType.DMA((4,)),
        ],
        limit=8,
        name="project",
    )(place, *map(in_hbm, (hidden, attn_gain, w_query, w_keyval.T)))
    straight, swapped = call(
        table_kernel,
        [sds((2, OWN, 128), f32)] * 2,
        [SMEM, HBM, HBM],
        [pltpu.VMEM((HEAD_WIDTH,), bf16)] * 2 + [pltpu.SemaphoreType.DMA((2,))],
        limit=4,
        name="tables",
    )(*map(in_hbm, (lengths, query_gain, key_norm_gain)))
    payload = call(
        heads_kernel,
        sds((WIDE, PACKED, 128), bf16),
        [VMEM] * 6,
        limit=8,
        name="heads",
        cost=pl.CostEstimate(flops=20_000_000_000, bytes_accessed=1 << 20, transcendentals=0),
    )(*to_rows(blocks), straight, swapped)
    gathered = exchange(payload)

    parts = call(
        attend_kernel,
        sds((WIDE, PACKED, 128), bf16),
        [SMEM, SMEM, VMEM, VMEM, VMEM],
        [
            pltpu.VMEM((OWN * QUERY_HEADS, 128), f32),
            pltpu.VMEM((OWN * QUERY_HEADS, 256), f32),
            pltpu.VMEM((OWN * QUERY_HEADS, 256), bf16),
            pltpu.VMEM((OWN * QUERY_HEADS, 128), f32),
            pltpu.VMEM((OWN * QUERY_HEADS, 128), f32),
        ],
        limit=8,
        name="attend",
    )(lengths, block_index.reshape(OWN), gathered, in_vmem(keys_cache), in_vmem(values_cache))
    heads_out, heads_own = call(
        combine_kernel, [sds((OWN, 256), bf16)] * 2, [SMEM] + [VMEM] * 4, limit=8, name="combine"
    )(place, exchange(parts), gathered, straight, swapped)

    out_part = call(output_kernel, sds((WIDE, 2, 1280), bf16), [VMEM] * 5, limit=8, name="output")(
        *from_rows(heads_own), w_out
    )
    attended = sum_wide(out_part)

    stream, *blocks = call(
        gate_up_kernel,
        [sds((64, 1280), f32)] + [sds((OWN, 2 * HALF), bf16)] * ROWS,
        [SMEM] + [VMEM] * 5,
        limit=12,
        name="gate_up",
    )(place, hidden, attended, mlp_gain, w_gate.T, w_up.T)
    activated = call(
        activate_kernel, sds((OWN, HALF), bf16), [VMEM] * 4, limit=8, name="activate"
    )(*to_rows(blocks))
    down_part = call(down_kernel, sds((WIDE, 2, 1280), bf16), [VMEM] * 5, limit=8, name="down")(
        *from_rows(activated), w_down
    )
    layer_out = call(final_kernel, sds((64, 1280), bf16), [SMEM] + [VMEM] * 2, limit=8, name="final")(
        place, stream, sum_wide(down_part)
    )
    return (layer_out, heads_out)


def solution(mesh):
    in_specs = (
        P(None, "rows"),
        P("rows"),
        P("rows", "wide"),
        P("rows", "wide"),
        P(),
        P(),
        P("rows", "wide", None),
        P("rows", "wide", None),
        P("rows"),
        P("rows", "wide"),
        P("wide", "rows"),
        P("rows"),
        P("rows", "wide"),
        P("rows", "wide"),
        P("wide", "rows"),
    )
    out_specs = (P(None, "rows"), P("rows", "wide"))
    return jax.shard_map(body, mesh=mesh, in_specs=in_specs, out_specs=out_specs, check_vma=False)
```

```python
import jax
import jax.numpy as jnp
import numpy as np
from jax import lax
from jax.experimental import pallas as pl
from jax.experimental.pallas import tpu as pltpu
from jax.sharding import PartitionSpec as P

MODEL_WIDTH = 5120
QUERY_HEADS = 64
KEY_VALUE_HEADS = 8
HEAD_WIDTH = 128
EPSILON = 1e-06
ROPE_BASE = 1000000.0
MASKED = -1e30
SCALE = HEAD_WIDTH ** (-0.5)

ROWS = 4
WIDE = 32
PACKED = 40
AT_ONCE = 2
GROUPS = 8
OWN = 16
BLOCK = 256
HIDDEN_UNITS = 800
HALF = 896

f32 = jnp.float32
bf16 = jnp.bfloat16
VMEM = pl.BlockSpec(memory_space=pltpu.VMEM)
HBM = pl.BlockSpec(memory_space=pltpu.HBM)
SMEM = pl.BlockSpec(memory_space=pltpu.SMEM)
NT = (((1,), (1,)), ((), ()))


def call(
    kernel, out_shape, in_specs, scratch_shapes=(), limit=24, name=None, cost=None
):
    many = isinstance(out_shape, (tuple, list))
    return pl.pallas_call(
        kernel,
        out_shape=out_shape,
        in_specs=in_specs,
        out_specs=[VMEM] * len(out_shape) if many else VMEM,
        scratch_shapes=list(scratch_shapes),
        compiler_params=pltpu.CompilerParams(vmem_limit_bytes=limit << 20),
        cost_estimate=cost,
        name=name,
    )


def in_vmem(value):
    return pltpu.with_memory_space_constraint(value, pltpu.VMEM)


def in_hbm(value):
    return pltpu.with_memory_space_constraint(value, pltpu.HBM)


def row_block(mine, k):
    return pl.ds(pl.multiple_of(lax.rem(mine + k, ROWS) * OWN, OWN), OWN)


def height(place_ref):
    return lax.rem(place_ref[0], WIDE) // 8


def terms(value, count):
    out = []
    for _ in range(count):
        out.append(value.astype(bf16).astype(f32))
        value = value - out[-1]
    return out


def swap_halves(value):
    half = HEAD_WIDTH // 2
    return jnp.concatenate([value[..., half:], value[..., :half]], axis=-1)


def norm_rope(value, straight, swapped):
    value = value * lax.rsqrt(jnp.mean(value * value, axis=-1, keepdims=True) + EPSILON)
    return value * straight + swap_halves(value) * swapped


def pack(value):
    return jnp.concatenate([value[:8], value[8:]], axis=1)


def unpack(value):
    return jnp.concatenate([value[:, :64], value[:, 64:]], axis=0)


def project_kernel(place_ref, hidden_hbm, gain_hbm, wq_hbm, wkv_hbm, *rest):
    outs, (whole, hidden_ref, gain_ref, wq_ref, wkv_ref, sems) = rest[:ROWS], rest[ROWS:]
    moves = [
        pltpu.make_async_copy(source, target, sems.at[at])
        for at, (source, target) in enumerate(
            (
                (hidden_hbm, hidden_ref),
                (wkv_hbm, wkv_ref),
                (wq_hbm, wq_ref),
                (gain_hbm, gain_ref),
            )
        )
    ]
    for move in moves:
        move.start()
    moves[0].wait()
    hidden = hidden_ref[...].astype(f32)
    square = jnp.sum(hidden * hidden, axis=1, keepdims=True)
    moves[3].wait()
    scaled = (hidden * gain_ref[...].astype(f32)[None]).astype(bf16)
    moves[1].wait()
    keyval = lax.dot_general(scaled, wkv_ref[...], NT, preferred_element_type=f32)
    whole[:, 256:] = jnp.concatenate([keyval, jnp.broadcast_to(square, keyval.shape)], axis=1)
    moves[2].wait()
    whole[:, :256] = jnp.dot(scaled, wq_ref[...], preferred_element_type=f32)
    split_rows(outs, whole, place_ref[0] // WIDE)


def table_kernel(
    length_ref, query_hbm, key_hbm, straight_ref, swapped_ref, query_ref, key_ref, sems
):
    gains = (query_ref, key_ref)
    moves = [
        pltpu.make_async_copy(source, gains[at], sems.at[at])
        for at, source in enumerate((query_hbm, key_hbm))
    ]
    for move in moves:
        move.start()
    row = lax.broadcasted_iota(jnp.int32, (OWN, 128), 0)
    lane = lax.broadcasted_iota(jnp.int32, (OWN, 128), 1)
    position = jnp.zeros((OWN, 128), jnp.int32)
    for b in range(OWN):
        position = jnp.where(row == b, length_ref[b], position)
    half = HEAD_WIDTH // 2
    pair = lax.rem(lax.broadcasted_iota(jnp.int32, (1, 128), 1), half)
    frequency = jnp.zeros((1, 128), f32)
    for at in range(half):
        frequency = jnp.where(pair == at, np.float32(ROPE_BASE ** (-2.0 * at / HEAD_WIDTH)), frequency)
    angle = position.astype(f32) * frequency
    cosine, sine = jnp.cos(angle), jnp.sin(angle)
    sine = jnp.where(lane < half, -sine, sine)
    for at in range(2):
        moves[at].wait()
        gain = gains[at][...].astype(f32)[None]
        straight_ref[at] = cosine * gain
        swapped_ref[at] = sine * swap_halves(gain)


def heads_kernel(a_ref, b_ref, c_ref, d_ref, straight_ref, swapped_ref, out_ref):
    total = (a_ref[...] + b_ref[...]) + (c_ref[...] + d_ref[...])
    inverse = lax.rsqrt(total[:, 320:321] / MODEL_WIDTH + EPSILON)
    scaled = total * inverse
    straight, swapped = straight_ref[0], swapped_ref[0]
    parts = [
        norm_rope(scaled[:, j * 128 : (j + 1) * 128], straight, swapped) for j in range(2)
    ]
    parts.append(pack(scaled[:, 256:320]))
    out = jnp.concatenate(parts, axis=0).astype(bf16)
    out_ref[...] = jnp.broadcast_to(out[None], out_ref.shape)


def attend_kernel(
    length_ref, block_ref, g_ref, k_ref, v_ref, o_ref, q_scr, p_scr, w_scr, n_scr, s_scr
):
    for head in range(QUERY_HEADS):
        w, j = divmod(head, 2)
        q_scr[pl.ds(head, OWN, stride=QUERY_HEADS), :] = g_ref[
            w, j * OWN : (j + 1) * OWN, :
        ].astype(f32)

    row = lax.broadcasted_iota(jnp.int32, (16, 256), 0)
    lane = lax.broadcasted_iota(jnp.int32, (16, 256), 1)
    own_half = (row < 8) == (lane < 128)
    slot = lax.broadcasted_iota(jnp.int32, (QUERY_HEADS, 256), 1)
    place = lax.rem(lax.broadcasted_iota(jnp.int32, (QUERY_HEADS, 128), 1), 8)

    def score(group):
        for u in range(AT_ONCE):
            b = group * AT_ONCE + u
            for p in range(4):
                here = pl.ds(pl.multiple_of(b * QUERY_HEADS + 16 * p, 16), 16)
                pair = q_scr[here, :]
                query = jnp.where(own_half, jnp.concatenate([pair, pair], axis=1), 0.0)
                p_scr[here, :] = lax.dot_general(
                    query.astype(bf16),
                    k_ref[b, :, 256 * p : 256 * p + 256],
                    NT,
                    preferred_element_type=f32,
                )

    def weigh(group):
        for u in range(AT_ONCE):
            b = group * AT_ONCE + u
            here = pl.ds(pl.multiple_of(b * QUERY_HEADS, QUERY_HEADS), QUERY_HEADS)
            visible = slot < length_ref[b] - block_ref[b] * BLOCK
            scores = jnp.where(visible, p_scr[here, :] * SCALE, MASKED)
            shift = jnp.max(scores, axis=1, keepdims=True).astype(bf16).astype(f32)
            weights = jnp.where(visible, jnp.exp(scores - shift), 0.0)
            total = jnp.sum(weights, axis=1, keepdims=True)
            w_scr[here, :] = weights.astype(bf16)
            stats = jnp.where(place == 0, shift, 0.0)
            for at, term in enumerate(terms(total, 2)):
                stats = jnp.where(place == at + 1, term, stats)
            s_scr[pl.ds(b, QUERY_HEADS, stride=OWN), :] = stats

    def add_up(group):
        for u in range(AT_ONCE):
            b = group * AT_ONCE + u
            for p in range(4):
                here = pl.ds(pl.multiple_of(b * QUERY_HEADS + 16 * p, 16), 16)
                both = jnp.dot(
                    w_scr[here, :],
                    v_ref[b, :, 256 * p : 256 * p + 256],
                    preferred_element_type=f32,
                )
                n_scr[pl.ds(16 * p * OWN + b, 16, stride=OWN), :] = jnp.concatenate(
                    [both[:8, :128], both[8:, 128:]], axis=0
                )

    last = GROUPS - 1
    score(0)
    weigh(0)
    score(1)

    @pl.loop(1, last)
    def _(group):
        add_up(group - 1)
        weigh(group)
        score(group + 1)

    add_up(last - 1)
    weigh(last)
    add_up(last)

    lane = lax.broadcasted_iota(jnp.int32, (OWN, 128), 1)
    first = lax.rem(lane, 64) < 8
    for w in range(WIDE):
        rows = [slice((2 * w + j) * OWN, (2 * w + j + 1) * OWN) for j in range(2)]
        o_ref[w, : 2 * OWN, :] = n_scr[2 * w * OWN : 2 * (w + 1) * OWN, :].astype(bf16)
        stats = jnp.where(first, s_scr[rows[0], :], s_scr[rows[1], :])
        o_ref[w, 2 * OWN :, :] = jnp.where(lane[:8] < 64, stats[:8], stats[8:]).astype(bf16)


def combine_kernel(place_ref, r_ref, g_ref, straight_ref, swapped_ref, out_ref, again_ref):
    wide = lax.rem(place_ref[0], WIDE)
    group = wide // 4

    def half(source):
        return unpack(g_ref[source, 2 * OWN :, :].astype(f32))

    def column(value, at):
        return jnp.concatenate(
            [value[..., at : at + 1], value[..., 64 + at : 65 + at]], axis=-2
        )

    key = jnp.concatenate([half(2 * group), half(2 * group + 1)], axis=1)
    value = jnp.concatenate([half(16 + 2 * group), half(17 + 2 * group)], axis=1)
    key = norm_rope(key, straight_ref[1], swapped_ref[1]).astype(bf16).astype(f32)
    fresh = [
        jnp.sum(g_ref[wide, j * OWN : (j + 1) * OWN, :].astype(f32) * key, axis=1, keepdims=True)
        * SCALE
        for j in range(2)
    ]
    lane = lax.broadcasted_iota(jnp.int32, (8, 128), 1)
    stats = r_ref[:, 2 * OWN :, :].astype(f32)
    highest = jnp.max(stats, axis=0)
    for j in range(2):
        packed = jnp.where(lane < 64, fresh[j][:8], fresh[j][8:])
        highest = jnp.where(lax.rem(lane, 64) == 8 * j, jnp.maximum(highest, packed), highest)
    shift_lane = (lax.rem(lane, 64) == 0) | (lax.rem(lane, 64) == 8)
    factors = jnp.where(shift_lane[None], jnp.exp(jnp.where(shift_lane, stats - highest, 0.0)), 0.0)
    spread_factors = factors
    for shift in (1, 2):
        spread_factors = spread_factors + jnp.roll(factors, shift, axis=2)
    totals = jnp.sum(spread_factors * jnp.where(shift_lane, 0.0, stats), axis=0)
    for j in range(2):
        lanes = slice(j * 128, (j + 1) * 128)
        here = slice(j * OWN, (j + 1) * OWN)
        fresh_weight = jnp.exp(fresh[j] - column(highest, 8 * j))
        weight_sum = column(totals, 8 * j + 1) + column(totals, 8 * j + 2) + fresh_weight
        numer = jnp.sum(r_ref[:, here, :].astype(f32) * column(factors, 8 * j), axis=0)
        numer = numer + fresh_weight.astype(bf16).astype(f32) * value
        heads = (numer / weight_sum).astype(bf16)
        out_ref[:, lanes] = heads
        again_ref[:, lanes] = heads


def split_rows(outs, whole, first):
    for k in range(ROWS):
        outs[k][...] = whole[row_block(first, k), :]


def output_kernel(place_ref, a_ref, b_ref, c_ref, d_ref, w_ref, *rest):
    outs, whole = rest[:ROWS], rest[ROWS]
    heads = jnp.concatenate([a_ref[...], b_ref[...], c_ref[...], d_ref[...]], axis=0)
    whole[...] = jnp.dot(heads, w_ref[...], preferred_element_type=f32).astype(bf16)
    split_rows(outs, whole, height(place_ref))


def add_kernel(*refs):
    out_ref = refs[-1]
    parts = [ref[...].astype(f32) for ref in refs[:-1]]
    if len(parts) == ROWS:
        parts = [parts[0] + parts[2], parts[1] + parts[3]]
    out_ref[...] = (parts[0] + parts[1]).astype(bf16)


def gate_up_kernel(place_ref, hidden_ref, a_ref, b_ref, c_ref, d_ref, gain_ref, wg_ref, wu_ref, stream_ref, *outs):
    mine, first = place_ref[0] // WIDE, height(place_ref)
    for k, ref in enumerate((a_ref, b_ref, c_ref, d_ref)):
        hidden = hidden_ref[row_block(mine + first, k), :].astype(f32)
        stream_ref[row_block(first, k), :] = hidden + ref[...].astype(f32)
    stream = stream_ref[...]
    square = jnp.sum(stream * stream, axis=1, keepdims=True)
    scaled = (stream * gain_ref[...].astype(f32)[None]).astype(bf16)
    gate = lax.dot_general(scaled, wg_ref[...], NT, preferred_element_type=f32).astype(bf16)
    up = lax.dot_general(scaled, wu_ref[...], NT, preferred_element_type=f32).astype(bf16)
    pad = HALF - HIDDEN_UNITS
    place = lax.broadcasted_iota(jnp.int32, (stream.shape[0], pad), 1)
    norm = jnp.zeros(place.shape, f32)
    for at, term in enumerate(terms(square, 3)):
        norm = jnp.where(place == at, term, norm)
    norm = norm.astype(bf16)
    for k in range(ROWS):
        at = slice(k * OWN, (k + 1) * OWN)
        outs[k][...] = jnp.concatenate([gate[at], norm[at], up[at], norm[at]], axis=1)


def activate_kernel(a_ref, b_ref, c_ref, d_ref, out_ref):
    total = (a_ref[...].astype(f32) + b_ref[...].astype(f32)) + (
        c_ref[...].astype(f32) + d_ref[...].astype(f32)
    )
    square = (
        total[:, HIDDEN_UNITS : HIDDEN_UNITS + 1]
        + total[:, HIDDEN_UNITS + 1 : HIDDEN_UNITS + 2]
        + total[:, HIDDEN_UNITS + 2 : HIDDEN_UNITS + 3]
    )
    inverse = lax.rsqrt(square / MODEL_WIDTH + EPSILON)
    gate = total[:, :HALF] * inverse
    up = total[:, HALF:] * inverse
    out_ref[...] = (gate / (1.0 + jnp.exp(-gate)) * up).astype(bf16)


def down_kernel(place_ref, a_ref, b_ref, c_ref, d_ref, w_ref, *rest):
    outs, whole = rest[:ROWS], rest[ROWS]
    units = jnp.concatenate([a_ref[...], b_ref[...], c_ref[...], d_ref[...]], axis=0)
    part = jnp.dot(units[:, :HIDDEN_UNITS], w_ref[...], preferred_element_type=f32)
    whole[...] = part.astype(bf16)
    split_rows(outs, whole, height(place_ref))


def final_kernel(place_ref, stream_ref, a_ref, b_ref, c_ref, d_ref, out_ref):
    mine, first = place_ref[0] // WIDE, height(place_ref)
    for k, ref in enumerate((a_ref, b_ref, c_ref, d_ref)):
        stream = stream_ref[row_block(first, k), :]
        out_ref[row_block(mine + first, k), :] = (stream + ref[...].astype(f32)).astype(bf16)


def ahead(axis, k):
    if axis == "x":
        return "rows", [(i, (i + k) % ROWS) for i in range(ROWS)]
    if axis == "y":
        return "wide", [(i, (i + 8 * k) % WIDE) for i in range(WIDE)]
    if axis == "z":
        return "wide", [(i, i // 8 * 8 + (i + 2 * k) % 8) for i in range(WIDE)]
    return "wide", [(i, i ^ 1) for i in range(WIDE)]


def to_peers(blocks, axis):
    got = list(blocks)
    for k in (2, 1, 3):
        got[k] = lax.ppermute(blocks[k], *ahead(axis, k))
    return got


def from_peers(own, axis):
    got = [own] * ROWS
    for k in (2, 1, 3):
        got[k] = lax.ppermute(own, *ahead(axis, ROWS - k))
    return got


def exchange(blocks):
    return lax.all_to_all(blocks, "wide", split_axis=0, concat_axis=0, tiled=True)


def sum_wide(blocks):
    def add(parts):
        return call(
            add_kernel,
            jax.ShapeDtypeStruct(parts[0].shape, bf16),
            [VMEM] * len(parts),
            limit=4,
            name="add",
        )(*parts)

    own = add(to_peers(blocks, "y"))
    own = add(from_peers(own, "z"))
    own = add([own, lax.ppermute(own, *ahead("core", 1))])
    return from_peers(own, "y")


def body(
    hidden,
    attn_gain,
    w_query,
    w_keyval,
    query_gain,
    key_norm_gain,
    keys_cache,
    values_cache,
    lengths,
    block_index,
    w_out,
    mlp_gain,
    w_gate,
    w_up,
    w_down,
):
    place = lax.axis_index(("rows", "wide")).astype(jnp.int32).reshape(1)
    sds = jax.ShapeDtypeStruct

    blocks = call(
        project_kernel,
        [sds((OWN, 384), f32)] * ROWS,
        [SMEM] + [HBM] * 4,
        [
            pltpu.VMEM((64, 384), f32),
            pltpu.VMEM(hidden.shape, bf16),
            pltpu.VMEM(attn_gain.shape, bf16),
            pltpu.VMEM(w_query.shape, bf16),
            pltpu.VMEM(w_keyval.shape[::-1], bf16),
            pltpu.SemaphoreType.DMA((4,)),
        ],
        limit=8,
        name="project",
    )(place, *map(in_hbm, (hidden, attn_gain, w_query, w_keyval.T)))
    straight, swapped = call(
        table_kernel,
        [sds((2, OWN, 128), f32)] * 2,
        [SMEM, HBM, HBM],
        [pltpu.VMEM((HEAD_WIDTH,), bf16)] * 2 + [pltpu.SemaphoreType.DMA((2,))],
        limit=4,
        name="tables",
    )(*map(in_hbm, (lengths, query_gain, key_norm_gain)))
    payload = call(
        heads_kernel,
        sds((WIDE, PACKED, 128), bf16),
        [VMEM] * 6,
        limit=8,
        name="heads",
        cost=pl.CostEstimate(flops=20_000_000_000, bytes_accessed=1 << 20, transcendentals=0),
    )(*to_peers(blocks, "x"), straight, swapped)
    gathered = exchange(payload)

    parts = call(
        attend_kernel,
        sds((WIDE, PACKED, 128), bf16),
        [SMEM, SMEM, VMEM, VMEM, VMEM],
        [
            pltpu.VMEM((OWN * QUERY_HEADS, 128), f32),
            pltpu.VMEM((OWN * QUERY_HEADS, 256), f32),
            pltpu.VMEM((OWN * QUERY_HEADS, 256), bf16),
            pltpu.VMEM((OWN * QUERY_HEADS, 128), f32),
            pltpu.VMEM((OWN * QUERY_HEADS, 128), f32),
        ],
        limit=8,
        name="attend",
    )(lengths, block_index.reshape(OWN), gathered, in_vmem(keys_cache), in_vmem(values_cache))
    heads_out, heads_own = call(
        combine_kernel, [sds((OWN, 256), bf16)] * 2, [SMEM] + [VMEM] * 4, limit=8, name="combine"
    )(place, exchange(parts), gathered, straight, swapped)

    part = [sds((OWN, 1280), bf16)] * ROWS
    whole = [pltpu.VMEM((64, 1280), bf16)]
    parts = call(output_kernel, part, [SMEM] + [VMEM] * 5, whole, limit=8, name="output")(
        place, *from_peers(heads_own, "x"), w_out
    )
    stream, *blocks = call(
        gate_up_kernel,
        [sds((64, 1280), f32)] + [sds((OWN, 2 * HALF), bf16)] * ROWS,
        [SMEM] + [VMEM] * 8,
        limit=12,
        name="gate_up",
    )(place, hidden, *sum_wide(parts), mlp_gain, w_gate.T, w_up.T)
    activated = call(
        activate_kernel, sds((OWN, HALF), bf16), [VMEM] * 4, limit=8, name="activate"
    )(*to_peers(blocks, "x"))
    parts = call(down_kernel, part, [SMEM] + [VMEM] * 5, whole, limit=8, name="down")(
        place, *from_peers(activated, "x"), w_down
    )
    layer_out = call(
        final_kernel, sds((64, 1280), bf16), [SMEM] + [VMEM] * 5, limit=8, name="final"
    )(place, stream, *sum_wide(parts))
    return (layer_out, heads_out)


def solution(mesh):
    in_specs = (
        P(None, "rows"),
        P("rows"),
        P("rows", "wide"),
        P("rows", "wide"),
        P(),
        P(),
        P("rows", "wide", None),
        P("rows", "wide", None),
        P("rows"),
        P("rows", "wide"),
        P("wide", "rows"),
        P("rows"),
        P("rows", "wide"),
        P("rows", "wide"),
        P("wide", "rows"),
    )
    out_specs = (P(None, "rows"), P("rows", "wide"))
    return jax.shard_map(body, mesh=mesh, in_specs=in_specs, out_specs=out_specs, check_vma=False)
```

```python
import jax
import jax.numpy as jnp
import numpy as np
from jax import lax
from jax.experimental import pallas as pl
from jax.experimental.pallas import tpu as pltpu
from jax.sharding import PartitionSpec as P

MODEL_WIDTH = 5120
QUERY_HEADS = 64
KEY_VALUE_HEADS = 8
HEAD_WIDTH = 128
EPSILON = 1e-06
ROPE_BASE = 1000000.0
MASKED = -1e30
SCALE = HEAD_WIDTH ** (-0.5)

ROWS = 4
WIDE = 32
PACKED = 40
AT_ONCE = 2
GROUPS = 8
OWN = 16
BLOCK = 256
HIDDEN_UNITS = 800
HALF = 896

f32 = jnp.float32
bf16 = jnp.bfloat16
VMEM = pl.BlockSpec(memory_space=pltpu.VMEM)
HBM = pl.BlockSpec(memory_space=pltpu.HBM)
SMEM = pl.BlockSpec(memory_space=pltpu.SMEM)
NT = (((1,), (1,)), ((), ()))


def call(
    kernel, out_shape, in_specs, scratch_shapes=(), limit=24, name=None, cost=None
):
    many = isinstance(out_shape, (tuple, list))
    return pl.pallas_call(
        kernel,
        out_shape=out_shape,
        in_specs=in_specs,
        out_specs=[VMEM] * len(out_shape) if many else VMEM,
        scratch_shapes=list(scratch_shapes),
        compiler_params=pltpu.CompilerParams(vmem_limit_bytes=limit << 20),
        cost_estimate=cost,
        name=name,
    )


def in_vmem(value):
    return pltpu.with_memory_space_constraint(value, pltpu.VMEM)


def in_hbm(value):
    return pltpu.with_memory_space_constraint(value, pltpu.HBM)


def rows_at(block):
    return pl.ds(pl.multiple_of(block * OWN, OWN), OWN)


def split(mine, whole, keep_ref, send_ref):
    for ref, pair in ((keep_ref, (0, 3)), (send_ref, (1, 2))):
        for at, other in enumerate(pair):
            block = whole[rows_at(mine ^ other), :]
            ref[at * OWN : (at + 1) * OWN, :] = block.astype(ref.dtype)


def gathered_blocks(mine, near_ref, far_ref):
    for ref, pair in ((near_ref, (0, 3)), (far_ref, (1, 2))):
        for at, other in enumerate(pair):
            yield mine ^ other, ref[at * OWN : (at + 1) * OWN, :]


def along_x(place_ref):
    return place_ref[0] // WIDE


def along_y(place_ref):
    return lax.rem(place_ref[0], WIDE) // 8


def terms(value, count):
    out = []
    for _ in range(count):
        out.append(value.astype(bf16).astype(f32))
        value = value - out[-1]
    return out


def swap_halves(value):
    half = HEAD_WIDTH // 2
    return jnp.concatenate([value[..., half:], value[..., :half]], axis=-1)


def norm_rope(value, straight, swapped):
    value = value * lax.rsqrt(jnp.mean(value * value, axis=-1, keepdims=True) + EPSILON)
    return value * straight + swap_halves(value) * swapped


def pack(value):
    return jnp.concatenate([value[:8], value[8:]], axis=1)


def unpack(value):
    return jnp.concatenate([value[:, :64], value[:, 64:]], axis=0)


def project_kernel(place_ref, hidden_hbm, gain_hbm, wq_hbm, wkv_hbm, *rest):
    keep_ref, send_ref, whole, hidden_ref, gain_ref, wq_ref, wkv_ref, sems = rest
    moves = [
        pltpu.make_async_copy(source, target, sems.at[at])
        for at, (source, target) in enumerate(
            (
                (hidden_hbm, hidden_ref),
                (wkv_hbm, wkv_ref),
                (wq_hbm, wq_ref),
                (gain_hbm, gain_ref),
            )
        )
    ]
    for move in moves:
        move.start()
    moves[0].wait()
    hidden = hidden_ref[...].astype(f32)
    square = jnp.sum(hidden * hidden, axis=1, keepdims=True)
    moves[3].wait()
    scaled = (hidden * gain_ref[...].astype(f32)[None]).astype(bf16)
    moves[1].wait()
    keyval = lax.dot_general(scaled, wkv_ref[...], NT, preferred_element_type=f32)
    whole[:, 256:] = jnp.concatenate([keyval, jnp.broadcast_to(square, keyval.shape)], axis=1)
    moves[2].wait()
    whole[:, :256] = jnp.dot(scaled, wq_ref[...], preferred_element_type=f32)
    split(along_x(place_ref), whole, keep_ref, send_ref)


def table_kernel(
    length_ref, query_hbm, key_hbm, straight_ref, swapped_ref, query_ref, key_ref, sems
):
    gains = (query_ref, key_ref)
    moves = [
        pltpu.make_async_copy(source, gains[at], sems.at[at])
        for at, source in enumerate((query_hbm, key_hbm))
    ]
    for move in moves:
        move.start()
    row = lax.broadcasted_iota(jnp.int32, (OWN, 128), 0)
    lane = lax.broadcasted_iota(jnp.int32, (OWN, 128), 1)
    position = jnp.zeros((OWN, 128), jnp.int32)
    for b in range(OWN):
        position = jnp.where(row == b, length_ref[b], position)
    half = HEAD_WIDTH // 2
    pair = lax.rem(lax.broadcasted_iota(jnp.int32, (1, 128), 1), half)
    frequency = jnp.zeros((1, 128), f32)
    for at in range(half):
        frequency = jnp.where(pair == at, np.float32(ROPE_BASE ** (-2.0 * at / HEAD_WIDTH)), frequency)
    angle = position.astype(f32) * frequency
    cosine, sine = jnp.cos(angle), jnp.sin(angle)
    sine = jnp.where(lane < half, -sine, sine)
    for at in range(2):
        moves[at].wait()
        gain = gains[at][...].astype(f32)[None]
        straight_ref[at] = cosine * gain
        swapped_ref[at] = sine * swap_halves(gain)


def heads_kernel(a_ref, b_ref, straight_ref, swapped_ref, out_ref):
    total = a_ref[...] + b_ref[...]
    inverse = lax.rsqrt(total[:, 320:321] / MODEL_WIDTH + EPSILON)
    scaled = total * inverse
    straight, swapped = straight_ref[0], swapped_ref[0]
    parts = [
        norm_rope(scaled[:, j * 128 : (j + 1) * 128], straight, swapped) for j in range(2)
    ]
    parts.append(pack(scaled[:, 256:320]))
    out = jnp.concatenate(parts, axis=0).astype(bf16)
    out_ref[...] = jnp.broadcast_to(out[None], out_ref.shape)


def attend_kernel(
    length_ref, block_ref, g_ref, k_ref, v_ref, o_ref, q_scr, p_scr, w_scr, n_scr, s_scr
):
    for head in range(QUERY_HEADS):
        w, j = divmod(head, 2)
        q_scr[pl.ds(head, OWN, stride=QUERY_HEADS), :] = g_ref[
            w, j * OWN : (j + 1) * OWN, :
        ].astype(f32)

    row = lax.broadcasted_iota(jnp.int32, (16, 256), 0)
    lane = lax.broadcasted_iota(jnp.int32, (16, 256), 1)
    own_half = (row < 8) == (lane < 128)
    slot = lax.broadcasted_iota(jnp.int32, (QUERY_HEADS, 256), 1)
    place = lax.rem(lax.broadcasted_iota(jnp.int32, (QUERY_HEADS, 128), 1), 8)

    def score(group):
        for u in range(AT_ONCE):
            b = group * AT_ONCE + u
            for p in range(4):
                here = pl.ds(pl.multiple_of(b * QUERY_HEADS + 16 * p, 16), 16)
                pair = q_scr[here, :]
                query = jnp.where(own_half, jnp.concatenate([pair, pair], axis=1), 0.0)
                p_scr[here, :] = lax.dot_general(
                    query.astype(bf16),
                    k_ref[b, :, 256 * p : 256 * p + 256],
                    NT,
                    preferred_element_type=f32,
                )

    def weigh(group):
        for u in range(AT_ONCE):
            b = group * AT_ONCE + u
            here = pl.ds(pl.multiple_of(b * QUERY_HEADS, QUERY_HEADS), QUERY_HEADS)
            visible = slot < length_ref[b] - block_ref[b] * BLOCK
            scores = jnp.where(visible, p_scr[here, :] * SCALE, MASKED)
            shift = jnp.max(scores, axis=1, keepdims=True).astype(bf16).astype(f32)
            weights = jnp.where(visible, jnp.exp(scores - shift), 0.0)
            total = jnp.sum(weights, axis=1, keepdims=True)
            w_scr[here, :] = weights.astype(bf16)
            stats = jnp.where(place == 0, shift, 0.0)
            for at, term in enumerate(terms(total, 2)):
                stats = jnp.where(place == at + 1, term, stats)
            s_scr[pl.ds(b, QUERY_HEADS, stride=OWN), :] = stats

    def add_up(group):
        for u in range(AT_ONCE):
            b = group * AT_ONCE + u
            for p in range(4):
                here = pl.ds(pl.multiple_of(b * QUERY_HEADS + 16 * p, 16), 16)
                both = jnp.dot(
                    w_scr[here, :],
                    v_ref[b, :, 256 * p : 256 * p + 256],
                    preferred_element_type=f32,
                )
                n_scr[pl.ds(16 * p * OWN + b, 16, stride=OWN), :] = jnp.concatenate(
                    [both[:8, :128], both[8:, 128:]], axis=0
                )

    last = GROUPS - 1
    score(0)
    weigh(0)
    score(1)

    @pl.loop(1, last)
    def _(group):
        add_up(group - 1)
        weigh(group)
        score(group + 1)

    add_up(last - 1)
    weigh(last)
    add_up(last)

    lane = lax.broadcasted_iota(jnp.int32, (OWN, 128), 1)
    first = lax.rem(lane, 64) < 8
    for w in range(WIDE):
        rows = [slice((2 * w + j) * OWN, (2 * w + j + 1) * OWN) for j in range(2)]
        o_ref[w, : 2 * OWN, :] = n_scr[2 * w * OWN : 2 * (w + 1) * OWN, :].astype(bf16)
        stats = jnp.where(first, s_scr[rows[0], :], s_scr[rows[1], :])
        o_ref[w, 2 * OWN :, :] = jnp.where(lane[:8] < 64, stats[:8], stats[8:]).astype(bf16)


def combine_kernel(place_ref, r_ref, g_ref, straight_ref, swapped_ref, out_ref, again_ref):
    wide = lax.rem(place_ref[0], WIDE)
    group = wide // 4

    def half(source):
        return unpack(g_ref[source, 2 * OWN :, :].astype(f32))

    def column(value, at):
        return jnp.concatenate(
            [value[..., at : at + 1], value[..., 64 + at : 65 + at]], axis=-2
        )

    key = jnp.concatenate([half(2 * group), half(2 * group + 1)], axis=1)
    value = jnp.concatenate([half(16 + 2 * group), half(17 + 2 * group)], axis=1)
    key = norm_rope(key, straight_ref[1], swapped_ref[1]).astype(bf16).astype(f32)
    fresh = [
        jnp.sum(g_ref[wide, j * OWN : (j + 1) * OWN, :].astype(f32) * key, axis=1, keepdims=True)
        * SCALE
        for j in range(2)
    ]
    lane = lax.broadcasted_iota(jnp.int32, (8, 128), 1)
    stats = r_ref[:, 2 * OWN :, :].astype(f32)
    highest = jnp.max(stats, axis=0)
    for j in range(2):
        packed = jnp.where(lane < 64, fresh[j][:8], fresh[j][8:])
        highest = jnp.where(lax.rem(lane, 64) == 8 * j, jnp.maximum(highest, packed), highest)
    shift_lane = (lax.rem(lane, 64) == 0) | (lax.rem(lane, 64) == 8)
    factors = jnp.where(shift_lane[None], jnp.exp(jnp.where(shift_lane, stats - highest, 0.0)), 0.0)
    spread_factors = factors
    for shift in (1, 2):
        spread_factors = spread_factors + jnp.roll(factors, shift, axis=2)
    totals = jnp.sum(spread_factors * jnp.where(shift_lane, 0.0, stats), axis=0)
    for j in range(2):
        lanes = slice(j * 128, (j + 1) * 128)
        here = slice(j * OWN, (j + 1) * OWN)
        fresh_weight = jnp.exp(fresh[j] - column(highest, 8 * j))
        weight_sum = column(totals, 8 * j + 1) + column(totals, 8 * j + 2) + fresh_weight
        numer = jnp.sum(r_ref[:, here, :].astype(f32) * column(factors, 8 * j), axis=0)
        numer = numer + fresh_weight.astype(bf16).astype(f32) * value
        heads = (numer / weight_sum).astype(bf16)
        out_ref[:, lanes] = heads
        again_ref[:, lanes] = heads


def product_kernel(place_ref, near_ref, far_ref, w_ref, keep_ref, send_ref, left, whole):
    for block, value in gathered_blocks(along_x(place_ref), near_ref, far_ref):
        left[rows_at(block), :] = value
    depth = w_ref.shape[0]
    whole[...] = jnp.dot(left[:, :depth], w_ref[...], preferred_element_type=f32)
    split(along_y(place_ref), whole, keep_ref, send_ref)


def pass_on_kernel(keep_ref, got_ref, own_ref, next_ref):
    own_ref[...] = keep_ref[:OWN, :] + got_ref[:OWN, :].astype(f32)
    following = keep_ref[OWN:, :] + got_ref[OWN:, :].astype(f32)
    if next_ref.shape[1] == 2 * HALF:
        place = lax.broadcasted_iota(jnp.int32, (OWN, HALF - HIDDEN_UNITS), 1)
        norm = norm_lanes(squared_sum(following), place)
        following = jnp.concatenate([following[:, :HIDDEN_UNITS], norm, following[:, HALF:]], axis=1)
    next_ref[...] = following.astype(next_ref.dtype)


def add_kernel(a_ref, b_ref, out_ref):
    out_ref[...] = (a_ref[...].astype(f32) + b_ref[...].astype(f32)).astype(bf16)


def join_kernel(a_ref, b_ref, out_ref):
    out_ref[:OWN, :] = a_ref[...]
    out_ref[OWN:, :] = b_ref[...]


def norm_lanes(square, place):
    norm = jnp.zeros(place.shape, f32)
    for at, term in enumerate(terms(square, 3)):
        norm = jnp.where(place == at, term, norm)
    return norm


def squared_sum(value):
    first = HIDDEN_UNITS
    return value[:, first : first + 1] + value[:, first + 1 : first + 2] + value[:, first + 2 : first + 3]


def gate_up_kernel(
    place_ref,
    hidden_ref,
    near_ref,
    far_ref,
    gain_ref,
    wg_ref,
    wu_ref,
    stream_ref,
    keep_ref,
    send_ref,
    whole,
):
    for block, value in gathered_blocks(along_y(place_ref), near_ref, far_ref):
        at = rows_at(block)
        stream_ref[at, :] = hidden_ref[at, :].astype(f32) + value.astype(f32)
    stream = stream_ref[...]
    square = jnp.sum(stream * stream, axis=1, keepdims=True)
    scaled = (stream * gain_ref[...].astype(f32)[None]).astype(bf16)
    gate = lax.dot_general(scaled, wg_ref[...], NT, preferred_element_type=f32)
    up = lax.dot_general(scaled, wu_ref[...], NT, preferred_element_type=f32)
    place = lax.broadcasted_iota(jnp.int32, (stream.shape[0], HALF - HIDDEN_UNITS), 1)
    norm = norm_lanes(square, place)
    whole[...] = jnp.concatenate([gate, norm, up, jnp.zeros(norm.shape, f32)], axis=1)
    split(along_x(place_ref), whole, keep_ref, send_ref)


def activate_kernel(a_ref, b_ref, out_ref):
    total = a_ref[...] + b_ref[...].astype(f32)
    inverse = lax.rsqrt(squared_sum(total) / MODEL_WIDTH + EPSILON)
    gate = total[:, :HALF] * inverse
    up = total[:, HALF:] * inverse
    out_ref[...] = (gate / (1.0 + jnp.exp(-gate)) * up).astype(bf16)


def final_kernel(place_ref, stream_ref, near_ref, far_ref, out_ref):
    for block, value in gathered_blocks(along_y(place_ref), near_ref, far_ref):
        at = rows_at(block)
        out_ref[at, :] = (stream_ref[at, :] + value.astype(f32)).astype(bf16)


def swap(value, axis, other):
    if axis == "x":
        return lax.ppermute(value, "rows", [(i, i ^ other) for i in range(ROWS)])
    other *= {"y": 8, "z": 2, "core": 1}[axis]
    return lax.ppermute(value, "wide", [(i, i ^ other) for i in range(WIDE)])


def reduce_blocks(keep, send, axis):
    width = keep.shape[1]
    own, following = call(
        pass_on_kernel,
        [
            jax.ShapeDtypeStruct((OWN, width), f32),
            jax.ShapeDtypeStruct((OWN, width), send.dtype),
        ],
        [VMEM] * 2,
        limit=4,
        name="pass_on",
    )(keep, swap(send, axis, 1))
    return own, swap(following, axis, 3)


def add(a, b):
    shape = jax.ShapeDtypeStruct(a.shape, bf16)
    return call(add_kernel, shape, [VMEM] * 2, limit=4, name="add")(a, b)


def gather(own, axis):
    shape = jax.ShapeDtypeStruct((2 * OWN, own.shape[1]), own.dtype)
    near = call(join_kernel, shape, [VMEM] * 2, limit=4, name="join")(own, swap(own, axis, 3))
    return near, swap(near, axis, 1)


def exchange(blocks):
    return lax.all_to_all(blocks, "wide", split_axis=0, concat_axis=0, tiled=True)


def sum_wide(keep, send):
    own = add(*reduce_blocks(keep, send, "y"))
    own = add(own, swap(own, "z", 1))
    own = add(own, swap(own, "z", 3))
    own = add(own, swap(own, "core", 1))
    return gather(own, "y")


def body(
    hidden,
    attn_gain,
    w_query,
    w_keyval,
    query_gain,
    key_norm_gain,
    keys_cache,
    values_cache,
    lengths,
    block_index,
    w_out,
    mlp_gain,
    w_gate,
    w_up,
    w_down,
):
    place = lax.axis_index(("rows", "wide")).astype(jnp.int32).reshape(1)
    sds = jax.ShapeDtypeStruct

    keep, send = call(
        project_kernel,
        [sds((2 * OWN, 384), f32)] * 2,
        [SMEM] + [HBM] * 4,
        [
            pltpu.VMEM((64, 384), f32),
            pltpu.VMEM(hidden.shape, bf16),
            pltpu.VMEM(attn_gain.shape, bf16),
            pltpu.VMEM(w_query.shape, bf16),
            pltpu.VMEM(w_keyval.shape[::-1], bf16),
            pltpu.SemaphoreType.DMA((4,)),
        ],
        limit=8,
        name="project",
    )(place, *map(in_hbm, (hidden, attn_gain, w_query, w_keyval.T)))
    straight, swapped = call(
        table_kernel,
        [sds((2, OWN, 128), f32)] * 2,
        [SMEM, HBM, HBM],
        [pltpu.VMEM((HEAD_WIDTH,), bf16)] * 2 + [pltpu.SemaphoreType.DMA((2,))],
        limit=4,
        name="tables",
    )(*map(in_hbm, (lengths, query_gain, key_norm_gain)))
    payload = call(
        heads_kernel,
        sds((WIDE, PACKED, 128), bf16),
        [VMEM] * 4,
        limit=8,
        name="heads",
        cost=pl.CostEstimate(flops=20_000_000_000, bytes_accessed=1 << 20, transcendentals=0),
    )(*reduce_blocks(keep, send, "x"), straight, swapped)
    gathered = exchange(payload)

    parts = call(
        attend_kernel,
        sds((WIDE, PACKED, 128), bf16),
        [SMEM, SMEM, VMEM, VMEM, VMEM],
        [
            pltpu.VMEM((OWN * QUERY_HEADS, 128), f32),
            pltpu.VMEM((OWN * QUERY_HEADS, 256), f32),
            pltpu.VMEM((OWN * QUERY_HEADS, 256), bf16),
            pltpu.VMEM((OWN * QUERY_HEADS, 128), f32),
            pltpu.VMEM((OWN * QUERY_HEADS, 128), f32),
        ],
        limit=8,
        name="attend",
    )(lengths, block_index.reshape(OWN), gathered, in_vmem(keys_cache), in_vmem(values_cache))
    heads_out, heads_own = call(
        combine_kernel, [sds((OWN, 256), bf16)] * 2, [SMEM] + [VMEM] * 4, limit=8, name="combine"
    )(place, exchange(parts), gathered, straight, swapped)

    def product(own, weight, name):
        return call(
            product_kernel,
            [sds((2 * OWN, 1280), f32), sds((2 * OWN, 1280), bf16)],
            [SMEM] + [VMEM] * 3,
            [pltpu.VMEM((64, own.shape[1]), bf16), pltpu.VMEM((64, 1280), f32)],
            limit=8,
            name=name,
        )(place, *gather(own, "x"), weight)

    stream, keep, send = call(
        gate_up_kernel,
        [
            sds((64, 1280), f32),
            sds((2 * OWN, 2 * HALF), f32),
            sds((2 * OWN, 2 * HALF), bf16),
        ],
        [SMEM] + [VMEM] * 6,
        [pltpu.VMEM((64, 2 * HALF), f32)],
        limit=12,
        name="gate_up",
    )(place, hidden, *sum_wide(*product(heads_own, w_out, "output")), mlp_gain, w_gate.T, w_up.T)
    activated = call(
        activate_kernel, sds((OWN, HALF), bf16), [VMEM] * 2, limit=8, name="activate"
    )(*reduce_blocks(keep, send, "x"))
    layer_out = call(
        final_kernel, sds((64, 1280), bf16), [SMEM] + [VMEM] * 3, limit=8, name="final"
    )(place, stream, *sum_wide(*product(activated, w_down, "down")))
    return (layer_out, heads_out)


def solution(mesh):
    in_specs = (
        P(None, "rows"),
        P("rows"),
        P("rows", "wide"),
        P("rows", "wide"),
        P(),
        P(),
        P("rows", "wide", None),
        P("rows", "wide", None),
        P("rows"),
        P("rows", "wide"),
        P("wide", "rows"),
        P("rows"),
        P("rows", "wide"),
        P("rows", "wide"),
        P("wide", "rows"),
    )
    out_specs = (P(None, "rows"), P("rows", "wide"))
    return jax.shard_map(body, mesh=mesh, in_specs=in_specs, out_specs=out_specs, check_vma=False)
```

```python
import jax
import jax.numpy as jnp
import numpy as np
from jax import lax
from jax.experimental import pallas as pl
from jax.experimental.pallas import tpu as pltpu
from jax.sharding import PartitionSpec as P

MODEL_WIDTH = 5120
QUERY_HEADS = 64
KEY_VALUE_HEADS = 8
HEAD_WIDTH = 128
EPSILON = 1e-06
ROPE_BASE = 1000000.0
MASKED = -1e30
SCALE = HEAD_WIDTH ** (-0.5)

ROWS = 4
WIDE = 32
WIDE_AXES = ("y", "z", "core")
CHIPS = 16
CHIP_AXES = ("y", "z")
PACKED = 40
AT_ONCE = 2
GROUPS = 8
OWN = 16
BLOCK = 256
HIDDEN_UNITS = 800
HALF = 896

f32 = jnp.float32
bf16 = jnp.bfloat16
VMEM = pl.BlockSpec(memory_space=pltpu.VMEM)
HBM = pl.BlockSpec(memory_space=pltpu.HBM)
SMEM = pl.BlockSpec(memory_space=pltpu.SMEM)
NT = (((1,), (1,)), ((), ()))


def call(
    kernel, out_shape, in_specs, scratch_shapes=(), limit=24, name=None, cost=None
):
    many = isinstance(out_shape, (tuple, list))
    return pl.pallas_call(
        kernel,
        out_shape=out_shape,
        in_specs=in_specs,
        out_specs=[VMEM] * len(out_shape) if many else VMEM,
        scratch_shapes=list(scratch_shapes),
        compiler_params=pltpu.CompilerParams(vmem_limit_bytes=limit << 20),
        cost_estimate=cost,
        name=name,
    )


def in_vmem(value):
    return pltpu.with_memory_space_constraint(value, pltpu.VMEM)


def in_hbm(value):
    return pltpu.with_memory_space_constraint(value, pltpu.HBM)


def row_block(mine, k):
    return pl.ds(pl.multiple_of(lax.rem(mine + k, ROWS) * OWN, OWN), OWN)


def terms(value, count):
    out = []
    for _ in range(count):
        out.append(value.astype(bf16).astype(f32))
        value = value - out[-1]
    return out


def swap_halves(value):
    half = HEAD_WIDTH // 2
    return jnp.concatenate([value[..., half:], value[..., :half]], axis=-1)


def norm_rope(value, straight, swapped):
    value = value * lax.rsqrt(jnp.mean(value * value, axis=-1, keepdims=True) + EPSILON)
    return value * straight + swap_halves(value) * swapped


def pack(value):
    return jnp.concatenate([value[:8], value[8:]], axis=1)


def unpack(value):
    return jnp.concatenate([value[:, :64], value[:, 64:]], axis=0)


def project_kernel(place_ref, hidden_hbm, gain_hbm, wq_hbm, wkv_hbm, *rest):
    outs, (whole, hidden_ref, gain_ref, wq_ref, wkv_ref, sems) = rest[:ROWS], rest[ROWS:]
    moves = [
        pltpu.make_async_copy(source, target, sems.at[at])
        for at, (source, target) in enumerate(
            (
                (hidden_hbm, hidden_ref),
                (wkv_hbm, wkv_ref),
                (wq_hbm, wq_ref),
                (gain_hbm, gain_ref),
            )
        )
    ]
    for move in moves:
        move.start()
    moves[0].wait()
    hidden = hidden_ref[...].astype(f32)
    square = jnp.sum(hidden * hidden, axis=1, keepdims=True)
    moves[3].wait()
    scaled = (hidden * gain_ref[...].astype(f32)[None]).astype(bf16)
    moves[1].wait()
    keyval = lax.dot_general(scaled, wkv_ref[...], NT, preferred_element_type=f32)
    whole[:, 256:] = jnp.concatenate([keyval, jnp.broadcast_to(square, keyval.shape)], axis=1)
    moves[2].wait()
    whole[:, :256] = jnp.dot(scaled, wq_ref[...], preferred_element_type=f32)
    mine = place_ref[0] // WIDE
    for k in range(ROWS):
        outs[k][...] = whole[row_block(mine, k), :]


def table_kernel(
    length_ref, query_hbm, key_hbm, straight_ref, swapped_ref, query_ref, key_ref, sems
):
    gains = (query_ref, key_ref)
    moves = [
        pltpu.make_async_copy(source, gains[at], sems.at[at])
        for at, source in enumerate((query_hbm, key_hbm))
    ]
    for move in moves:
        move.start()
    row = lax.broadcasted_iota(jnp.int32, (OWN, 128), 0)
    lane = lax.broadcasted_iota(jnp.int32, (OWN, 128), 1)
    position = jnp.zeros((OWN, 128), jnp.int32)
    for b in range(OWN):
        position = jnp.where(row == b, length_ref[b], position)
    half = HEAD_WIDTH // 2
    pair = lax.rem(lax.broadcasted_iota(jnp.int32, (1, 128), 1), half)
    frequency = jnp.zeros((1, 128), f32)
    for at in range(half):
        frequency = jnp.where(pair == at, np.float32(ROPE_BASE ** (-2.0 * at / HEAD_WIDTH)), frequency)
    angle = position.astype(f32) * frequency
    cosine, sine = jnp.cos(angle), jnp.sin(angle)
    sine = jnp.where(lane < half, -sine, sine)
    for at in range(2):
        moves[at].wait()
        gain = gains[at][...].astype(f32)[None]
        straight_ref[at] = cosine * gain
        swapped_ref[at] = sine * swap_halves(gain)


def heads_kernel(a_ref, b_ref, c_ref, d_ref, straight_ref, swapped_ref, out_ref):
    total = (a_ref[...] + b_ref[...]) + (c_ref[...] + d_ref[...])
    inverse = lax.rsqrt(total[:, 320:321] / MODEL_WIDTH + EPSILON)
    scaled = total * inverse
    straight, swapped = straight_ref[0], swapped_ref[0]
    parts = [
        norm_rope(scaled[:, j * 128 : (j + 1) * 128], straight, swapped) for j in range(2)
    ]
    parts.append(pack(scaled[:, 256:320]))
    out = jnp.concatenate(parts, axis=0).astype(bf16)
    out_ref[...] = jnp.broadcast_to(out[None], out_ref.shape)


def of_cores(place_ref, own_ref, other_ref):
    core = lax.rem(place_ref[0], 2)
    return (own_ref, core), (other_ref, 1 - core)


def attend_kernel(
    place_ref,
    length_ref,
    block_ref,
    own_ref,
    other_ref,
    k_ref,
    v_ref,
    o_ref,
    q_scr,
    p_scr,
    w_scr,
    n_scr,
    s_scr,
):
    for ref, core in of_cores(place_ref, own_ref, other_ref):
        for chip in range(CHIPS):
            for j in range(2):
                head = 4 * chip + 2 * core + j
                q_scr[pl.ds(head, OWN, stride=QUERY_HEADS), :] = ref[
                    chip, j * OWN : (j + 1) * OWN, :
                ].astype(f32)

    row = lax.broadcasted_iota(jnp.int32, (16, 256), 0)
    lane = lax.broadcasted_iota(jnp.int32, (16, 256), 1)
    own_half = (row < 8) == (lane < 128)
    slot = lax.broadcasted_iota(jnp.int32, (QUERY_HEADS, 256), 1)
    place = lax.rem(lax.broadcasted_iota(jnp.int32, (QUERY_HEADS, 128), 1), 8)

    def score(group):
        for u in range(AT_ONCE):
            b = group * AT_ONCE + u
            for p in range(4):
                here = pl.ds(pl.multiple_of(b * QUERY_HEADS + 16 * p, 16), 16)
                pair = q_scr[here, :]
                query = jnp.where(own_half, jnp.concatenate([pair, pair], axis=1), 0.0)
                p_scr[here, :] = lax.dot_general(
                    query.astype(bf16),
                    k_ref[b, :, 256 * p : 256 * p + 256],
                    NT,
                    preferred_element_type=f32,
                )

    def weigh(group):
        for u in range(AT_ONCE):
            b = group * AT_ONCE + u
            here = pl.ds(pl.multiple_of(b * QUERY_HEADS, QUERY_HEADS), QUERY_HEADS)
            visible = slot < length_ref[b] - block_ref[b] * BLOCK
            scores = jnp.where(visible, p_scr[here, :] * SCALE, MASKED)
            shift = jnp.max(scores, axis=1, keepdims=True).astype(bf16).astype(f32)
            weights = jnp.where(visible, jnp.exp(scores - shift), 0.0)
            total = jnp.sum(weights, axis=1, keepdims=True)
            w_scr[here, :] = weights.astype(bf16)
            stats = jnp.where(place == 0, shift, 0.0)
            for at, term in enumerate(terms(total, 2)):
                stats = jnp.where(place == at + 1, term, stats)
            s_scr[pl.ds(b, QUERY_HEADS, stride=OWN), :] = stats

    def add_up(group):
        for u in range(AT_ONCE):
            b = group * AT_ONCE + u
            for p in range(4):
                here = pl.ds(pl.multiple_of(b * QUERY_HEADS + 16 * p, 16), 16)
                both = jnp.dot(
                    w_scr[here, :],
                    v_ref[b, :, 256 * p : 256 * p + 256],
                    preferred_element_type=f32,
                )
                n_scr[pl.ds(16 * p * OWN + b, 16, stride=OWN), :] = jnp.concatenate(
                    [both[:8, :128], both[8:, 128:]], axis=0
                )

    last = GROUPS - 1
    score(0)
    weigh(0)
    score(1)

    @pl.loop(1, last)
    def _(group):
        add_up(group - 1)
        weigh(group)
        score(group + 1)

    add_up(last - 1)
    weigh(last)
    add_up(last)

    lane = lax.broadcasted_iota(jnp.int32, (OWN, 128), 1)
    first = lax.rem(lane, 64) < 8
    for w in range(WIDE):
        rows = [slice((2 * w + j) * OWN, (2 * w + j + 1) * OWN) for j in range(2)]
        o_ref[w, : 2 * OWN, :] = n_scr[2 * w * OWN : 2 * (w + 1) * OWN, :].astype(bf16)
        stats = jnp.where(first, s_scr[rows[0], :], s_scr[rows[1], :])
        o_ref[w, 2 * OWN :, :] = jnp.where(lane[:8] < 64, stats[:8], stats[8:]).astype(bf16)


def combine_kernel(
    place_ref, r_ref, own_ref, other_ref, straight_ref, swapped_ref, out_ref, again_ref
):
    wide = lax.rem(place_ref[0], WIDE)
    group = wide // 4

    def both_halves(chip):
        parts = [unpack(ref[chip, 2 * OWN :, :].astype(f32)) for ref in (own_ref, other_ref)]
        return jnp.where(
            lax.rem(wide, 2) == 0,
            jnp.concatenate(parts, axis=1),
            jnp.concatenate(parts[::-1], axis=1),
        )

    def column(value, at):
        return jnp.concatenate(
            [value[..., at : at + 1], value[..., 64 + at : 65 + at]], axis=-2
        )

    key = both_halves(group)
    value = both_halves(8 + group)
    key = norm_rope(key, straight_ref[1], swapped_ref[1]).astype(bf16).astype(f32)
    fresh = [
        jnp.sum(own_ref[wide // 2, j * OWN : (j + 1) * OWN, :].astype(f32) * key, axis=1, keepdims=True)
        * SCALE
        for j in range(2)
    ]
    lane = lax.broadcasted_iota(jnp.int32, (8, 128), 1)
    stats = r_ref[:, 2 * OWN :, :].astype(f32)
    highest = jnp.max(stats, axis=0)
    for j in range(2):
        packed = jnp.where(lane < 64, fresh[j][:8], fresh[j][8:])
        highest = jnp.where(lax.rem(lane, 64) == 8 * j, jnp.maximum(highest, packed), highest)
    shift_lane = (lax.rem(lane, 64) == 0) | (lax.rem(lane, 64) == 8)
    factors = jnp.where(shift_lane[None], jnp.exp(jnp.where(shift_lane, stats - highest, 0.0)), 0.0)
    spread_factors = factors
    for shift in (1, 2):
        spread_factors = spread_factors + jnp.roll(factors, shift, axis=2)
    totals = jnp.sum(spread_factors * jnp.where(shift_lane, 0.0, stats), axis=0)
    for j in range(2):
        lanes = slice(j * 128, (j + 1) * 128)
        here = slice(j * OWN, (j + 1) * OWN)
        fresh_weight = jnp.exp(fresh[j] - column(highest, 8 * j))
        weight_sum = column(totals, 8 * j + 1) + column(totals, 8 * j + 2) + fresh_weight
        numer = jnp.sum(r_ref[:, here, :].astype(f32) * column(factors, 8 * j), axis=0)
        numer = numer + fresh_weight.astype(bf16).astype(f32) * value
        heads = (numer / weight_sum).astype(bf16)
        out_ref[:, lanes] = heads
        again_ref[:, lanes] = heads


def product_kernel(place_ref, a_ref, b_ref, c_ref, d_ref, w_ref, keep_ref, send_ref, whole):
    left = jnp.concatenate([a_ref[...], b_ref[...], c_ref[...], d_ref[...]], axis=0)
    whole[...] = jnp.dot(left[:, : w_ref.shape[0]], w_ref[...], preferred_element_type=f32)
    half = keep_ref.shape[0]
    for ref, core in of_cores(place_ref, keep_ref, send_ref):
        ref[...] = whole[pl.ds(pl.multiple_of(core * half, half), half), :].astype(ref.dtype)


def chip_sum_kernel(keep_ref, got_ref, out_ref):
    total = (keep_ref[...] + got_ref[...].astype(f32)).astype(bf16)
    for chip in range(CHIPS):
        out_ref[chip] = total[2 * chip : 2 * chip + 2]


def sum_spread_kernel(got_ref, out_ref):
    total = jnp.sum(got_ref[...].astype(f32), axis=0).astype(bf16)
    out_ref[...] = jnp.broadcast_to(total[None], out_ref.shape)


def row_blocks(place_ref, own_ref, other_ref):
    for ref, core in of_cores(place_ref, own_ref, other_ref):
        for at in range(2):
            block = ref[at * 8 : (at + 1) * 8].astype(f32)
            yield 2 * core + at, block.reshape(OWN, block.shape[-1])


def gate_up_kernel(
    place_ref, hidden_ref, own_ref, other_ref, gain_ref, wg_ref, wu_ref, stream_ref, *outs
):
    mine = place_ref[0] // WIDE
    for block, attended in row_blocks(place_ref, own_ref, other_ref):
        hidden = hidden_ref[row_block(mine, block), :].astype(f32)
        stream_ref[row_block(0, block), :] = hidden + attended
    stream = stream_ref[...]
    square = jnp.sum(stream * stream, axis=1, keepdims=True)
    scaled = (stream * gain_ref[...].astype(f32)[None]).astype(bf16)
    gate = lax.dot_general(scaled, wg_ref[...], NT, preferred_element_type=f32).astype(bf16)
    up = lax.dot_general(scaled, wu_ref[...], NT, preferred_element_type=f32).astype(bf16)
    pad = HALF - HIDDEN_UNITS
    place = lax.broadcasted_iota(jnp.int32, (stream.shape[0], pad), 1)
    norm = jnp.zeros(place.shape, f32)
    for at, term in enumerate(terms(square, 3)):
        norm = jnp.where(place == at, term, norm)
    norm = norm.astype(bf16)
    for k in range(ROWS):
        at = slice(k * OWN, (k + 1) * OWN)
        outs[k][...] = jnp.concatenate([gate[at], norm[at], up[at], norm[at]], axis=1)


def activate_kernel(a_ref, b_ref, c_ref, d_ref, out_ref):
    total = (a_ref[...].astype(f32) + b_ref[...].astype(f32)) + (
        c_ref[...].astype(f32) + d_ref[...].astype(f32)
    )
    square = (
        total[:, HIDDEN_UNITS : HIDDEN_UNITS + 1]
        + total[:, HIDDEN_UNITS + 1 : HIDDEN_UNITS + 2]
        + total[:, HIDDEN_UNITS + 2 : HIDDEN_UNITS + 3]
    )
    inverse = lax.rsqrt(square / MODEL_WIDTH + EPSILON)
    gate = total[:, :HALF] * inverse
    up = total[:, HALF:] * inverse
    out_ref[...] = (gate / (1.0 + jnp.exp(-gate)) * up).astype(bf16)


def final_kernel(place_ref, stream_ref, own_ref, other_ref, out_ref):
    mine = place_ref[0] // WIDE
    for block, down in row_blocks(place_ref, own_ref, other_ref):
        total = stream_ref[row_block(0, block), :] + down
        out_ref[row_block(mine, block), :] = total.astype(bf16)


def to_rows(blocks):
    got = list(blocks)
    for k in (2, 1, 3):
        got[k] = lax.ppermute(blocks[k], "rows", [(i, (i + k) % ROWS) for i in range(ROWS)])
    return got


def from_rows(own):
    got = [own] * ROWS
    for k in (2, 1, 3):
        got[k] = lax.ppermute(own, "rows", [((i + k) % ROWS, i) for i in range(ROWS)])
    return got


def exchange(blocks, axes):
    return lax.all_to_all(blocks, axes, split_axis=0, concat_axis=0, tiled=True)


def from_other_core(value):
    return lax.ppermute(value, "core", [(0, 1), (1, 0)])


def sum_wide(keep, send):
    blocks = jax.ShapeDtypeStruct((CHIPS, 2, send.shape[1]), bf16)
    part = call(chip_sum_kernel, blocks, [VMEM] * 2, limit=4, name="chip_sum")(
        keep, from_other_core(send)
    )
    total = call(sum_spread_kernel, blocks, [VMEM], limit=4, name="sum_spread")(
        exchange(part, CHIP_AXES)
    )
    own = exchange(total, CHIP_AXES)
    return own, from_other_core(own)


def body(
    hidden,
    attn_gain,
    w_query,
    w_keyval,
    query_gain,
    key_norm_gain,
    keys_cache,
    values_cache,
    lengths,
    block_index,
    w_out,
    mlp_gain,
    w_gate,
    w_up,
    w_down,
):
    place = lax.axis_index(("rows", *WIDE_AXES)).astype(jnp.int32).reshape(1)
    sds = jax.ShapeDtypeStruct

    blocks = call(
        project_kernel,
        [sds((OWN, 384), f32)] * ROWS,
        [SMEM] + [HBM] * 4,
        [
            pltpu.VMEM((64, 384), f32),
            pltpu.VMEM(hidden.shape, bf16),
            pltpu.VMEM(attn_gain.shape, bf16),
            pltpu.VMEM(w_query.shape, bf16),
            pltpu.VMEM(w_keyval.shape[::-1], bf16),
            pltpu.SemaphoreType.DMA((4,)),
        ],
        limit=8,
        name="project",
    )(place, *map(in_hbm, (hidden, attn_gain, w_query, w_keyval.T)))
    straight, swapped = call(
        table_kernel,
        [sds((2, OWN, 128), f32)] * 2,
        [SMEM, HBM, HBM],
        [pltpu.VMEM((HEAD_WIDTH,), bf16)] * 2 + [pltpu.SemaphoreType.DMA((2,))],
        limit=4,
        name="tables",
    )(*map(in_hbm, (lengths, query_gain, key_norm_gain)))
    payload = call(
        heads_kernel,
        sds((CHIPS, PACKED, 128), bf16),
        [VMEM] * 6,
        limit=8,
        name="heads",
        cost=pl.CostEstimate(flops=20_000_000_000, bytes_accessed=1 << 20, transcendentals=0),
    )(*to_rows(blocks), straight, swapped)
    gathered = exchange(payload, CHIP_AXES)
    gathered = (gathered, from_other_core(gathered))

    parts = call(
        attend_kernel,
        sds((WIDE, PACKED, 128), bf16),
        [SMEM] * 3 + [VMEM] * 4,
        [
            pltpu.VMEM((OWN * QUERY_HEADS, 128), f32),
            pltpu.VMEM((OWN * QUERY_HEADS, 256), f32),
            pltpu.VMEM((OWN * QUERY_HEADS, 256), bf16),
            pltpu.VMEM((OWN * QUERY_HEADS, 128), f32),
            pltpu.VMEM((OWN * QUERY_HEADS, 128), f32),
        ],
        limit=8,
        name="attend",
    )(place, lengths, block_index.reshape(OWN), *gathered, in_vmem(keys_cache), in_vmem(values_cache))
    heads_out, heads_own = call(
        combine_kernel, [sds((OWN, 256), bf16)] * 2, [SMEM] + [VMEM] * 5, limit=8, name="combine"
    )(place, exchange(parts, WIDE_AXES), *gathered, straight, swapped)

    def product(own, weight, name):
        return call(
            product_kernel,
            [sds((32, 1280), f32), sds((32, 1280), bf16)],
            [SMEM] + [VMEM] * 5,
            [pltpu.VMEM((64, 1280), f32)],
            limit=8,
            name=name,
        )(place, *from_rows(own), weight)

    attended = sum_wide(*product(heads_own, w_out, "output"))
    stream, *blocks = call(
        gate_up_kernel,
        [sds((64, 1280), f32)] + [sds((OWN, 2 * HALF), bf16)] * ROWS,
        [SMEM] + [VMEM] * 6,
        limit=12,
        name="gate_up",
    )(place, hidden, *attended, mlp_gain, w_gate.T, w_up.T)
    activated = call(
        activate_kernel, sds((OWN, HALF), bf16), [VMEM] * 4, limit=8, name="activate"
    )(*to_rows(blocks))
    down = sum_wide(*product(activated, w_down, "down"))
    layer_out = call(
        final_kernel, sds((64, 1280), bf16), [SMEM] + [VMEM] * 3, limit=8, name="final"
    )(place, stream, *down)
    return (layer_out, heads_out)


def solution(mesh):
    mesh = jax.sharding.Mesh(
        mesh.devices.reshape(4, 4, 4, 2), ("rows", "y", "z", "core")
    )
    in_specs = (
        P(None, "rows"),
        P("rows"),
        P("rows", WIDE_AXES),
        P("rows", WIDE_AXES),
        P(),
        P(),
        P("rows", WIDE_AXES, None),
        P("rows", WIDE_AXES, None),
        P("rows"),
        P("rows", WIDE_AXES),
        P(WIDE_AXES, "rows"),
        P("rows"),
        P("rows", WIDE_AXES),
        P("rows", WIDE_AXES),
        P(WIDE_AXES, "rows"),
    )
    out_specs = (P(None, "rows"), P("rows", WIDE_AXES))
    return jax.shard_map(body, mesh=mesh, in_specs=in_specs, out_specs=out_specs, check_vma=False)
```

```python
import jax
import jax.numpy as jnp
import numpy as np
from jax import lax
from jax.experimental import pallas as pl
from jax.experimental.pallas import tpu as pltpu
from jax.sharding import PartitionSpec as P

MODEL_WIDTH = 5120
QUERY_HEADS = 64
KEY_VALUE_HEADS = 8
HEAD_WIDTH = 128
EPSILON = 1e-06
ROPE_BASE = 1000000.0
MASKED = -1e30
SCALE = HEAD_WIDTH ** (-0.5)

ROWS = 4
WIDE = 32
WIDE_AXES = ("y", "z", "core")
CHIPS = 16
CHIP_AXES = ("y", "z")
PACKED = 40
AT_ONCE = 2
GROUPS = 8
OWN = 16
BLOCK = 256
HIDDEN_UNITS = 800
HALF = 896

f32 = jnp.float32
bf16 = jnp.bfloat16
VMEM = pl.BlockSpec(memory_space=pltpu.VMEM)
HBM = pl.BlockSpec(memory_space=pltpu.HBM)
SMEM = pl.BlockSpec(memory_space=pltpu.SMEM)
NT = (((1,), (1,)), ((), ()))


def call(
    kernel, out_shape, in_specs, scratch_shapes=(), limit=24, name=None, cost=None
):
    many = isinstance(out_shape, (tuple, list))
    return pl.pallas_call(
        kernel,
        out_shape=out_shape,
        in_specs=in_specs,
        out_specs=[VMEM] * len(out_shape) if many else VMEM,
        scratch_shapes=list(scratch_shapes),
        compiler_params=pltpu.CompilerParams(vmem_limit_bytes=limit << 20),
        cost_estimate=cost,
        name=name,
    )


def in_vmem(value):
    return pltpu.with_memory_space_constraint(value, pltpu.VMEM)


def in_hbm(value):
    return pltpu.with_memory_space_constraint(value, pltpu.HBM)


def row_block(mine, k):
    return pl.ds(pl.multiple_of(lax.rem(mine + k, ROWS) * OWN, OWN), OWN)


def terms(value, count):
    out = []
    for _ in range(count):
        out.append(value.astype(bf16).astype(f32))
        value = value - out[-1]
    return out


def swap_halves(value):
    half = HEAD_WIDTH // 2
    return jnp.concatenate([value[..., half:], value[..., :half]], axis=-1)


def norm_rope(value, straight, swapped):
    value = value * lax.rsqrt(jnp.mean(value * value, axis=-1, keepdims=True) + EPSILON)
    return value * straight + swap_halves(value) * swapped


def pack(value):
    return jnp.concatenate([value[:8], value[8:]], axis=1)


def unpack(value):
    return jnp.concatenate([value[:, :64], value[:, 64:]], axis=0)


def project_kernel(place_ref, hidden_hbm, gain_hbm, wq_hbm, wkv_hbm, *rest):
    outs, (whole, hidden_ref, gain_ref, wq_ref, wkv_ref, sems) = rest[:ROWS], rest[ROWS:]
    moves = [
        pltpu.make_async_copy(source, target, sems.at[at])
        for at, (source, target) in enumerate(
            (
                (hidden_hbm, hidden_ref),
                (wkv_hbm, wkv_ref),
                (wq_hbm, wq_ref),
                (gain_hbm, gain_ref),
            )
        )
    ]
    for move in moves:
        move.start()
    moves[0].wait()
    hidden = hidden_ref[...].astype(f32)
    square = jnp.sum(hidden * hidden, axis=1, keepdims=True)
    moves[3].wait()
    scaled = (hidden * gain_ref[...].astype(f32)[None]).astype(bf16)
    moves[1].wait()
    keyval = lax.dot_general(scaled, wkv_ref[...], NT, preferred_element_type=f32)
    whole[:, 256:] = jnp.concatenate([keyval, jnp.broadcast_to(square, keyval.shape)], axis=1)
    moves[2].wait()
    whole[:, :256] = jnp.dot(scaled, wq_ref[...], preferred_element_type=f32)
    mine = place_ref[0] // WIDE
    for k in range(ROWS):
        outs[k][...] = whole[row_block(mine, k), :]


def table_kernel(
    length_ref, query_hbm, key_hbm, straight_ref, swapped_ref, query_ref, key_ref, sems
):
    gains = (query_ref, key_ref)
    moves = [
        pltpu.make_async_copy(source, gains[at], sems.at[at])
        for at, source in enumerate((query_hbm, key_hbm))
    ]
    for move in moves:
        move.start()
    row = lax.broadcasted_iota(jnp.int32, (OWN, 128), 0)
    lane = lax.broadcasted_iota(jnp.int32, (OWN, 128), 1)
    position = jnp.zeros((OWN, 128), jnp.int32)
    for b in range(OWN):
        position = jnp.where(row == b, length_ref[b], position)
    half = HEAD_WIDTH // 2
    pair = lax.rem(lax.broadcasted_iota(jnp.int32, (1, 128), 1), half)
    frequency = jnp.zeros((1, 128), f32)
    for at in range(half):
        frequency = jnp.where(pair == at, np.float32(ROPE_BASE ** (-2.0 * at / HEAD_WIDTH)), frequency)
    angle = position.astype(f32) * frequency
    cosine, sine = jnp.cos(angle), jnp.sin(angle)
    sine = jnp.where(lane < half, -sine, sine)
    for at in range(2):
        moves[at].wait()
        gain = gains[at][...].astype(f32)[None]
        straight_ref[at] = cosine * gain
        swapped_ref[at] = sine * swap_halves(gain)


def heads_kernel(a_ref, b_ref, c_ref, d_ref, straight_ref, swapped_ref, out_ref):
    total = (a_ref[...] + b_ref[...]) + (c_ref[...] + d_ref[...])
    inverse = lax.rsqrt(total[:, 320:321] / MODEL_WIDTH + EPSILON)
    scaled = total * inverse
    straight, swapped = straight_ref[0], swapped_ref[0]
    parts = [
        norm_rope(scaled[:, j * 128 : (j + 1) * 128], straight, swapped) for j in range(2)
    ]
    parts.append(pack(scaled[:, 256:320]))
    out = jnp.concatenate(parts, axis=0).astype(bf16)
    out_ref[...] = jnp.broadcast_to(out[None], out_ref.shape)


def of_cores(place_ref, own_ref, other_ref):
    core = lax.rem(place_ref[0], 2)
    return (own_ref, core), (other_ref, 1 - core)


def attend_kernel(
    place_ref,
    length_ref,
    block_ref,
    own_ref,
    other_ref,
    k_ref,
    v_ref,
    o_ref,
    q_scr,
    p_scr,
    w_scr,
    n_scr,
    s_scr,
):
    for ref, core in of_cores(place_ref, own_ref, other_ref):
        for chip in range(CHIPS):
            for j in range(2):
                head = 4 * chip + 2 * core + j
                q_scr[pl.ds(head, OWN, stride=QUERY_HEADS), :] = ref[
                    chip, j * OWN : (j + 1) * OWN, :
                ].astype(f32)

    row = lax.broadcasted_iota(jnp.int32, (16, 256), 0)
    lane = lax.broadcasted_iota(jnp.int32, (16, 256), 1)
    own_half = (row < 8) == (lane < 128)
    slot = lax.broadcasted_iota(jnp.int32, (QUERY_HEADS, 256), 1)
    place = lax.rem(lax.broadcasted_iota(jnp.int32, (QUERY_HEADS, 128), 1), 8)

    def score(group):
        for u in range(AT_ONCE):
            b = group * AT_ONCE + u
            for p in range(4):
                here = pl.ds(pl.multiple_of(b * QUERY_HEADS + 16 * p, 16), 16)
                pair = q_scr[here, :]
                query = jnp.where(own_half, jnp.concatenate([pair, pair], axis=1), 0.0)
                p_scr[here, :] = lax.dot_general(
                    query.astype(bf16),
                    k_ref[b, :, 256 * p : 256 * p + 256],
                    NT,
                    preferred_element_type=f32,
                )

    def weigh(group):
        for u in range(AT_ONCE):
            b = group * AT_ONCE + u
            here = pl.ds(pl.multiple_of(b * QUERY_HEADS, QUERY_HEADS), QUERY_HEADS)
            visible = slot < length_ref[b] - block_ref[b] * BLOCK
            scores = jnp.where(visible, p_scr[here, :] * SCALE, MASKED)
            shift = jnp.max(scores, axis=1, keepdims=True).astype(bf16).astype(f32)
            weights = jnp.where(visible, jnp.exp(scores - shift), 0.0)
            total = jnp.sum(weights, axis=1, keepdims=True)
            w_scr[here, :] = weights.astype(bf16)
            stats = jnp.where(place == 0, shift, 0.0)
            for at, term in enumerate(terms(total, 2)):
                stats = jnp.where(place == at + 1, term, stats)
            s_scr[pl.ds(b, QUERY_HEADS, stride=OWN), :] = stats

    def add_up(group):
        for u in range(AT_ONCE):
            b = group * AT_ONCE + u
            for p in range(4):
                here = pl.ds(pl.multiple_of(b * QUERY_HEADS + 16 * p, 16), 16)
                both = jnp.dot(
                    w_scr[here, :],
                    v_ref[b, :, 256 * p : 256 * p + 256],
                    preferred_element_type=f32,
                )
                n_scr[pl.ds(16 * p * OWN + b, 16, stride=OWN), :] = jnp.concatenate(
                    [both[:8, :128], both[8:, 128:]], axis=0
                )

    last = GROUPS - 1
    score(0)
    weigh(0)
    score(1)

    @pl.loop(1, last)
    def _(group):
        add_up(group - 1)
        weigh(group)
        score(group + 1)

    add_up(last - 1)
    weigh(last)
    add_up(last)

    lane = lax.broadcasted_iota(jnp.int32, (OWN, 128), 1)
    first = lax.rem(lane, 64) < 8
    for w in range(WIDE):
        rows = [slice((2 * w + j) * OWN, (2 * w + j + 1) * OWN) for j in range(2)]
        o_ref[w, : 2 * OWN, :] = n_scr[2 * w * OWN : 2 * (w + 1) * OWN, :].astype(bf16)
        stats = jnp.where(first, s_scr[rows[0], :], s_scr[rows[1], :])
        o_ref[w, 2 * OWN :, :] = jnp.where(lane[:8] < 64, stats[:8], stats[8:]).astype(bf16)


def combine_kernel(
    place_ref, r_ref, own_ref, other_ref, straight_ref, swapped_ref, out_ref, again_ref
):
    wide = lax.rem(place_ref[0], WIDE)
    group = wide // 4

    def both_halves(chip):
        parts = [unpack(ref[chip, 2 * OWN :, :].astype(f32)) for ref in (own_ref, other_ref)]
        return jnp.where(
            lax.rem(wide, 2) == 0,
            jnp.concatenate(parts, axis=1),
            jnp.concatenate(parts[::-1], axis=1),
        )

    def column(value, at):
        return jnp.concatenate(
            [value[..., at : at + 1], value[..., 64 + at : 65 + at]], axis=-2
        )

    key = both_halves(group)
    value = both_halves(8 + group)
    key = norm_rope(key, straight_ref[1], swapped_ref[1]).astype(bf16).astype(f32)
    fresh = [
        jnp.sum(own_ref[wide // 2, j * OWN : (j + 1) * OWN, :].astype(f32) * key, axis=1, keepdims=True)
        * SCALE
        for j in range(2)
    ]
    lane = lax.broadcasted_iota(jnp.int32, (8, 128), 1)
    stats = r_ref[:, 2 * OWN :, :].astype(f32)
    highest = jnp.max(stats, axis=0)
    for j in range(2):
        packed = jnp.where(lane < 64, fresh[j][:8], fresh[j][8:])
        highest = jnp.where(lax.rem(lane, 64) == 8 * j, jnp.maximum(highest, packed), highest)
    shift_lane = (lax.rem(lane, 64) == 0) | (lax.rem(lane, 64) == 8)
    factors = jnp.where(shift_lane[None], jnp.exp(jnp.where(shift_lane, stats - highest, 0.0)), 0.0)
    spread_factors = factors
    for shift in (1, 2):
        spread_factors = spread_factors + jnp.roll(factors, shift, axis=2)
    totals = jnp.sum(spread_factors * jnp.where(shift_lane, 0.0, stats), axis=0)
    for j in range(2):
        lanes = slice(j * 128, (j + 1) * 128)
        here = slice(j * OWN, (j + 1) * OWN)
        fresh_weight = jnp.exp(fresh[j] - column(highest, 8 * j))
        weight_sum = column(totals, 8 * j + 1) + column(totals, 8 * j + 2) + fresh_weight
        numer = jnp.sum(r_ref[:, here, :].astype(f32) * column(factors, 8 * j), axis=0)
        numer = numer + fresh_weight.astype(bf16).astype(f32) * value
        heads = (numer / weight_sum).astype(bf16)
        out_ref[:, lanes] = heads
        again_ref[:, lanes] = heads


def product_kernel(place_ref, a_ref, b_ref, c_ref, d_ref, w_ref, keep_ref, send_ref, whole):
    left = jnp.concatenate([a_ref[...], b_ref[...], c_ref[...], d_ref[...]], axis=0)
    whole[...] = jnp.dot(left[:, : w_ref.shape[0]], w_ref[...], preferred_element_type=f32)
    half = keep_ref.shape[0]
    for ref, core in of_cores(place_ref, keep_ref, send_ref):
        ref[...] = whole[pl.ds(pl.multiple_of(core * half, half), half), :].astype(ref.dtype)


def add_kernel(*refs):
    out_ref = refs[-1]
    parts = [ref[...].astype(f32) for ref in refs[:-1]]
    if len(parts) == ROWS:
        parts = [parts[0] + parts[2], parts[1] + parts[3]]
    out_ref[...] = (parts[0] + parts[1]).astype(bf16)


def row_blocks(place_ref, own_ref, other_ref):
    for ref, core in of_cores(place_ref, own_ref, other_ref):
        for at in range(2):
            yield 2 * core + at, ref[at * OWN : (at + 1) * OWN, :].astype(f32)


def gate_up_kernel(
    place_ref, hidden_ref, own_ref, other_ref, gain_ref, wg_ref, wu_ref, stream_ref, *outs
):
    mine = place_ref[0] // WIDE
    for block, attended in row_blocks(place_ref, own_ref, other_ref):
        hidden = hidden_ref[row_block(mine, block), :].astype(f32)
        stream_ref[row_block(0, block), :] = hidden + attended
    stream = stream_ref[...]
    square = jnp.sum(stream * stream, axis=1, keepdims=True)
    scaled = (stream * gain_ref[...].astype(f32)[None]).astype(bf16)
    gate = lax.dot_general(scaled, wg_ref[...], NT, preferred_element_type=f32).astype(bf16)
    up = lax.dot_general(scaled, wu_ref[...], NT, preferred_element_type=f32).astype(bf16)
    pad = HALF - HIDDEN_UNITS
    place = lax.broadcasted_iota(jnp.int32, (stream.shape[0], pad), 1)
    norm = jnp.zeros(place.shape, f32)
    for at, term in enumerate(terms(square, 3)):
        norm = jnp.where(place == at, term, norm)
    norm = norm.astype(bf16)
    for k in range(ROWS):
        at = slice(k * OWN, (k + 1) * OWN)
        outs[k][...] = jnp.concatenate([gate[at], norm[at], up[at], norm[at]], axis=1)


def activate_kernel(a_ref, b_ref, c_ref, d_ref, out_ref):
    total = (a_ref[...].astype(f32) + b_ref[...].astype(f32)) + (
        c_ref[...].astype(f32) + d_ref[...].astype(f32)
    )
    square = (
        total[:, HIDDEN_UNITS : HIDDEN_UNITS + 1]
        + total[:, HIDDEN_UNITS + 1 : HIDDEN_UNITS + 2]
        + total[:, HIDDEN_UNITS + 2 : HIDDEN_UNITS + 3]
    )
    inverse = lax.rsqrt(square / MODEL_WIDTH + EPSILON)
    gate = total[:, :HALF] * inverse
    up = total[:, HALF:] * inverse
    out_ref[...] = (gate / (1.0 + jnp.exp(-gate)) * up).astype(bf16)


def final_kernel(place_ref, stream_ref, own_ref, other_ref, out_ref):
    mine = place_ref[0] // WIDE
    for block, down in row_blocks(place_ref, own_ref, other_ref):
        total = stream_ref[row_block(0, block), :] + down
        out_ref[row_block(mine, block), :] = total.astype(bf16)


def to_rows(blocks):
    got = list(blocks)
    for k in (2, 1, 3):
        got[k] = lax.ppermute(blocks[k], "rows", [(i, (i + k) % ROWS) for i in range(ROWS)])
    return got


def from_peers(own, axis):
    got = [own] * ROWS
    for k in (2, 1, 3):
        got[k] = lax.ppermute(own, axis, [((i + k) % ROWS, i) for i in range(ROWS)])
    return got


def exchange(blocks, axes):
    return lax.all_to_all(blocks, axes, split_axis=0, concat_axis=0, tiled=True)


def from_other_core(value):
    return lax.ppermute(value, "core", [(0, 1), (1, 0)])


def sum_wide(keep, send):
    def add(*parts):
        shape = jax.ShapeDtypeStruct(send.shape, bf16)
        return call(add_kernel, shape, [VMEM] * len(parts), limit=4, name="add")(*parts)

    own = add(keep, from_other_core(send))
    own = add(*from_peers(own, "y"))
    own = add(*from_peers(own, "z"))
    return own, from_other_core(own)


def body(
    hidden,
    attn_gain,
    w_query,
    w_keyval,
    query_gain,
    key_norm_gain,
    keys_cache,
    values_cache,
    lengths,
    block_index,
    w_out,
    mlp_gain,
    w_gate,
    w_up,
    w_down,
):
    place = lax.axis_index(("rows", *WIDE_AXES)).astype(jnp.int32).reshape(1)
    sds = jax.ShapeDtypeStruct

    blocks = call(
        project_kernel,
        [sds((OWN, 384), f32)] * ROWS,
        [SMEM] + [HBM] * 4,
        [
            pltpu.VMEM((64, 384), f32),
            pltpu.VMEM(hidden.shape, bf16),
            pltpu.VMEM(attn_gain.shape, bf16),
            pltpu.VMEM(w_query.shape, bf16),
            pltpu.VMEM(w_keyval.shape[::-1], bf16),
            pltpu.SemaphoreType.DMA((4,)),
        ],
        limit=8,
        name="project",
    )(place, *map(in_hbm, (hidden, attn_gain, w_query, w_keyval.T)))
    straight, swapped = call(
        table_kernel,
        [sds((2, OWN, 128), f32)] * 2,
        [SMEM, HBM, HBM],
        [pltpu.VMEM((HEAD_WIDTH,), bf16)] * 2 + [pltpu.SemaphoreType.DMA((2,))],
        limit=4,
        name="tables",
    )(*map(in_hbm, (lengths, query_gain, key_norm_gain)))
    payload = call(
        heads_kernel,
        sds((CHIPS, PACKED, 128), bf16),
        [VMEM] * 6,
        limit=8,
        name="heads",
        cost=pl.CostEstimate(flops=20_000_000_000, bytes_accessed=1 << 20, transcendentals=0),
    )(*to_rows(blocks), straight, swapped)
    gathered = exchange(payload, CHIP_AXES)
    gathered = (gathered, from_other_core(gathered))

    parts = call(
        attend_kernel,
        sds((WIDE, PACKED, 128), bf16),
        [SMEM] * 3 + [VMEM] * 4,
        [
            pltpu.VMEM((OWN * QUERY_HEADS, 128), f32),
            pltpu.VMEM((OWN * QUERY_HEADS, 256), f32),
            pltpu.VMEM((OWN * QUERY_HEADS, 256), bf16),
            pltpu.VMEM((OWN * QUERY_HEADS, 128), f32),
            pltpu.VMEM((OWN * QUERY_HEADS, 128), f32),
        ],
        limit=8,
        name="attend",
    )(place, lengths, block_index.reshape(OWN), *gathered, in_vmem(keys_cache), in_vmem(values_cache))
    heads_out, heads_own = call(
        combine_kernel, [sds((OWN, 256), bf16)] * 2, [SMEM] + [VMEM] * 5, limit=8, name="combine"
    )(place, exchange(parts, WIDE_AXES), *gathered, straight, swapped)

    def product(own, weight, name):
        return call(
            product_kernel,
            [sds((32, 1280), f32), sds((32, 1280), bf16)],
            [SMEM] + [VMEM] * 5,
            [pltpu.VMEM((64, 1280), f32)],
            limit=8,
            name=name,
        )(place, *from_peers(own, "rows"), weight)

    attended = sum_wide(*product(heads_own, w_out, "output"))
    stream, *blocks = call(
        gate_up_kernel,
        [sds((64, 1280), f32)] + [sds((OWN, 2 * HALF), bf16)] * ROWS,
        [SMEM] + [VMEM] * 6,
        limit=12,
        name="gate_up",
    )(place, hidden, *attended, mlp_gain, w_gate.T, w_up.T)
    activated = call(
        activate_kernel, sds((OWN, HALF), bf16), [VMEM] * 4, limit=8, name="activate"
    )(*to_rows(blocks))
    down = sum_wide(*product(activated, w_down, "down"))
    layer_out = call(
        final_kernel, sds((64, 1280), bf16), [SMEM] + [VMEM] * 3, limit=8, name="final"
    )(place, stream, *down)
    return (layer_out, heads_out)


def solution(mesh):
    mesh = jax.sharding.Mesh(
        mesh.devices.reshape(4, 4, 4, 2), ("rows", "y", "z", "core")
    )
    in_specs = (
        P(None, "rows"),
        P("rows"),
        P("rows", WIDE_AXES),
        P("rows", WIDE_AXES),
        P(),
        P(),
        P("rows", WIDE_AXES, None),
        P("rows", WIDE_AXES, None),
        P("rows"),
        P("rows", WIDE_AXES),
        P(WIDE_AXES, "rows"),
        P("rows"),
        P("rows", WIDE_AXES),
        P("rows", WIDE_AXES),
        P(WIDE_AXES, "rows"),
    )
    out_specs = (P(None, "rows"), P("rows", WIDE_AXES))
    return jax.shard_map(body, mesh=mesh, in_specs=in_specs, out_specs=out_specs, check_vma=False)
```

```python
import jax
import jax.numpy as jnp
import numpy as np
from jax import lax
from jax.experimental import pallas as pl
from jax.experimental.pallas import tpu as pltpu
from jax.sharding import PartitionSpec as P

MODEL_WIDTH = 5120
QUERY_HEADS = 64
KEY_VALUE_HEADS = 8
HEAD_WIDTH = 128
EPSILON = 1e-06
ROPE_BASE = 1000000.0
MASKED = -1e30
SCALE = HEAD_WIDTH ** (-0.5)

ROWS = 4
WIDE = 32
WIDE_AXES = ("y", "z", "core")
CHIPS = 16
CHIP_AXES = ("y", "z")
PACKED = 40
AT_ONCE = 2
GROUPS = 8
OWN = 16
BLOCK = 256
HIDDEN_UNITS = 800
HALF = 896

f32 = jnp.float32
bf16 = jnp.bfloat16
VMEM = pl.BlockSpec(memory_space=pltpu.VMEM)
HBM = pl.BlockSpec(memory_space=pltpu.HBM)
SMEM = pl.BlockSpec(memory_space=pltpu.SMEM)
NT = (((1,), (1,)), ((), ()))


def call(
    kernel, out_shape, in_specs, scratch_shapes=(), limit=24, name=None, cost=None
):
    many = isinstance(out_shape, (tuple, list))
    return pl.pallas_call(
        kernel,
        out_shape=out_shape,
        in_specs=in_specs,
        out_specs=[VMEM] * len(out_shape) if many else VMEM,
        scratch_shapes=list(scratch_shapes),
        compiler_params=pltpu.CompilerParams(vmem_limit_bytes=limit << 20),
        cost_estimate=cost,
        name=name,
    )


def in_vmem(value):
    return pltpu.with_memory_space_constraint(value, pltpu.VMEM)


def in_hbm(value):
    return pltpu.with_memory_space_constraint(value, pltpu.HBM)


def row_block(mine, k):
    return pl.ds(pl.multiple_of(lax.rem(mine + k, ROWS) * OWN, OWN), OWN)


def terms(value, count):
    out = []
    for _ in range(count):
        out.append(value.astype(bf16).astype(f32))
        value = value - out[-1]
    return out


def swap_halves(value):
    half = HEAD_WIDTH // 2
    return jnp.concatenate([value[..., half:], value[..., :half]], axis=-1)


def norm_rope(value, straight, swapped):
    value = value * lax.rsqrt(jnp.mean(value * value, axis=-1, keepdims=True) + EPSILON)
    return value * straight + swap_halves(value) * swapped


def pack(value):
    return jnp.concatenate([value[:8], value[8:]], axis=1)


def unpack(value):
    return jnp.concatenate([value[:, :64], value[:, 64:]], axis=0)


def project_kernel(place_ref, hidden_hbm, gain_hbm, wq_hbm, wkv_hbm, *rest):
    outs, (whole, hidden_ref, gain_ref, wq_ref, wkv_ref, sems) = rest[:ROWS], rest[ROWS:]
    moves = [
        pltpu.make_async_copy(source, target, sems.at[at])
        for at, (source, target) in enumerate(
            (
                (hidden_hbm, hidden_ref),
                (wkv_hbm, wkv_ref),
                (wq_hbm, wq_ref),
                (gain_hbm, gain_ref),
            )
        )
    ]
    for move in moves:
        move.start()
    moves[0].wait()
    hidden = hidden_ref[...].astype(f32)
    square = jnp.sum(hidden * hidden, axis=1, keepdims=True)
    moves[3].wait()
    scaled = (hidden * gain_ref[...].astype(f32)[None]).astype(bf16)
    moves[1].wait()
    keyval = lax.dot_general(scaled, wkv_ref[...], NT, preferred_element_type=f32)
    whole[:, 256:] = jnp.concatenate([keyval, jnp.broadcast_to(square, keyval.shape)], axis=1)
    moves[2].wait()
    whole[:, :256] = jnp.dot(scaled, wq_ref[...], preferred_element_type=f32)
    mine = place_ref[0] // WIDE
    for k in range(ROWS):
        outs[k][...] = whole[row_block(mine, k), :]


def table_kernel(
    length_ref, query_hbm, key_hbm, straight_ref, swapped_ref, query_ref, key_ref, sems
):
    gains = (query_ref, key_ref)
    moves = [
        pltpu.make_async_copy(source, gains[at], sems.at[at])
        for at, source in enumerate((query_hbm, key_hbm))
    ]
    for move in moves:
        move.start()
    row = lax.broadcasted_iota(jnp.int32, (OWN, 128), 0)
    lane = lax.broadcasted_iota(jnp.int32, (OWN, 128), 1)
    position = jnp.zeros((OWN, 128), jnp.int32)
    for b in range(OWN):
        position = jnp.where(row == b, length_ref[b], position)
    half = HEAD_WIDTH // 2
    pair = lax.rem(lax.broadcasted_iota(jnp.int32, (1, 128), 1), half)
    frequency = jnp.zeros((1, 128), f32)
    for at in range(half):
        frequency = jnp.where(pair == at, np.float32(ROPE_BASE ** (-2.0 * at / HEAD_WIDTH)), frequency)
    angle = position.astype(f32) * frequency
    cosine, sine = jnp.cos(angle), jnp.sin(angle)
    sine = jnp.where(lane < half, -sine, sine)
    for at in range(2):
        moves[at].wait()
        gain = gains[at][...].astype(f32)[None]
        straight_ref[at] = cosine * gain
        swapped_ref[at] = sine * swap_halves(gain)


def heads_kernel(a_ref, b_ref, c_ref, d_ref, straight_ref, swapped_ref, out_ref):
    total = (a_ref[...] + b_ref[...]) + (c_ref[...] + d_ref[...])
    inverse = lax.rsqrt(total[:, 320:321] / MODEL_WIDTH + EPSILON)
    scaled = total * inverse
    straight, swapped = straight_ref[0], swapped_ref[0]
    parts = [
        norm_rope(scaled[:, j * 128 : (j + 1) * 128], straight, swapped) for j in range(2)
    ]
    parts.append(pack(scaled[:, 256:320]))
    out = jnp.concatenate(parts, axis=0).astype(bf16)
    out_ref[...] = jnp.broadcast_to(out[None], out_ref.shape)


def of_cores(place_ref, own_ref, other_ref):
    core = lax.rem(place_ref[0], 2)
    return (own_ref, core), (other_ref, 1 - core)


def attend_kernel(
    place_ref,
    length_ref,
    block_ref,
    own_ref,
    other_ref,
    k_ref,
    v_ref,
    o_ref,
    q_scr,
    p_scr,
    w_scr,
    n_scr,
    s_scr,
):
    for ref, core in of_cores(place_ref, own_ref, other_ref):
        for chip in range(CHIPS):
            for j in range(2):
                head = 4 * chip + 2 * core + j
                q_scr[pl.ds(head, OWN, stride=QUERY_HEADS), :] = ref[
                    chip, j * OWN : (j + 1) * OWN, :
                ].astype(f32)

    row = lax.broadcasted_iota(jnp.int32, (16, 256), 0)
    lane = lax.broadcasted_iota(jnp.int32, (16, 256), 1)
    own_half = (row < 8) == (lane < 128)
    slot = lax.broadcasted_iota(jnp.int32, (QUERY_HEADS, 256), 1)
    place = lax.rem(lax.broadcasted_iota(jnp.int32, (QUERY_HEADS, 128), 1), 8)

    def score(group):
        for u in range(AT_ONCE):
            b = group * AT_ONCE + u
            for p in range(4):
                here = pl.ds(pl.multiple_of(b * QUERY_HEADS + 16 * p, 16), 16)
                pair = q_scr[here, :]
                query = jnp.where(own_half, jnp.concatenate([pair, pair], axis=1), 0.0)
                p_scr[here, :] = lax.dot_general(
                    query.astype(bf16),
                    k_ref[b, :, 256 * p : 256 * p + 256],
                    NT,
                    preferred_element_type=f32,
                )

    def weigh(group):
        for u in range(AT_ONCE):
            b = group * AT_ONCE + u
            here = pl.ds(pl.multiple_of(b * QUERY_HEADS, QUERY_HEADS), QUERY_HEADS)
            visible = slot < length_ref[b] - block_ref[b] * BLOCK
            scores = jnp.where(visible, p_scr[here, :] * SCALE, MASKED)
            shift = jnp.max(scores, axis=1, keepdims=True).astype(bf16).astype(f32)
            weights = jnp.where(visible, jnp.exp(scores - shift), 0.0)
            total = jnp.sum(weights, axis=1, keepdims=True)
            w_scr[here, :] = weights.astype(bf16)
            stats = jnp.where(place == 0, shift, 0.0)
            for at, term in enumerate(terms(total, 2)):
                stats = jnp.where(place == at + 1, term, stats)
            s_scr[pl.ds(b, QUERY_HEADS, stride=OWN), :] = stats

    def add_up(group):
        for u in range(AT_ONCE):
            b = group * AT_ONCE + u
            for p in range(4):
                here = pl.ds(pl.multiple_of(b * QUERY_HEADS + 16 * p, 16), 16)
                both = jnp.dot(
                    w_scr[here, :],
                    v_ref[b, :, 256 * p : 256 * p + 256],
                    preferred_element_type=f32,
                )
                n_scr[pl.ds(16 * p * OWN + b, 16, stride=OWN), :] = jnp.concatenate(
                    [both[:8, :128], both[8:, 128:]], axis=0
                )

    last = GROUPS - 1
    score(0)
    weigh(0)
    score(1)

    @pl.loop(1, last)
    def _(group):
        add_up(group - 1)
        weigh(group)
        score(group + 1)

    add_up(last - 1)
    weigh(last)
    add_up(last)

    lane = lax.broadcasted_iota(jnp.int32, (OWN, 128), 1)
    first = lax.rem(lane, 64) < 8
    for w in range(WIDE):
        rows = [slice((2 * w + j) * OWN, (2 * w + j + 1) * OWN) for j in range(2)]
        o_ref[w, : 2 * OWN, :] = n_scr[2 * w * OWN : 2 * (w + 1) * OWN, :].astype(bf16)
        stats = jnp.where(first, s_scr[rows[0], :], s_scr[rows[1], :])
        o_ref[w, 2 * OWN :, :] = jnp.where(lane[:8] < 64, stats[:8], stats[8:]).astype(bf16)


def combine_kernel(
    place_ref, r_ref, own_ref, other_ref, straight_ref, swapped_ref, out_ref, again_ref
):
    wide = lax.rem(place_ref[0], WIDE)
    group = wide // 4

    def both_halves(chip):
        parts = [unpack(ref[chip, 2 * OWN :, :].astype(f32)) for ref in (own_ref, other_ref)]
        return jnp.where(
            lax.rem(wide, 2) == 0,
            jnp.concatenate(parts, axis=1),
            jnp.concatenate(parts[::-1], axis=1),
        )

    def column(value, at):
        return jnp.concatenate(
            [value[..., at : at + 1], value[..., 64 + at : 65 + at]], axis=-2
        )

    key = both_halves(group)
    value = both_halves(8 + group)
    key = norm_rope(key, straight_ref[1], swapped_ref[1]).astype(bf16).astype(f32)
    fresh = [
        jnp.sum(own_ref[wide // 2, j * OWN : (j + 1) * OWN, :].astype(f32) * key, axis=1, keepdims=True)
        * SCALE
        for j in range(2)
    ]
    lane = lax.broadcasted_iota(jnp.int32, (8, 128), 1)
    stats = r_ref[:, 2 * OWN :, :].astype(f32)
    highest = jnp.max(stats, axis=0)
    for j in range(2):
        packed = jnp.where(lane < 64, fresh[j][:8], fresh[j][8:])
        highest = jnp.where(lax.rem(lane, 64) == 8 * j, jnp.maximum(highest, packed), highest)
    shift_lane = (lax.rem(lane, 64) == 0) | (lax.rem(lane, 64) == 8)
    factors = jnp.where(shift_lane[None], jnp.exp(jnp.where(shift_lane, stats - highest, 0.0)), 0.0)
    spread_factors = factors
    for shift in (1, 2):
        spread_factors = spread_factors + jnp.roll(factors, shift, axis=2)
    totals = jnp.sum(spread_factors * jnp.where(shift_lane, 0.0, stats), axis=0)
    for j in range(2):
        lanes = slice(j * 128, (j + 1) * 128)
        here = slice(j * OWN, (j + 1) * OWN)
        fresh_weight = jnp.exp(fresh[j] - column(highest, 8 * j))
        weight_sum = column(totals, 8 * j + 1) + column(totals, 8 * j + 2) + fresh_weight
        numer = jnp.sum(r_ref[:, here, :].astype(f32) * column(factors, 8 * j), axis=0)
        numer = numer + fresh_weight.astype(bf16).astype(f32) * value
        heads = (numer / weight_sum).astype(bf16)
        out_ref[:, lanes] = heads
        again_ref[:, lanes] = heads


def product_kernel(place_ref, a_ref, b_ref, d_ref, c_ref, w_ref, keep_ref, send_ref, whole):
    left = jnp.concatenate([a_ref[...], b_ref[...], c_ref[...], d_ref[...]], axis=0)
    whole[...] = jnp.dot(left[:, : w_ref.shape[0]], w_ref[...], preferred_element_type=f32)
    half = keep_ref.shape[0]
    for ref, core in of_cores(place_ref, keep_ref, send_ref):
        ref[...] = whole[pl.ds(pl.multiple_of(core * half, half), half), :].astype(ref.dtype)


def add_kernel(*refs):
    out_ref = refs[-1]
    parts = [ref[...].astype(f32) for ref in refs[:-1]]
    if len(parts) == ROWS:
        parts = [parts[0] + parts[3], parts[1] + parts[2]]
    out_ref[...] = (parts[0] + parts[1]).astype(bf16)


def row_blocks(place_ref, own_ref, other_ref):
    for ref, core in of_cores(place_ref, own_ref, other_ref):
        for at in range(2):
            yield 2 * core + at, ref[at * OWN : (at + 1) * OWN, :].astype(f32)


def gate_up_kernel(
    place_ref, hidden_ref, own_ref, other_ref, gain_ref, wg_ref, wu_ref, stream_ref, *outs
):
    mine = place_ref[0] // WIDE
    for block, attended in row_blocks(place_ref, own_ref, other_ref):
        hidden = hidden_ref[row_block(mine, block), :].astype(f32)
        stream_ref[row_block(0, block), :] = hidden + attended
    stream = stream_ref[...]
    square = jnp.sum(stream * stream, axis=1, keepdims=True)
    scaled = (stream * gain_ref[...].astype(f32)[None]).astype(bf16)
    gate = lax.dot_general(scaled, wg_ref[...], NT, preferred_element_type=f32).astype(bf16)
    up = lax.dot_general(scaled, wu_ref[...], NT, preferred_element_type=f32).astype(bf16)
    pad = HALF - HIDDEN_UNITS
    place = lax.broadcasted_iota(jnp.int32, (stream.shape[0], pad), 1)
    norm = jnp.zeros(place.shape, f32)
    for at, term in enumerate(terms(square, 3)):
        norm = jnp.where(place == at, term, norm)
    norm = norm.astype(bf16)
    for k in range(ROWS):
        at = slice(k * OWN, (k + 1) * OWN)
        outs[k][...] = jnp.concatenate([gate[at], norm[at], up[at], norm[at]], axis=1)


def activate_kernel(a_ref, b_ref, c_ref, d_ref, out_ref):
    total = (a_ref[...].astype(f32) + b_ref[...].astype(f32)) + (
        c_ref[...].astype(f32) + d_ref[...].astype(f32)
    )
    square = (
        total[:, HIDDEN_UNITS : HIDDEN_UNITS + 1]
        + total[:, HIDDEN_UNITS + 1 : HIDDEN_UNITS + 2]
        + total[:, HIDDEN_UNITS + 2 : HIDDEN_UNITS + 3]
    )
    inverse = lax.rsqrt(square / MODEL_WIDTH + EPSILON)
    gate = total[:, :HALF] * inverse
    up = total[:, HALF:] * inverse
    out_ref[...] = (gate / (1.0 + jnp.exp(-gate)) * up).astype(bf16)


def final_kernel(place_ref, stream_ref, own_ref, other_ref, out_ref):
    mine = place_ref[0] // WIDE
    for block, down in row_blocks(place_ref, own_ref, other_ref):
        total = stream_ref[row_block(0, block), :] + down
        out_ref[row_block(mine, block), :] = total.astype(bf16)


def to_rows(blocks):
    return [blocks[0]] + [
        lax.ppermute(blocks[k], "rows", [(i, (i + k) % ROWS) for i in range(ROWS)])
        for k in (2, 1, 3)
    ]


def from_peers(own, axis):
    return [own] + [
        lax.ppermute(own, axis, [((i + k) % ROWS, i) for i in range(ROWS)]) for k in (1, 3, 2)
    ]


def exchange(blocks, axes):
    return lax.all_to_all(blocks, axes, split_axis=0, concat_axis=0, tiled=True)


def from_other_core(value):
    return lax.ppermute(value, "core", [(0, 1), (1, 0)])


def sum_wide(keep, send):
    def add(*parts):
        shape = jax.ShapeDtypeStruct(send.shape, bf16)
        return call(add_kernel, shape, [VMEM] * len(parts), limit=4, name="add")(*parts)

    own = add(keep, from_other_core(send))
    own = add(*from_peers(own, "y"))
    own = add(*from_peers(own, "z"))
    return own, from_other_core(own)


def body(
    hidden,
    attn_gain,
    w_query,
    w_keyval,
    query_gain,
    key_norm_gain,
    keys_cache,
    values_cache,
    lengths,
    block_index,
    w_out,
    mlp_gain,
    w_gate,
    w_up,
    w_down,
):
    place = lax.axis_index(("rows", *WIDE_AXES)).astype(jnp.int32).reshape(1)
    sds = jax.ShapeDtypeStruct

    blocks = call(
        project_kernel,
        [sds((OWN, 384), f32)] * ROWS,
        [SMEM] + [HBM] * 4,
        [
            pltpu.VMEM((64, 384), f32),
            pltpu.VMEM(hidden.shape, bf16),
            pltpu.VMEM(attn_gain.shape, bf16),
            pltpu.VMEM(w_query.shape, bf16),
            pltpu.VMEM(w_keyval.shape[::-1], bf16),
            pltpu.SemaphoreType.DMA((4,)),
        ],
        limit=8,
        name="project",
    )(place, *map(in_hbm, (hidden, attn_gain, w_query, w_keyval.T)))
    straight, swapped = call(
        table_kernel,
        [sds((2, OWN, 128), f32)] * 2,
        [SMEM, HBM, HBM],
        [pltpu.VMEM((HEAD_WIDTH,), bf16)] * 2 + [pltpu.SemaphoreType.DMA((2,))],
        limit=4,
        name="tables",
    )(*map(in_hbm, (lengths, query_gain, key_norm_gain)))
    payload = call(
        heads_kernel,
        sds((CHIPS, PACKED, 128), bf16),
        [VMEM] * 6,
        limit=8,
        name="heads",
        cost=pl.CostEstimate(flops=20_000_000_000, bytes_accessed=1 << 20, transcendentals=0),
    )(*to_rows(blocks), straight, swapped)
    gathered = exchange(payload, CHIP_AXES)
    gathered = (gathered, from_other_core(gathered))

    parts = call(
        attend_kernel,
        sds((WIDE, PACKED, 128), bf16),
        [SMEM] * 3 + [VMEM] * 4,
        [
            pltpu.VMEM((OWN * QUERY_HEADS, 128), f32),
            pltpu.VMEM((OWN * QUERY_HEADS, 256), f32),
            pltpu.VMEM((OWN * QUERY_HEADS, 256), bf16),
            pltpu.VMEM((OWN * QUERY_HEADS, 128), f32),
            pltpu.VMEM((OWN * QUERY_HEADS, 128), f32),
        ],
        limit=8,
        name="attend",
    )(place, lengths, block_index.reshape(OWN), *gathered, in_vmem(keys_cache), in_vmem(values_cache))
    heads_out, heads_own = call(
        combine_kernel, [sds((OWN, 256), bf16)] * 2, [SMEM] + [VMEM] * 5, limit=8, name="combine"
    )(place, exchange(parts, WIDE_AXES), *gathered, straight, swapped)

    def product(own, weight, name):
        return call(
            product_kernel,
            [sds((32, 1280), f32), sds((32, 1280), bf16)],
            [SMEM] + [VMEM] * 5,
            [pltpu.VMEM((64, 1280), f32)],
            limit=8,
            name=name,
        )(place, *from_peers(own, "rows"), weight)

    attended = sum_wide(*product(heads_own, w_out, "output"))
    stream, *blocks = call(
        gate_up_kernel,
        [sds((64, 1280), f32)] + [sds((OWN, 2 * HALF), bf16)] * ROWS,
        [SMEM] + [VMEM] * 6,
        limit=12,
        name="gate_up",
    )(place, hidden, *attended, mlp_gain, w_gate.T, w_up.T)
    activated = call(
        activate_kernel, sds((OWN, HALF), bf16), [VMEM] * 4, limit=8, name="activate"
    )(*to_rows(blocks))
    down = sum_wide(*product(activated, w_down, "down"))
    layer_out = call(
        final_kernel, sds((64, 1280), bf16), [SMEM] + [VMEM] * 3, limit=8, name="final"
    )(place, stream, *down)
    return (layer_out, heads_out)


def solution(mesh):
    mesh = jax.sharding.Mesh(
        mesh.devices.reshape(4, 4, 4, 2), ("rows", "y", "z", "core")
    )
    in_specs = (
        P(None, "rows"),
        P("rows"),
        P("rows", WIDE_AXES),
        P("rows", WIDE_AXES),
        P(),
        P(),
        P("rows", WIDE_AXES, None),
        P("rows", WIDE_AXES, None),
        P("rows"),
        P("rows", WIDE_AXES),
        P(WIDE_AXES, "rows"),
        P("rows"),
        P("rows", WIDE_AXES),
        P("rows", WIDE_AXES),
        P(WIDE_AXES, "rows"),
    )
    out_specs = (P(None, "rows"), P("rows", WIDE_AXES))
    return jax.shard_map(body, mesh=mesh, in_specs=in_specs, out_specs=out_specs, check_vma=False)
```

```python
import jax
import jax.numpy as jnp
import numpy as np
from jax import lax
from jax.experimental import pallas as pl
from jax.experimental.pallas import tpu as pltpu
from jax.sharding import PartitionSpec as P

MODEL_WIDTH = 5120
QUERY_HEADS = 64
KEY_VALUE_HEADS = 8
HEAD_WIDTH = 128
EPSILON = 1e-06
ROPE_BASE = 1000000.0
MASKED = -1e30
SCALE = HEAD_WIDTH ** (-0.5)

ROWS = 4
WIDE = 32
WIDE_AXES = ("y", "z", "core")
CHIPS = 16
CHIP_AXES = ("y", "z")
PACKED = 40
AT_ONCE = 2
GROUPS = 8
OWN = 16
BLOCK = 256
HIDDEN_UNITS = 800
HALF = 896

f32 = jnp.float32
bf16 = jnp.bfloat16
VMEM = pl.BlockSpec(memory_space=pltpu.VMEM)
HBM = pl.BlockSpec(memory_space=pltpu.HBM)
SMEM = pl.BlockSpec(memory_space=pltpu.SMEM)
NT = (((1,), (1,)), ((), ()))


def call(
    kernel, out_shape, in_specs, scratch_shapes=(), limit=24, name=None, cost=None
):
    many = isinstance(out_shape, (tuple, list))
    return pl.pallas_call(
        kernel,
        out_shape=out_shape,
        in_specs=in_specs,
        out_specs=[VMEM] * len(out_shape) if many else VMEM,
        scratch_shapes=list(scratch_shapes),
        compiler_params=pltpu.CompilerParams(vmem_limit_bytes=limit << 20),
        cost_estimate=cost,
        name=name,
    )


def in_vmem(value):
    return pltpu.with_memory_space_constraint(value, pltpu.VMEM)


def in_hbm(value):
    return pltpu.with_memory_space_constraint(value, pltpu.HBM)


def row_block(mine, k):
    return pl.ds(pl.multiple_of(lax.rem(mine + k, ROWS) * OWN, OWN), OWN)


def terms(value, count):
    out = []
    for _ in range(count):
        out.append(value.astype(bf16).astype(f32))
        value = value - out[-1]
    return out


def swap_halves(value):
    half = HEAD_WIDTH // 2
    return jnp.concatenate([value[..., half:], value[..., :half]], axis=-1)


def norm_rope(value, straight, swapped):
    value = value * lax.rsqrt(jnp.mean(value * value, axis=-1, keepdims=True) + EPSILON)
    return value * straight + swap_halves(value) * swapped


def pack(value):
    return jnp.concatenate([value[:8], value[8:]], axis=1)


def unpack(value):
    return jnp.concatenate([value[:, :64], value[:, 64:]], axis=0)


def project_kernel(place_ref, hidden_hbm, gain_hbm, wq_hbm, wkv_hbm, *rest):
    outs, (whole, hidden_ref, gain_ref, wq_ref, wkv_ref, sems) = rest[:ROWS], rest[ROWS:]
    moves = [
        pltpu.make_async_copy(source, target, sems.at[at])
        for at, (source, target) in enumerate(
            (
                (gain_hbm, gain_ref),
                (hidden_hbm, hidden_ref),
                (wkv_hbm, wkv_ref),
                (wq_hbm, wq_ref),
            )
        )
    ]
    for move in moves:
        move.start()
    moves[1].wait()
    hidden = hidden_ref[...].astype(f32)
    square = jnp.sum(hidden * hidden, axis=1, keepdims=True)
    moves[0].wait()
    scaled = (hidden * gain_ref[...].astype(f32)[None]).astype(bf16)
    moves[2].wait()
    keyval = lax.dot_general(scaled, wkv_ref[...], NT, preferred_element_type=f32)
    whole[:, 256:] = jnp.concatenate([keyval, jnp.broadcast_to(square, keyval.shape)], axis=1)
    moves[3].wait()
    whole[:, :256] = jnp.dot(scaled, wq_ref[...], preferred_element_type=f32)
    mine = place_ref[0] // WIDE
    for k in range(ROWS):
        outs[k][...] = whole[row_block(mine, k), :]


def table_kernel(
    length_ref, query_hbm, key_hbm, straight_ref, swapped_ref, query_ref, key_ref, sems
):
    gains = (query_ref, key_ref)
    moves = [
        pltpu.make_async_copy(source, gains[at], sems.at[at])
        for at, source in enumerate((query_hbm, key_hbm))
    ]
    for move in moves:
        move.start()
    row = lax.broadcasted_iota(jnp.int32, (OWN, 128), 0)
    lane = lax.broadcasted_iota(jnp.int32, (OWN, 128), 1)
    position = jnp.zeros((OWN, 128), jnp.int32)
    for b in range(OWN):
        position = jnp.where(row == b, length_ref[b], position)
    half = HEAD_WIDTH // 2
    pair = lax.rem(lax.broadcasted_iota(jnp.int32, (1, 128), 1), half)
    frequency = jnp.zeros((1, 128), f32)
    for at in range(half):
        frequency = jnp.where(pair == at, np.float32(ROPE_BASE ** (-2.0 * at / HEAD_WIDTH)), frequency)
    angle = position.astype(f32) * frequency
    cosine, sine = jnp.cos(angle), jnp.sin(angle)
    sine = jnp.where(lane < half, -sine, sine)
    for at in range(2):
        moves[at].wait()
        gain = gains[at][...].astype(f32)[None]
        straight_ref[at] = cosine * gain
        swapped_ref[at] = sine * swap_halves(gain)


def heads_kernel(a_ref, b_ref, c_ref, d_ref, straight_ref, swapped_ref, out_ref):
    total = (a_ref[...] + b_ref[...]) + (c_ref[...] + d_ref[...])
    inverse = lax.rsqrt(total[:, 320:321] / MODEL_WIDTH + EPSILON)
    scaled = total * inverse
    straight, swapped = straight_ref[0], swapped_ref[0]
    parts = [
        norm_rope(scaled[:, j * 128 : (j + 1) * 128], straight, swapped) for j in range(2)
    ]
    parts.append(pack(scaled[:, 256:320]))
    out = jnp.concatenate(parts, axis=0).astype(bf16)
    out_ref[...] = jnp.broadcast_to(out[None], out_ref.shape)


def of_cores(place_ref, own_ref, other_ref):
    core = lax.rem(place_ref[0], 2)
    return (own_ref, core), (other_ref, 1 - core)


def fresh_parts(place_ref, own_ref, other_ref, straight_ref, swapped_ref, fresh_ref, value_ref):
    wide = lax.rem(place_ref[0], WIDE)
    group = wide // 4

    def both_halves(chip):
        parts = [unpack(ref[chip, 2 * OWN :, :].astype(f32)) for ref in (own_ref, other_ref)]
        return jnp.where(
            lax.rem(wide, 2) == 0,
            jnp.concatenate(parts, axis=1),
            jnp.concatenate(parts[::-1], axis=1),
        )

    key = norm_rope(both_halves(group), straight_ref[1], swapped_ref[1])
    key = key.astype(bf16).astype(f32)
    for j in range(2):
        query = own_ref[wide // 2, j * OWN : (j + 1) * OWN, :].astype(f32)
        scores = jnp.sum(query * key, axis=1, keepdims=True) * SCALE
        fresh_ref[j] = jnp.broadcast_to(scores, key.shape)
    value_ref[...] = both_halves(8 + group)


def attend_kernel(
    place_ref,
    length_ref,
    block_ref,
    own_ref,
    other_ref,
    straight_ref,
    swapped_ref,
    k_ref,
    v_ref,
    o_ref,
    fresh_ref,
    value_ref,
    q_scr,
    p_scr,
    w_scr,
    n_scr,
    s_scr,
):
    for ref, core in of_cores(place_ref, own_ref, other_ref):
        for chip in range(CHIPS):
            for j in range(2):
                head = 4 * chip + 2 * core + j
                q_scr[pl.ds(head, OWN, stride=QUERY_HEADS), :] = ref[
                    chip, j * OWN : (j + 1) * OWN, :
                ].astype(f32)
    fresh_parts(place_ref, own_ref, other_ref, straight_ref, swapped_ref, fresh_ref, value_ref)

    row = lax.broadcasted_iota(jnp.int32, (16, 256), 0)
    lane = lax.broadcasted_iota(jnp.int32, (16, 256), 1)
    own_half = (row < 8) == (lane < 128)
    slot = lax.broadcasted_iota(jnp.int32, (QUERY_HEADS, 256), 1)
    place = lax.rem(lax.broadcasted_iota(jnp.int32, (QUERY_HEADS, 128), 1), 8)

    def score(group):
        for u in range(AT_ONCE):
            b = group * AT_ONCE + u
            for p in range(4):
                here = pl.ds(pl.multiple_of(b * QUERY_HEADS + 16 * p, 16), 16)
                pair = q_scr[here, :]
                query = jnp.where(own_half, jnp.concatenate([pair, pair], axis=1), 0.0)
                p_scr[here, :] = lax.dot_general(
                    query.astype(bf16),
                    k_ref[b, :, 256 * p : 256 * p + 256],
                    NT,
                    preferred_element_type=f32,
                )

    def weigh(group):
        for u in range(AT_ONCE):
            b = group * AT_ONCE + u
            here = pl.ds(pl.multiple_of(b * QUERY_HEADS, QUERY_HEADS), QUERY_HEADS)
            visible = slot < length_ref[b] - block_ref[b] * BLOCK
            scores = jnp.where(visible, p_scr[here, :] * SCALE, MASKED)
            shift = jnp.max(scores, axis=1, keepdims=True).astype(bf16).astype(f32)
            weights = jnp.where(visible, jnp.exp(scores - shift), 0.0)
            total = jnp.sum(weights, axis=1, keepdims=True)
            w_scr[here, :] = weights.astype(bf16)
            stats = jnp.where(place == 0, shift, 0.0)
            for at, term in enumerate(terms(total, 2)):
                stats = jnp.where(place == at + 1, term, stats)
            s_scr[pl.ds(b, QUERY_HEADS, stride=OWN), :] = stats

    def add_up(group):
        for u in range(AT_ONCE):
            b = group * AT_ONCE + u
            for p in range(4):
                here = pl.ds(pl.multiple_of(b * QUERY_HEADS + 16 * p, 16), 16)
                both = jnp.dot(
                    w_scr[here, :],
                    v_ref[b, :, 256 * p : 256 * p + 256],
                    preferred_element_type=f32,
                )
                n_scr[pl.ds(16 * p * OWN + b, 16, stride=OWN), :] = jnp.concatenate(
                    [both[:8, :128], both[8:, 128:]], axis=0
                )

    last = GROUPS - 1
    score(0)
    weigh(0)
    score(1)

    @pl.loop(1, last)
    def _(group):
        add_up(group - 1)
        weigh(group)
        score(group + 1)

    add_up(last - 1)
    weigh(last)
    add_up(last)

    lane = lax.broadcasted_iota(jnp.int32, (OWN, 128), 1)
    first = lax.rem(lane, 64) < 8
    for w in range(WIDE):
        rows = [slice((2 * w + j) * OWN, (2 * w + j + 1) * OWN) for j in range(2)]
        o_ref[w, : 2 * OWN, :] = n_scr[2 * w * OWN : 2 * (w + 1) * OWN, :].astype(bf16)
        stats = jnp.where(first, s_scr[rows[0], :], s_scr[rows[1], :])
        o_ref[w, 2 * OWN :, :] = jnp.where(lane[:8] < 64, stats[:8], stats[8:]).astype(bf16)


def combine_kernel(r_ref, fresh_ref, value_ref, out_ref, again_ref):
    def column(value, at):
        return jnp.concatenate(
            [value[..., at : at + 1], value[..., 64 + at : 65 + at]], axis=-2
        )

    lane = lax.broadcasted_iota(jnp.int32, (8, 128), 1)
    stats = r_ref[:, 2 * OWN :, :].astype(f32)
    highest = jnp.max(stats, axis=0)
    for j in range(2):
        packed = jnp.where(lane < 64, fresh_ref[j, :8, :], fresh_ref[j, 8:, :])
        highest = jnp.where(lax.rem(lane, 64) == 8 * j, jnp.maximum(highest, packed), highest)
    shift_lane = (lax.rem(lane, 64) == 0) | (lax.rem(lane, 64) == 8)
    factors = jnp.where(shift_lane[None], jnp.exp(jnp.where(shift_lane, stats - highest, 0.0)), 0.0)
    spread_factors = factors
    for shift in (1, 2):
        spread_factors = spread_factors + jnp.roll(factors, shift, axis=2)
    totals = jnp.sum(spread_factors * jnp.where(shift_lane, 0.0, stats), axis=0)
    for j in range(2):
        lanes = slice(j * 128, (j + 1) * 128)
        here = slice(j * OWN, (j + 1) * OWN)
        fresh_weight = jnp.exp(fresh_ref[j] - column(highest, 8 * j))
        weight_sum = column(totals, 8 * j + 1) + column(totals, 8 * j + 2) + fresh_weight
        numer = jnp.sum(r_ref[:, here, :].astype(f32) * column(factors, 8 * j), axis=0)
        numer = numer + fresh_weight.astype(bf16).astype(f32) * value_ref[...]
        heads = (numer / weight_sum).astype(bf16)
        out_ref[:, lanes] = heads
        again_ref[:, lanes] = heads


def product_kernel(place_ref, a_ref, b_ref, d_ref, c_ref, w_ref, keep_ref, send_ref, whole):
    left = jnp.concatenate([a_ref[...], b_ref[...], c_ref[...], d_ref[...]], axis=0)
    whole[...] = jnp.dot(left[:, : w_ref.shape[0]], w_ref[...], preferred_element_type=f32)
    half = keep_ref.shape[0]
    for ref, core in of_cores(place_ref, keep_ref, send_ref):
        ref[...] = whole[pl.ds(pl.multiple_of(core * half, half), half), :].astype(ref.dtype)


def add_kernel(*refs):
    out_ref = refs[-1]
    parts = [ref[...].astype(f32) for ref in refs[:-1]]
    if len(parts) == ROWS:
        parts = [parts[0] + parts[3], parts[1] + parts[2]]
    out_ref[...] = (parts[0] + parts[1]).astype(bf16)


def row_blocks(place_ref, own_ref, other_ref):
    for ref, core in of_cores(place_ref, own_ref, other_ref):
        for at in range(2):
            yield 2 * core + at, ref[at * OWN : (at + 1) * OWN, :].astype(f32)


def gate_up_kernel(
    place_ref, hidden_ref, own_ref, other_ref, gain_ref, wg_ref, wu_ref, stream_ref, *outs
):
    mine = place_ref[0] // WIDE
    for block, attended in row_blocks(place_ref, own_ref, other_ref):
        hidden = hidden_ref[row_block(mine, block), :].astype(f32)
        stream_ref[row_block(0, block), :] = hidden + attended
    stream = stream_ref[...]
    square = jnp.sum(stream * stream, axis=1, keepdims=True)
    scaled = (stream * gain_ref[...].astype(f32)[None]).astype(bf16)
    gate = lax.dot_general(scaled, wg_ref[...], NT, preferred_element_type=f32).astype(bf16)
    up = lax.dot_general(scaled, wu_ref[...], NT, preferred_element_type=f32).astype(bf16)
    pad = HALF - HIDDEN_UNITS
    place = lax.broadcasted_iota(jnp.int32, (stream.shape[0], pad), 1)
    norm = jnp.zeros(place.shape, f32)
    for at, term in enumerate(terms(square, 3)):
        norm = jnp.where(place == at, term, norm)
    norm = norm.astype(bf16)
    for k in range(ROWS):
        at = slice(k * OWN, (k + 1) * OWN)
        outs[k][...] = jnp.concatenate([gate[at], norm[at], up[at], norm[at]], axis=1)


def activate_kernel(a_ref, b_ref, c_ref, d_ref, out_ref):
    total = (a_ref[...].astype(f32) + b_ref[...].astype(f32)) + (
        c_ref[...].astype(f32) + d_ref[...].astype(f32)
    )
    square = (
        total[:, HIDDEN_UNITS : HIDDEN_UNITS + 1]
        + total[:, HIDDEN_UNITS + 1 : HIDDEN_UNITS + 2]
        + total[:, HIDDEN_UNITS + 2 : HIDDEN_UNITS + 3]
    )
    inverse = lax.rsqrt(square / MODEL_WIDTH + EPSILON)
    gate = total[:, :HALF] * inverse
    up = total[:, HALF:] * inverse
    out_ref[...] = (gate / (1.0 + jnp.exp(-gate)) * up).astype(bf16)


def final_kernel(place_ref, stream_ref, own_ref, other_ref, out_ref):
    mine = place_ref[0] // WIDE
    for block, down in row_blocks(place_ref, own_ref, other_ref):
        total = stream_ref[row_block(0, block), :] + down
        out_ref[row_block(mine, block), :] = total.astype(bf16)


def to_rows(blocks):
    return [blocks[0]] + [
        lax.ppermute(blocks[k], "rows", [(i, (i + k) % ROWS) for i in range(ROWS)])
        for k in (2, 1, 3)
    ]


def from_peers(own, axis):
    return [own] + [
        lax.ppermute(own, axis, [((i + k) % ROWS, i) for i in range(ROWS)]) for k in (1, 3, 2)
    ]


def exchange(blocks, axes):
    return lax.all_to_all(blocks, axes, split_axis=0, concat_axis=0, tiled=True)


def from_other_core(value):
    return lax.ppermute(value, "core", [(0, 1), (1, 0)])


def sum_wide(keep, send):
    def add(*parts):
        shape = jax.ShapeDtypeStruct(send.shape, bf16)
        return call(add_kernel, shape, [VMEM] * len(parts), limit=4, name="add")(*parts)

    own = add(keep, from_other_core(send))
    own = add(*from_peers(own, "y"))
    own = add(*from_peers(own, "z"))
    return own, from_other_core(own)


def body(
    hidden,
    attn_gain,
    w_query,
    w_keyval,
    query_gain,
    key_norm_gain,
    keys_cache,
    values_cache,
    lengths,
    block_index,
    w_out,
    mlp_gain,
    w_gate,
    w_up,
    w_down,
):
    place = lax.axis_index(("rows", *WIDE_AXES)).astype(jnp.int32).reshape(1)
    sds = jax.ShapeDtypeStruct

    blocks = call(
        project_kernel,
        [sds((OWN, 384), f32)] * ROWS,
        [SMEM] + [HBM] * 4,
        [
            pltpu.VMEM((64, 384), f32),
            pltpu.VMEM(hidden.shape, bf16),
            pltpu.VMEM(attn_gain.shape, bf16),
            pltpu.VMEM(w_query.shape, bf16),
            pltpu.VMEM(w_keyval.shape[::-1], bf16),
            pltpu.SemaphoreType.DMA((4,)),
        ],
        limit=8,
        name="project",
    )(place, *map(in_hbm, (hidden, attn_gain, w_query, w_keyval.T)))
    straight, swapped = call(
        table_kernel,
        [sds((2, OWN, 128), f32)] * 2,
        [SMEM, HBM, HBM],
        [pltpu.VMEM((HEAD_WIDTH,), bf16)] * 2 + [pltpu.SemaphoreType.DMA((2,))],
        limit=4,
        name="tables",
    )(*map(in_hbm, (lengths, query_gain, key_norm_gain)))
    payload = call(
        heads_kernel,
        sds((CHIPS, PACKED, 128), bf16),
        [VMEM] * 6,
        limit=8,
        name="heads",
        cost=pl.CostEstimate(flops=20_000_000_000, bytes_accessed=1 << 20, transcendentals=0),
    )(*to_rows(blocks), straight, swapped)
    gathered = exchange(payload, CHIP_AXES)
    gathered = (gathered, from_other_core(gathered))

    parts, fresh, value = call(
        attend_kernel,
        [sds((WIDE, PACKED, 128), bf16), sds((2, OWN, 128), f32), sds((OWN, 128), f32)],
        [SMEM] * 3 + [VMEM] * 6,
        [
            pltpu.VMEM((OWN * QUERY_HEADS, 128), f32),
            pltpu.VMEM((OWN * QUERY_HEADS, 256), f32),
            pltpu.VMEM((OWN * QUERY_HEADS, 256), bf16),
            pltpu.VMEM((OWN * QUERY_HEADS, 128), f32),
            pltpu.VMEM((OWN * QUERY_HEADS, 128), f32),
        ],
        limit=8,
        name="attend",
    )(place, lengths, block_index.reshape(OWN), *gathered, straight, swapped, in_vmem(keys_cache), in_vmem(values_cache))
    heads_out, heads_own = call(
        combine_kernel, [sds((OWN, 256), bf16)] * 2, [VMEM] * 3, limit=8, name="combine"
    )(exchange(parts, WIDE_AXES), fresh, value)

    def product(own, weight, name):
        return call(
            product_kernel,
            [sds((32, 1280), f32), sds((32, 1280), bf16)],
            [SMEM] + [VMEM] * 5,
            [pltpu.VMEM((64, 1280), f32)],
            limit=8,
            name=name,
        )(place, *from_peers(own, "rows"), weight)

    attended = sum_wide(*product(heads_own, w_out, "output"))
    stream, *blocks = call(
        gate_up_kernel,
        [sds((64, 1280), f32)] + [sds((OWN, 2 * HALF), bf16)] * ROWS,
        [SMEM] + [VMEM] * 6,
        limit=12,
        name="gate_up",
    )(place, hidden, *attended, mlp_gain, w_gate.T, w_up.T)
    activated = call(
        activate_kernel, sds((OWN, HALF), bf16), [VMEM] * 4, limit=8, name="activate"
    )(*to_rows(blocks))
    down = sum_wide(*product(activated, w_down, "down"))
    layer_out = call(
        final_kernel, sds((64, 1280), bf16), [SMEM] + [VMEM] * 3, limit=8, name="final"
    )(place, stream, *down)
    return (layer_out, heads_out)


def solution(mesh):
    mesh = jax.sharding.Mesh(
        mesh.devices.reshape(4, 4, 4, 2), ("rows", "y", "z", "core")
    )
    in_specs = (
        P(None, "rows"),
        P("rows"),
        P("rows", WIDE_AXES),
        P("rows", WIDE_AXES),
        P(),
        P(),
        P("rows", WIDE_AXES, None),
        P("rows", WIDE_AXES, None),
        P("rows"),
        P("rows", WIDE_AXES),
        P(WIDE_AXES, "rows"),
        P("rows"),
        P("rows", WIDE_AXES),
        P("rows", WIDE_AXES),
        P(WIDE_AXES, "rows"),
    )
    out_specs = (P(None, "rows"), P("rows", WIDE_AXES))
    return jax.shard_map(body, mesh=mesh, in_specs=in_specs, out_specs=out_specs, check_vma=False)
```

```python
import jax
import jax.numpy as jnp
import numpy as np
from jax import lax
from jax.experimental import pallas as pl
from jax.experimental.pallas import tpu as pltpu
from jax.sharding import PartitionSpec as P

MODEL_WIDTH = 5120
QUERY_HEADS = 64
KEY_VALUE_HEADS = 8
HEAD_WIDTH = 128
EPSILON = 1e-06
ROPE_BASE = 1000000.0
MASKED = -1e30
SCALE = HEAD_WIDTH ** (-0.5)

ROWS = 4
WIDE = 32
WIDE_AXES = ("y", "z", "core")
CHIPS = 16
CHIP_AXES = ("y", "z")
PACKED = 48
AT_ONCE = 2
GROUPS = 8
OWN = 16
BLOCK = 256
HIDDEN_UNITS = 800
HALF = 896

f32 = jnp.float32
bf16 = jnp.bfloat16
VMEM = pl.BlockSpec(memory_space=pltpu.VMEM)
HBM = pl.BlockSpec(memory_space=pltpu.HBM)
SMEM = pl.BlockSpec(memory_space=pltpu.SMEM)
NT = (((1,), (1,)), ((), ()))


def call(
    kernel, out_shape, in_specs, scratch_shapes=(), limit=24, name=None, cost=None
):
    many = isinstance(out_shape, (tuple, list))
    return pl.pallas_call(
        kernel,
        out_shape=out_shape,
        in_specs=in_specs,
        out_specs=[VMEM] * len(out_shape) if many else VMEM,
        scratch_shapes=list(scratch_shapes),
        compiler_params=pltpu.CompilerParams(vmem_limit_bytes=limit << 20),
        cost_estimate=cost,
        name=name,
    )


def in_vmem(value):
    return pltpu.with_memory_space_constraint(value, pltpu.VMEM)


def in_hbm(value):
    return pltpu.with_memory_space_constraint(value, pltpu.HBM)


def row_block(mine, k):
    return pl.ds(pl.multiple_of(lax.rem(mine + k, ROWS) * OWN, OWN), OWN)


def terms(value, count):
    out = []
    for _ in range(count):
        out.append(value.astype(bf16).astype(f32))
        value = value - out[-1]
    return out


def swap_halves(value):
    half = HEAD_WIDTH // 2
    return jnp.concatenate([value[..., half:], value[..., :half]], axis=-1)


def norm_rope(value, straight, swapped):
    value = value * lax.rsqrt(jnp.mean(value * value, axis=-1, keepdims=True) + EPSILON)
    return value * straight + swap_halves(value) * swapped


def project_kernel(place_ref, hidden_hbm, gain_hbm, wq_hbm, wkv_hbm, *rest):
    outs, (whole, hidden_ref, gain_ref, wq_ref, wkv_ref, sems) = rest[:ROWS], rest[ROWS:]
    moves = [
        pltpu.make_async_copy(source, target, sems.at[at])
        for at, (source, target) in enumerate(
            (
                (gain_hbm, gain_ref),
                (hidden_hbm, hidden_ref),
                (wkv_hbm, wkv_ref),
                (wq_hbm, wq_ref),
            )
        )
    ]
    for move in moves:
        move.start()
    moves[1].wait()
    hidden = hidden_ref[...].astype(f32)
    square = jnp.sum(hidden * hidden, axis=1, keepdims=True)
    moves[0].wait()
    scaled = (hidden * gain_ref[...].astype(f32)[None]).astype(bf16)
    moves[2].wait()
    keyval = lax.dot_general(scaled, wkv_ref[...], NT, preferred_element_type=f32)
    whole[:, 256:] = jnp.concatenate([keyval, jnp.broadcast_to(square, keyval.shape)], axis=1)
    moves[3].wait()
    whole[:, :256] = jnp.dot(scaled, wq_ref[...], preferred_element_type=f32)
    mine = place_ref[0] // WIDE
    for k in range(ROWS):
        outs[k][...] = whole[row_block(mine, k), :]


def table_kernel(
    length_ref, query_hbm, key_hbm, straight_ref, swapped_ref, query_ref, key_ref, sems
):
    gains = (query_ref, key_ref)
    moves = [
        pltpu.make_async_copy(source, gains[at], sems.at[at])
        for at, source in enumerate((query_hbm, key_hbm))
    ]
    for move in moves:
        move.start()
    row = lax.broadcasted_iota(jnp.int32, (OWN, 128), 0)
    lane = lax.broadcasted_iota(jnp.int32, (OWN, 128), 1)
    position = jnp.zeros((OWN, 128), jnp.int32)
    for b in range(OWN):
        position = jnp.where(row == b, length_ref[b], position)
    half = HEAD_WIDTH // 2
    pair = lax.rem(lax.broadcasted_iota(jnp.int32, (1, 128), 1), half)
    frequency = jnp.zeros((1, 128), f32)
    for at in range(half):
        frequency = jnp.where(pair == at, np.float32(ROPE_BASE ** (-2.0 * at / HEAD_WIDTH)), frequency)
    angle = position.astype(f32) * frequency
    cosine, sine = jnp.cos(angle), jnp.sin(angle)
    sine = jnp.where(lane < half, -sine, sine)
    for at in range(2):
        moves[at].wait()
        gain = gains[at][...].astype(f32)[None]
        straight_ref[at] = cosine * gain
        swapped_ref[at] = sine * swap_halves(gain)


def heads_kernel(a_ref, b_ref, c_ref, d_ref, straight_ref, swapped_ref, out_ref):
    total = (a_ref[...] + b_ref[...]) + (c_ref[...] + d_ref[...])
    inverse = lax.rsqrt(total[:, 320:321] / MODEL_WIDTH + EPSILON)
    scaled = total * inverse
    straight, swapped = straight_ref[0], swapped_ref[0]
    parts = [
        norm_rope(scaled[:, j * 128 : (j + 1) * 128], straight, swapped) for j in range(2)
    ]
    parts.append(scaled[:, 256:])
    out = jnp.concatenate(parts, axis=0).astype(bf16)
    out_ref[...] = jnp.broadcast_to(out[None], out_ref.shape)


def of_cores(place_ref, own_ref, other_ref):
    core = lax.rem(place_ref[0], 2)
    return (own_ref, core), (other_ref, 1 - core)


def fresh_parts(place_ref, own_ref, other_ref, straight_ref, swapped_ref, fresh_ref, value_ref):
    wide = lax.rem(place_ref[0], WIDE)
    group = wide // 4

    def both_halves(chip):
        parts = [ref[chip, 2 * OWN :, :].astype(f32)[:, :64] for ref in (own_ref, other_ref)]
        return jnp.where(
            lax.rem(wide, 2) == 0,
            jnp.concatenate(parts, axis=1),
            jnp.concatenate(parts[::-1], axis=1),
        )

    key = norm_rope(both_halves(group), straight_ref[1], swapped_ref[1])
    key = key.astype(bf16).astype(f32)
    for j in range(2):
        query = own_ref[wide // 2, j * OWN : (j + 1) * OWN, :].astype(f32)
        scores = jnp.sum(query * key, axis=1, keepdims=True) * SCALE
        fresh_ref[j] = jnp.broadcast_to(scores, key.shape)
    value_ref[...] = both_halves(8 + group)


def attend_kernel(
    place_ref,
    length_ref,
    block_ref,
    own_ref,
    other_ref,
    straight_ref,
    swapped_ref,
    k_ref,
    v_ref,
    o_ref,
    fresh_ref,
    value_ref,
    q_scr,
    p_scr,
    w_scr,
    n_scr,
    s_scr,
):
    for ref, core in of_cores(place_ref, own_ref, other_ref):
        for chip in range(CHIPS):
            for j in range(2):
                head = 4 * chip + 2 * core + j
                q_scr[pl.ds(head, OWN, stride=QUERY_HEADS), :] = ref[
                    chip, j * OWN : (j + 1) * OWN, :
                ].astype(f32)
    fresh_parts(place_ref, own_ref, other_ref, straight_ref, swapped_ref, fresh_ref, value_ref)

    row = lax.broadcasted_iota(jnp.int32, (16, 256), 0)
    lane = lax.broadcasted_iota(jnp.int32, (16, 256), 1)
    own_half = (row < 8) == (lane < 128)
    slot = lax.broadcasted_iota(jnp.int32, (QUERY_HEADS, 256), 1)
    place = lax.rem(lax.broadcasted_iota(jnp.int32, (QUERY_HEADS, 128), 1), 8)

    def score(group):
        for u in range(AT_ONCE):
            b = group * AT_ONCE + u
            for p in range(4):
                here = pl.ds(pl.multiple_of(b * QUERY_HEADS + 16 * p, 16), 16)
                pair = q_scr[here, :]
                query = jnp.where(own_half, jnp.concatenate([pair, pair], axis=1), 0.0)
                p_scr[here, :] = lax.dot_general(
                    query.astype(bf16),
                    k_ref[b, :, 256 * p : 256 * p + 256],
                    NT,
                    preferred_element_type=f32,
                )

    def weigh(group):
        for u in range(AT_ONCE):
            b = group * AT_ONCE + u
            here = pl.ds(pl.multiple_of(b * QUERY_HEADS, QUERY_HEADS), QUERY_HEADS)
            visible = slot < length_ref[b] - block_ref[b] * BLOCK
            scores = jnp.where(visible, p_scr[here, :] * SCALE, MASKED)
            shift = jnp.max(scores, axis=1, keepdims=True).astype(bf16).astype(f32)
            weights = jnp.where(visible, jnp.exp(scores - shift), 0.0)
            total = jnp.sum(weights, axis=1, keepdims=True)
            w_scr[here, :] = weights.astype(bf16)
            stats = jnp.where(place == 0, shift, 0.0)
            for at, term in enumerate(terms(total, 2)):
                stats = jnp.where(place == at + 1, term, stats)
            s_scr[pl.ds(b, QUERY_HEADS, stride=OWN), :] = stats

    def add_up(group):
        for u in range(AT_ONCE):
            b = group * AT_ONCE + u
            for p in range(4):
                here = pl.ds(pl.multiple_of(b * QUERY_HEADS + 16 * p, 16), 16)
                both = jnp.dot(
                    w_scr[here, :],
                    v_ref[b, :, 256 * p : 256 * p + 256],
                    preferred_element_type=f32,
                )
                n_scr[pl.ds(16 * p * OWN + b, 16, stride=OWN), :] = jnp.concatenate(
                    [both[:8, :128], both[8:, 128:]], axis=0
                )

    last = GROUPS - 1
    score(0)
    weigh(0)
    score(1)

    @pl.loop(1, last)
    def _(group):
        add_up(group - 1)
        weigh(group)
        score(group + 1)

    add_up(last - 1)
    weigh(last)
    add_up(last)

    lane = lax.broadcasted_iota(jnp.int32, (OWN, 128), 1)
    first = lane < 8
    for w in range(WIDE):
        rows = [slice((2 * w + j) * OWN, (2 * w + j + 1) * OWN) for j in range(2)]
        o_ref[w, : 2 * OWN, :] = n_scr[2 * w * OWN : 2 * (w + 1) * OWN, :].astype(bf16)
        stats = jnp.where(first, s_scr[rows[0], :], s_scr[rows[1], :])
        o_ref[w, 2 * OWN :, :] = stats.astype(bf16)


def combine_kernel(r_ref, fresh_ref, value_ref, out_ref, again_ref):
    def column(value, at):
        return value[..., at : at + 1]

    lane = lax.broadcasted_iota(jnp.int32, (OWN, 128), 1)
    stats = r_ref[:, 2 * OWN :, :].astype(f32)
    highest = jnp.max(stats, axis=0)
    for j in range(2):
        highest = jnp.where(lane == 8 * j, jnp.maximum(highest, fresh_ref[j]), highest)
    shift_lane = (lane == 0) | (lane == 8)
    factors = jnp.where(shift_lane[None], jnp.exp(jnp.where(shift_lane, stats - highest, 0.0)), 0.0)
    spread_factors = factors
    for shift in (1, 2):
        spread_factors = spread_factors + jnp.roll(factors, shift, axis=2)
    totals = jnp.sum(spread_factors * jnp.where(shift_lane, 0.0, stats), axis=0)
    for j in range(2):
        lanes = slice(j * 128, (j + 1) * 128)
        here = slice(j * OWN, (j + 1) * OWN)
        fresh_weight = jnp.exp(fresh_ref[j] - column(highest, 8 * j))
        weight_sum = column(totals, 8 * j + 1) + column(totals, 8 * j + 2) + fresh_weight
        numer = jnp.sum(r_ref[:, here, :].astype(f32) * column(factors, 8 * j), axis=0)
        numer = numer + fresh_weight.astype(bf16).astype(f32) * value_ref[...]
        heads = (numer / weight_sum).astype(bf16)
        out_ref[:, lanes] = heads
        again_ref[:, lanes] = heads


def product_kernel(place_ref, a_ref, b_ref, d_ref, c_ref, w_ref, keep_ref, send_ref, whole):
    left = jnp.concatenate([a_ref[...], b_ref[...], c_ref[...], d_ref[...]], axis=0)
    whole[...] = jnp.dot(left[:, : w_ref.shape[0]], w_ref[...], preferred_element_type=f32)
    half = keep_ref.shape[0]
    for ref, core in of_cores(place_ref, keep_ref, send_ref):
        ref[...] = whole[pl.ds(pl.multiple_of(core * half, half), half), :].astype(ref.dtype)


def add_kernel(*refs):
    out_ref = refs[-1]
    parts = [ref[...].astype(f32) for ref in refs[:-1]]
    if len(parts) == ROWS:
        parts = [parts[0] + parts[3], parts[1] + parts[2]]
    out_ref[...] = (parts[0] + parts[1]).astype(bf16)


def row_blocks(place_ref, own_ref, other_ref):
    for ref, core in of_cores(place_ref, own_ref, other_ref):
        for at in range(2):
            yield 2 * core + at, ref[at * OWN : (at + 1) * OWN, :].astype(f32)


def gate_up_kernel(
    place_ref, hidden_ref, own_ref, other_ref, gain_ref, wg_ref, wu_ref, stream_ref, *outs
):
    mine = place_ref[0] // WIDE
    for block, attended in row_blocks(place_ref, own_ref, other_ref):
        hidden = hidden_ref[row_block(mine, block), :].astype(f32)
        stream_ref[row_block(0, block), :] = hidden + attended
    stream = stream_ref[...]
    square = jnp.sum(stream * stream, axis=1, keepdims=True)
    scaled = (stream * gain_ref[...].astype(f32)[None]).astype(bf16)
    gate = lax.dot_general(scaled, wg_ref[...], NT, preferred_element_type=f32).astype(bf16)
    up = lax.dot_general(scaled, wu_ref[...], NT, preferred_element_type=f32).astype(bf16)
    pad = HALF - HIDDEN_UNITS
    place = lax.broadcasted_iota(jnp.int32, (stream.shape[0], pad), 1)
    norm = jnp.zeros(place.shape, f32)
    for at, term in enumerate(terms(square, 3)):
        norm = jnp.where(place == at, term, norm)
    norm = norm.astype(bf16)
    for k in range(ROWS):
        at = slice(k * OWN, (k + 1) * OWN)
        outs[k][...] = jnp.concatenate([gate[at], norm[at], up[at], norm[at]], axis=1)


def activate_kernel(a_ref, b_ref, c_ref, d_ref, out_ref):
    total = (a_ref[...].astype(f32) + b_ref[...].astype(f32)) + (
        c_ref[...].astype(f32) + d_ref[...].astype(f32)
    )
    square = (
        total[:, HIDDEN_UNITS : HIDDEN_UNITS + 1]
        + total[:, HIDDEN_UNITS + 1 : HIDDEN_UNITS + 2]
        + total[:, HIDDEN_UNITS + 2 : HIDDEN_UNITS + 3]
    )
    inverse = lax.rsqrt(square / MODEL_WIDTH + EPSILON)
    gate = total[:, :HALF] * inverse
    up = total[:, HALF:] * inverse
    out_ref[...] = (gate / (1.0 + jnp.exp(-gate)) * up).astype(bf16)


def final_kernel(place_ref, stream_ref, own_ref, other_ref, out_ref):
    mine = place_ref[0] // WIDE
    for block, down in row_blocks(place_ref, own_ref, other_ref):
        total = stream_ref[row_block(0, block), :] + down
        out_ref[row_block(mine, block), :] = total.astype(bf16)


def to_rows(blocks):
    return [blocks[0]] + [
        lax.ppermute(blocks[k], "rows", [(i, (i + k) % ROWS) for i in range(ROWS)])
        for k in (2, 1, 3)
    ]


def from_peers(own, axis):
    return [own] + [
        lax.ppermute(own, axis, [((i + k) % ROWS, i) for i in range(ROWS)]) for k in (1, 3, 2)
    ]


def exchange(blocks, axes):
    return lax.all_to_all(blocks, axes, split_axis=0, concat_axis=0, tiled=True)


def from_other_core(value):
    return lax.ppermute(value, "core", [(0, 1), (1, 0)])


def sum_wide(keep, send):
    def add(*parts):
        shape = jax.ShapeDtypeStruct(send.shape, bf16)
        return call(add_kernel, shape, [VMEM] * len(parts), limit=4, name="add")(*parts)

    own = add(keep, from_other_core(send))
    own = add(*from_peers(own, "y"))
    own = add(*from_peers(own, "z"))
    return own, from_other_core(own)


def body(
    hidden,
    attn_gain,
    w_query,
    w_keyval,
    query_gain,
    key_norm_gain,
    keys_cache,
    values_cache,
    lengths,
    block_index,
    w_out,
    mlp_gain,
    w_gate,
    w_up,
    w_down,
):
    place = lax.axis_index(("rows", *WIDE_AXES)).astype(jnp.int32).reshape(1)
    sds = jax.ShapeDtypeStruct

    blocks = call(
        project_kernel,
        [sds((OWN, 384), f32)] * ROWS,
        [SMEM] + [HBM] * 4,
        [
            pltpu.VMEM((64, 384), f32),
            pltpu.VMEM(hidden.shape, bf16),
            pltpu.VMEM(attn_gain.shape, bf16),
            pltpu.VMEM(w_query.shape, bf16),
            pltpu.VMEM(w_keyval.shape[::-1], bf16),
            pltpu.SemaphoreType.DMA((4,)),
        ],
        limit=8,
        name="project",
    )(place, *map(in_hbm, (hidden, attn_gain, w_query, w_keyval.T)))
    straight, swapped = call(
        table_kernel,
        [sds((2, OWN, 128), f32)] * 2,
        [SMEM, HBM, HBM],
        [pltpu.VMEM((HEAD_WIDTH,), bf16)] * 2 + [pltpu.SemaphoreType.DMA((2,))],
        limit=4,
        name="tables",
    )(*map(in_hbm, (lengths, query_gain, key_norm_gain)))
    payload = call(
        heads_kernel,
        sds((CHIPS, PACKED, 128), bf16),
        [VMEM] * 6,
        limit=8,
        name="heads",
        cost=pl.CostEstimate(flops=20_000_000_000, bytes_accessed=1 << 20, transcendentals=0),
    )(*to_rows(blocks), straight, swapped)
    gathered = exchange(payload, CHIP_AXES)
    gathered = (gathered, from_other_core(gathered))

    parts, fresh, value = call(
        attend_kernel,
        [sds((WIDE, PACKED, 128), bf16), sds((2, OWN, 128), f32), sds((OWN, 128), f32)],
        [SMEM] * 3 + [VMEM] * 6,
        [
            pltpu.VMEM((OWN * QUERY_HEADS, 128), f32),
            pltpu.VMEM((OWN * QUERY_HEADS, 256), f32),
            pltpu.VMEM((OWN * QUERY_HEADS, 256), bf16),
            pltpu.VMEM((OWN * QUERY_HEADS, 128), f32),
            pltpu.VMEM((OWN * QUERY_HEADS, 128), f32),
        ],
        limit=8,
        name="attend",
    )(place, lengths, block_index.reshape(OWN), *gathered, straight, swapped, in_vmem(keys_cache), in_vmem(values_cache))
    heads_out, heads_own = call(
        combine_kernel, [sds((OWN, 256), bf16)] * 2, [VMEM] * 3, limit=8, name="combine"
    )(exchange(parts, WIDE_AXES), fresh, value)

    def product(own, weight, name):
        return call(
            product_kernel,
            [sds((32, 1280), f32), sds((32, 1280), bf16)],
            [SMEM] + [VMEM] * 5,
            [pltpu.VMEM((64, 1280), f32)],
            limit=8,
            name=name,
        )(place, *from_peers(own, "rows"), weight)

    attended = sum_wide(*product(heads_own, w_out, "output"))
    stream, *blocks = call(
        gate_up_kernel,
        [sds((64, 1280), f32)] + [sds((OWN, 2 * HALF), bf16)] * ROWS,
        [SMEM] + [VMEM] * 6,
        limit=12,
        name="gate_up",
    )(place, hidden, *attended, mlp_gain, w_gate.T, w_up.T)
    activated = call(
        activate_kernel, sds((OWN, HALF), bf16), [VMEM] * 4, limit=8, name="activate"
    )(*to_rows(blocks))
    down = sum_wide(*product(activated, w_down, "down"))
    layer_out = call(
        final_kernel, sds((64, 1280), bf16), [SMEM] + [VMEM] * 3, limit=8, name="final"
    )(place, stream, *down)
    return (layer_out, heads_out)


def solution(mesh):
    mesh = jax.sharding.Mesh(
        mesh.devices.reshape(4, 4, 4, 2), ("rows", "y", "z", "core")
    )
    in_specs = (
        P(None, "rows"),
        P("rows"),
        P("rows", WIDE_AXES),
        P("rows", WIDE_AXES),
        P(),
        P(),
        P("rows", WIDE_AXES, None),
        P("rows", WIDE_AXES, None),
        P("rows"),
        P("rows", WIDE_AXES),
        P(WIDE_AXES, "rows"),
        P("rows"),
        P("rows", WIDE_AXES),
        P("rows", WIDE_AXES),
        P(WIDE_AXES, "rows"),
    )
    out_specs = (P(None, "rows"), P("rows", WIDE_AXES))
    return jax.shard_map(body, mesh=mesh, in_specs=in_specs, out_specs=out_specs, check_vma=False)
```
